32 devices in a mesh: lat: 2 (over y), chan: 4 (over z), tm: 4 (over x, core).
Axes of the slice: x: 2, y: 2, z: 4, core: 2. Of those that a mesh axis runs over, the one named last changes fastest.
Arguments:
- fields: bfloat16 [32, 1440, 256], P(('tm', 'lat'), None, 'chan'), parts along dimension 0, may hold values from -6 to 6
- disco_weight: bfloat16 [6, 256, 64], P(None, 'chan'), may hold values from -0.25 to 0.25
- support_lat: int32 [8, 9], P('lat'), may hold values from -2 to 2
- support_lon: int32 [8, 9], P('lat'), may hold values from -4 to 4
- support_basis: int32 [8, 9], P('lat'), may hold values from 0 to 5
- support_value: float32 [8, 9], P('lat'), may hold values from 0.25 to 1.5
- w_up: bfloat16 [256, 512], replicated, may hold values from -0.375 to 0.375
- w_down: bfloat16 [512, 256], replicated, may hold values from -0.25 to 0.25
- legendre: bfloat16 [24, 384, 8], P(('lat', 'chan')), may hold values from -2 to 2
Outputs:
- coefficients: bfloat16 [96, 384, 512], P(('tm', 'lat', 'chan')), parts along dimension 0
The draws below stay inside these ranges and needn't reach their ends.
There are 4 independent parts, one for each index of `tm`. The reference program is written for one: setup_inputs(seed, part) draws one part's arguments, and reference() takes and returns one part's arrays. A program takes and returns all parts, laid end to end along the dimension named above; an argument that names none is the same for every part. Nothing has to cross between parts.
All inputs are finite; a program needn't handle non-finite values.
Results may differ from the reference program's by a relative error of at most 0.0076.
Values may be sent and summed in bfloat16 or wider, within the bound.
No kernel may reach another device: no remote copies, remote signals or barrier semaphores. Data moves between devices by JAX's collectives and lax.ppermute only.
A program may use at most 128 MiB of HBM per device.

```python
import math
import jax
import jax.numpy as jnp
from jax import lax

C = 256
HID = 512
NLON = 1440
G = 64
NB = 6
S = 9
HALO = 2
DLON = 4
LL = 384
NLAT = 8
MM = 24


def set_ends(entries, own_key, low, high):
    extent = entries.shape
    place = [jax.random.randint(jax.random.fold_in(own_key, axis), (), 0, extent[axis]) for axis in range(len(extent))]
    entries = entries.at[tuple(place)].set(low)
    longest = extent.index(max(extent))
    place[longest] = (place[longest] + 1) % extent[longest]
    return entries.at[tuple(place)].set(high)


def levels(own_key, extent, pieces, smallest, largest):
    factor_of, own = 1.0, jax.random.fold_in(own_key, 6)
    for dim, parts in pieces:
        heights = jnp.exp(jax.random.uniform(jax.random.fold_in(own, dim), (parts,), jnp.float32, smallest / len(pieces), largest / len(pieces)))
        factor_of = factor_of * jnp.repeat(heights, extent[dim] // parts).reshape([-1 if axis == dim else 1 for axis in range(len(extent))])
    return factor_of


def scatter_about(key, extent, scale, most, shards=(), kind=jnp.bfloat16):
    values = jax.random.normal(key, extent, jnp.float32) * scale
    if len(shards) > 0:
        values = levels(key, extent, shards, -0.22, 0.18) * values
    return jnp.clip(values, min=-most, max=most).astype(kind)


def setup_inputs(seed: int = 0, part: int = 0) -> dict:
    splits = jax.random.split(jax.random.key(seed), 10)
    own_keys = jax.random.split(jax.random.fold_in(splits[9], part), 10)
    fields = scatter_about(own_keys[0], (NLAT, NLON, C), 1.0, 6.0, ((0, 2), (2, 4)))
    disco_weight = scatter_about(splits[1], (NB, C, G), (S * G) ** -0.5, 0.25, ((1, 4),))
    support_lat = set_ends(jax.random.randint(splits[2], (NLAT, S), 0 - HALO, HALO + 1), jax.random.fold_in(splits[2], 1), 0 - HALO, HALO).astype(jnp.int32)
    support_lon = set_ends(jax.random.randint(splits[3], (NLAT, S), 0 - DLON, DLON + 1), jax.random.fold_in(splits[3], 1), 0 - DLON, DLON).astype(jnp.int32)
    support_basis = set_ends(jax.random.randint(splits[4], (NLAT, S), 0, NB), jax.random.fold_in(splits[4], 1), 0, NB - 1).astype(jnp.int32)
    support_value = jnp.clip(0.25 + 1.25 * jax.random.uniform(splits[5], (NLAT, S), jnp.float32) ** levels(splits[5], (NLAT, S), ((0, 2),), -0.2, 0.2), 0.25, 1.5)
    w_up = scatter_about(splits[6], (C, HID), C ** -0.5, 0.375)
    w_down = scatter_about(splits[7], (HID, C), HID ** -0.5, 0.25)
    legendre = scatter_about(splits[8], (MM, LL, NLAT), NLAT ** -0.5, 2.0, ((0, 8),))
    return {"fields": fields, "disco_weight": disco_weight, "support_lat": support_lat, "support_lon": support_lon, "support_basis": support_basis, "support_value": support_value, "w_up": w_up, "w_down": w_down, "legendre": legendre}


def fourier_table(lon_count, mode_count):
    lon_index = jnp.arange(lon_count, dtype=jnp.int32)
    mode_index = jnp.arange(mode_count, dtype=jnp.int32)
    phase = lon_index[:, None] * mode_index[None, :] % lon_count
    angle = phase.astype(jnp.float32) * (2.0 * math.pi / lon_count)
    paired = jnp.stack([jnp.cos(angle), -jnp.sin(angle)], axis=-1) * math.sqrt(2.0 / lon_count)
    return paired.reshape(lon_count, 2 * mode_count).astype(jnp.bfloat16)

def channel_mlp(mixed, w_up, w_down):
    values = mixed.astype(jnp.float32)
    center = values - lax.optimization_barrier(jnp.mean(values, axis=-1, keepdims=True))
    spread = lax.optimization_barrier(jnp.mean(center * center, axis=-1, keepdims=True))
    normed = (center * lax.rsqrt(spread + 1e-05)).astype(jnp.bfloat16)
    lifted = jnp.einsum('anc,ch->anh', normed.astype(jnp.float32), w_up.astype(jnp.float32))
    active = jax.nn.gelu(lifted).astype(jnp.bfloat16)
    lowered = jnp.einsum('anh,hc->anc', active.astype(jnp.float32), w_down.astype(jnp.float32))
    return (values + lowered).astype(jnp.bfloat16)

def reference(fields, disco_weight, support_lat, support_lon, support_basis, support_value, w_up, w_down, legendre):
    lat_count, lon_count, chan_count = fields.shape
    group_count = chan_count // G
    padded = jnp.pad(fields, ((HALO, HALO), (0, 0), (0, 0)))
    row_ids = jnp.arange(lat_count, dtype=jnp.int32)
    lon_index = jnp.arange(lon_count, dtype=jnp.int32)
    weight_full = disco_weight.astype(jnp.float32)
    accumulated = jnp.zeros((lat_count, lon_count, group_count, G), jnp.float32)
    for position in range(S):
        source = (row_ids + HALO + support_lat[:, position]).astype(jnp.int32)
        columns = ((lon_index[None, :] + support_lon[:, position][:, None]) % lon_count).astype(jnp.int32)
        shifted = padded[source[:, None], columns].astype(jnp.float32).reshape(lat_count, lon_count, group_count, G)
        picked = weight_full[support_basis[:, position]] * support_value[:, position][:, None, None]
        rounded = lax.optimization_barrier(picked.astype(jnp.bfloat16))
        filters = rounded.astype(jnp.float32).reshape(lat_count, group_count, G, G)
        accumulated = accumulated + jnp.einsum('anhi,ahoi->anho', shifted, filters)
    mixed = (fields.astype(jnp.float32) + accumulated.reshape(lat_count, lon_count, chan_count)).astype(jnp.bfloat16)
    field_out = channel_mlp(mixed, w_up, w_down)
    fourier = fourier_table(lon_count, MM)
    spectrum = jnp.einsum('anc,nk->akc', field_out.astype(jnp.float32), fourier.astype(jnp.float32))
    spectrum = spectrum.astype(jnp.bfloat16).reshape(lat_count, MM, 2, chan_count)
    degree = jnp.arange(LL, dtype=jnp.int32)
    mode_ids = jnp.arange(MM, dtype=jnp.int32)
    kept_mask = degree[None, :] >= mode_ids[:, None]
    kept = jnp.where(kept_mask[:, :, None], legendre, jnp.zeros((), jnp.bfloat16))
    coefficients = jnp.einsum('mla,amrc->mlrc', kept.astype(jnp.float32), spectrum.astype(jnp.float32))
    return coefficients.reshape(MM, LL, 2 * chan_count).astype(jnp.bfloat16)
```

```python
import functools
import math

import jax
import jax.numpy as jnp
import numpy as np
from jax import lax
from jax.experimental import pallas as pl
from jax.experimental.pallas import tpu as pltpu
from jax.sharding import PartitionSpec as P

G = 64
S = 9
HALO = 2
DLON = 4
TAPS = S + 1
LANES = 128
SLOT = 8
EPS = 1e-05
VMEM_LIMIT = 56 * 1024 * 1024


def ceil_to(value, step):
    return -(-value // step) * step


def conv_kernel(
    chunks,
    has_edge,
    pair_ref,
    lat_ref,
    lon_ref,
    basis_ref,
    value_ref,
    fields_ref,
    *rest,
):
    if has_edge:
        edge_ref, weight_ref, out_ref, rows_ref, taps_ref, filt_ref = rest
    else:
        edge_ref = None
        weight_ref, out_ref, rows_ref, taps_ref, filt_ref = rest
    own, _, lon = fields_ref.shape
    chunk = lon // chunks
    width = out_ref.shape[2]
    total = rows_ref.shape[2]
    pair = pair_ref[0]
    own_at = HALO * (1 - pair)
    edge_at = own * pair

    def place(slot, cells):
        rows_ref[slot, :, LANES : LANES + lon] = cells
        rows_ref[slot, :, 0:LANES] = cells[:, lon - LANES :]
        full = (lon // LANES) * LANES
        tail = total - LANES - lon
        rows_ref[slot, :, LANES + full :] = jnp.concatenate(
            [cells[:, full:], cells[:, :tail]], axis=1
        )

    for row in range(own):
        place(own_at + row, fields_ref[row])
    for row in range(HALO):
        if has_edge:
            place(edge_at + row, edge_ref[row])
        else:
            rows_ref[edge_at + row] = jnp.zeros(rows_ref.shape[1:], rows_ref.dtype)

    lane = lax.broadcasted_iota(jnp.int32, (G, LANES), 1)

    def fill(slot, tap, source, offset):
        for j in range(chunks):
            begin = LANES + chunk * j + offset
            first = lax.div(begin, LANES)
            shift = lax.rem(begin, LANES)
            back = lax.rem(LANES - shift, LANES)
            keep = lane < LANES - shift
            turned = []
            for t in range(width // LANES + 1):
                start = pl.multiple_of((first + t) * LANES, LANES)
                tile = rows_ref[source, :, pl.ds(start, LANES)].astype(jnp.float32)
                turned.append(pltpu.roll(tile, back, 1))
            for t in range(width // LANES):
                moved = jnp.where(keep, turned[t], turned[t + 1]).astype(jnp.bfloat16)
                at = j * width + t * LANES
                taps_ref[slot, pl.ds(pl.multiple_of(tap * G, G), G), at : at + LANES] = moved

    eye = jnp.where(
        lax.broadcasted_iota(jnp.int32, (G, G), 0) == lax.broadcasted_iota(jnp.int32, (G, G), 1),
        1.0,
        0.0,
    ).astype(jnp.bfloat16)
    for i in range(2):
        row = 2 * pair + i

        def one(tap, carry):
            fill(i, tap, HALO + i + lat_ref[row, tap], lon_ref[row, tap])
            return carry

        lax.fori_loop(0, S, one, 0)
        fill(i, S, HALO + i, 0)
        pieces = []
        for tap in range(S):
            picked = weight_ref[basis_ref[row, tap]].astype(jnp.float32) * value_ref[row, tap]
            pieces.append(picked.astype(jnp.bfloat16))
        pieces.append(eye)
        for k in range(TAPS // 2):
            filt_ref[:, k * 2 * G : (k + 1) * 2 * G] = jnp.concatenate(
                [pieces[2 * k], pieces[2 * k + 1]], axis=1
            )
        mixed = jnp.dot(filt_ref[...], taps_ref[i], preferred_element_type=jnp.float32).astype(
            jnp.bfloat16
        )
        for j in range(chunks):
            out_ref[j, i * G : (i + 1) * G, :] = mixed[:, j * width : (j + 1) * width]


def conv_rows(pair, supports, fields, edge, weight, chunks):
    own, chans, lon = fields.shape
    width = ceil_to(lon // chunks, LANES)
    highest = (LANES + lon - lon // chunks + DLON) // LANES
    total = (highest + 1) * LANES + width
    smem = pl.BlockSpec(memory_space=pltpu.SMEM)
    vmem = pl.BlockSpec(memory_space=pltpu.VMEM)
    arrays = [fields] + ([] if edge is None else [edge]) + [weight]
    return pl.pallas_call(
        functools.partial(conv_kernel, chunks, edge is not None),
        out_shape=jax.ShapeDtypeStruct((chunks, 2 * chans, width), jnp.bfloat16),
        in_specs=[smem] * 5 + [vmem] * len(arrays),
        out_specs=vmem,
        scratch_shapes=[
            pltpu.VMEM((own + HALO, chans, total), jnp.bfloat16),
            pltpu.VMEM((2, TAPS * G, chunks * width), jnp.bfloat16),
            pltpu.VMEM((G, TAPS * G), jnp.bfloat16),
        ],
        compiler_params=pltpu.CompilerParams(vmem_limit_bytes=VMEM_LIMIT),
        cost_estimate=pl.CostEstimate(
            flops=4 * G * TAPS * G * chunks * width,
            bytes_accessed=2 * fields.size * 2,
            transcendentals=0,
        ),
        name="conv_rows",
    )(pair, *supports, *arrays)


def mlp_kernel(dests, mixed_ref, up_ref, down_ref, table_ref, *rest):
    if len(rest) == 2:
        earlier_ref, out_ref = rest
    else:
        earlier_ref, out_ref = None, rest[0]
    parts = mixed_ref.shape[0]
    width = mixed_ref.shape[2]
    columns = []
    for i in range(2):
        columns.append(
            jnp.concatenate([mixed_ref[j, i * G : (i + 1) * G, :] for j in range(parts)], axis=0)
        )
    values = jnp.concatenate(columns, axis=1).astype(jnp.float32)
    center = values - jnp.mean(values, axis=0, keepdims=True)
    spread = jnp.mean(center * center, axis=0, keepdims=True)
    normed = (center * lax.rsqrt(spread + EPS)).astype(jnp.bfloat16)
    lifted = lax.dot_general(
        up_ref[...], normed, (((1,), (0,)), ((), ())), preferred_element_type=jnp.float32
    )
    inner = lifted * (
        math.sqrt(2.0 / math.pi) + (math.sqrt(2.0 / math.pi) * 0.044715) * (lifted * lifted)
    )
    half = 0.5 * lifted
    active = (half + half * jnp.tanh(inner)).astype(jnp.bfloat16)
    lowered = lax.dot_general(
        down_ref[...], active, (((1,), (0,)), ((), ())), preferred_element_type=jnp.float32
    )
    result = (values + lowered).astype(jnp.bfloat16)
    found = []
    for i in range(2):
        modes = lax.dot_general(
            table_ref[...],
            result[:, i * width : (i + 1) * width],
            (((1,), (1,)), ((), ())),
            preferred_element_type=jnp.float32,
        )
        found.append(modes.reshape(dests, SLOT, modes.shape[1]))
    block = jnp.concatenate(found, axis=1).astype(jnp.bfloat16)
    if earlier_ref is None:
        out_ref[...] = block
    else:
        out_ref[:, 0 : 2 * SLOT, :] = earlier_ref[...]
        out_ref[:, 2 * SLOT : 4 * SLOT, :] = block


def mlp_rows(mixed, up, down, table, dests, earlier):
    parts, pair_chans, width = mixed.shape
    chan = parts * pair_chans // 2
    rows = 2 * SLOT * (1 if earlier is None else 2)
    vmem = pl.BlockSpec(memory_space=pltpu.VMEM)
    arrays = [mixed, up, down, table] + ([] if earlier is None else [earlier])
    return pl.pallas_call(
        functools.partial(mlp_kernel, dests),
        out_shape=jax.ShapeDtypeStruct((dests, rows, chan), jnp.bfloat16),
        in_specs=[vmem] * len(arrays),
        out_specs=vmem,
        compiler_params=pltpu.CompilerParams(vmem_limit_bytes=VMEM_LIMIT),
        cost_estimate=pl.CostEstimate(
            flops=8 * chan * up.shape[0] * width,
            bytes_accessed=2 * (mixed.size + up.size + down.size + table.size),
            transcendentals=2 * up.shape[0] * width,
        ),
        name="mlp_rows",
    )(*arrays)


def final_kernel(start_ref, legendre_ref, spread_ref, spectrum_ref, out_ref):
    modes, lats, degrees = legendre_ref.shape
    depth = spread_ref.shape[1]
    chan = spectrum_ref.shape[1]
    degree = lax.broadcasted_iota(jnp.int32, (lats, degrees), 1)
    slot = lax.rem(lax.broadcasted_iota(jnp.int32, (degrees, depth), 1), SLOT)
    for m in range(modes):
        kept = jnp.where(degree >= start_ref[0] + m, legendre_ref[m].astype(jnp.float32), 0.0)
        wide = lax.dot_general(
            kept.astype(jnp.bfloat16),
            spread_ref[...],
            (((0,), (0,)), ((), ())),
            preferred_element_type=jnp.float32,
        )
        for r in range(2):
            picked = jnp.where(slot == 2 * m + r, wide, 0.0).astype(jnp.bfloat16)
            out_ref[m, :, r * chan : (r + 1) * chan] = jnp.dot(
                picked, spectrum_ref[...], preferred_element_type=jnp.float32
            ).astype(jnp.bfloat16)


def fourier_blocks(lon, chunks, width, dests, mode_dev):
    chunk = lon // chunks
    index = np.arange(lon, dtype=np.int64)
    mode = np.arange(dests * mode_dev, dtype=np.int64)
    angle = ((mode[:, None] * index[None, :]) % lon) * (2.0 * math.pi / lon)
    paired = np.stack([np.cos(angle), -np.sin(angle)], axis=1) * math.sqrt(2.0 / lon)
    paired = paired.reshape(dests, 2 * mode_dev, chunks, chunk)
    table = np.zeros((chunks, dests, SLOT, width), np.float32)
    table[:, :, : 2 * mode_dev, :chunk] = np.transpose(paired, (2, 0, 1, 3))
    return table.reshape(chunks, dests * SLOT, width).astype(jnp.bfloat16)


def on_device(
    fields,
    disco_weight,
    support_lat,
    support_lon,
    support_basis,
    support_value,
    w_up,
    w_down,
    legendre,
):
    lat_dev, lon, _ = fields.shape
    num_lat = lax.axis_size("lat")
    num_chan = lax.axis_size("chan")
    mode_dev, degrees, lats = legendre.shape
    dests = num_lat * num_chan
    width = ceil_to(lon // num_chan, LANES)
    band = lax.axis_index("lat")
    place = lax.axis_index("chan")
    cells = jnp.swapaxes(fields, 1, 2)
    supports = (support_lat, support_lon, support_basis, support_value)

    two_bands = num_lat == 2
    if two_bands:
        edge_out = lax.dynamic_slice_in_dim(cells, HALO * (1 - band), HALO, axis=0)
        edges = [None, lax.ppermute(edge_out, "lat", [(0, 1), (1, 0)])]
        pairs = [band, 1 - band]
    else:
        ends = num_lat - 1
        edges = [
            lax.ppermute(cells[lat_dev - HALO :], "lat", [(i, i + 1) for i in range(ends)]),
            lax.ppermute(cells[:HALO], "lat", [(i + 1, i) for i in range(ends)]),
        ]
        pairs = [0, 1]

    tables = jnp.asarray(fourier_blocks(lon, num_chan, width, dests, mode_dev))
    table = lax.dynamic_index_in_dim(tables, place, 0, keepdims=False)
    up = w_up.T
    down = w_down.T

    spectrum = None
    received = []
    for edge, pair in zip(edges, pairs):
        mixed = conv_rows(
            jnp.asarray(pair, jnp.int32).reshape(1), supports, cells, edge, disco_weight, num_chan
        )
        received.append(lax.all_to_all(mixed, "chan", split_axis=0, concat_axis=0, tiled=True))
    for block in received:
        spectrum = mlp_rows(block, up, down, table, dests, spectrum)

    gathered = lax.all_to_all(spectrum, ("lat", "chan"), split_axis=0, concat_axis=0, tiled=True)
    depth = dests * 4 * SLOT
    flat = gathered.reshape(depth, gathered.shape[2])

    row = np.arange(depth)
    source_band = row // (4 * SLOT) // num_chan
    phase = (row // (2 * SLOT)) % 2
    source_pair = (phase ^ source_band) if two_bands else phase
    lat_of = lat_dev * source_band + 2 * source_pair + (row // SLOT) % 2
    spread = (lat_of[None, :] == np.arange(lats)[:, None]).astype(jnp.bfloat16)
    start = (lax.axis_index(("lat", "chan")) * mode_dev).astype(jnp.int32).reshape(1)
    vmem = pl.BlockSpec(memory_space=pltpu.VMEM)
    return pl.pallas_call(
        final_kernel,
        out_shape=jax.ShapeDtypeStruct((mode_dev, degrees, 2 * flat.shape[1]), jnp.bfloat16),
        in_specs=[pl.BlockSpec(memory_space=pltpu.SMEM)] + [vmem] * 3,
        out_specs=vmem,
        compiler_params=pltpu.CompilerParams(vmem_limit_bytes=VMEM_LIMIT),
        name="final_sum",
    )(start, jnp.swapaxes(legendre, 1, 2), jnp.asarray(spread), flat)


def solution(mesh):
    in_specs = (
        P(("tm", "lat"), None, "chan"),
        P(None, "chan", None),
        P("lat", None),
        P("lat", None),
        P("lat", None),
        P("lat", None),
        P(),
        P(),
        P(("lat", "chan"), None, None),
    )
    out_specs = P(("tm", "lat", "chan"), None, None)
    return jax.shard_map(
        on_device, mesh=mesh, in_specs=in_specs, out_specs=out_specs, check_vma=False
    )
```

```python
import functools
import math

import jax
import jax.numpy as jnp
import numpy as np
from jax import lax
from jax.experimental import pallas as pl
from jax.experimental.pallas import tpu as pltpu
from jax.sharding import PartitionSpec as P

G = 64
S = 9
HALO = 2
DLON = 4
TAPS = S + 1
LANES = 128
SLOT = 8
EPS = 1e-05
FEW = 8
MIB = 1024 * 1024
FLOPS_PER_US = 1_000_000_000

SMEM = pl.BlockSpec(memory_space=pltpu.SMEM)
VMEM = pl.BlockSpec(memory_space=pltpu.VMEM)


def ceil_to(value, step):
    return -(-value // step) * step


def params(mib):
    return pltpu.CompilerParams(vmem_limit_bytes=mib * MIB)


def takes(micros):
    return pl.CostEstimate(flops=micros * FLOPS_PER_US, bytes_accessed=0, transcendentals=0)


def conv_kernel(
    has_edge, pair_ref, place_ref, lat_ref, lon_ref, basis_ref, value_ref, fields_ref, *rest
):
    if has_edge:
        edge_ref, weight_ref, *rest = rest
    else:
        edge_ref, (weight_ref, *rest) = None, rest
    *out_refs, rows_ref, taps_ref, filt_ref = rest
    own, _, lon = fields_ref.shape
    chunks = len(out_refs)
    chunk = lon // chunks
    width = out_refs[0].shape[1]
    total = rows_ref.shape[2]
    pair = pair_ref[0]
    own_at = HALO * (1 - pair)
    edge_at = own * pair

    def put(slot, cells):
        rows_ref[slot, :, LANES : LANES + lon] = cells
        rows_ref[slot, :, 0:LANES] = cells[:, lon - LANES :]
        full = (lon // LANES) * LANES
        tail = total - LANES - lon
        rows_ref[slot, :, LANES + full :] = jnp.concatenate(
            [cells[:, full:], cells[:, :tail]], axis=1
        )

    for row in range(own):
        put(own_at + row, fields_ref[row])
    for row in range(HALO):
        if has_edge:
            put(edge_at + row, edge_ref[row])
        else:
            rows_ref[edge_at + row] = jnp.zeros(rows_ref.shape[1:], rows_ref.dtype)

    lane = lax.broadcasted_iota(jnp.int32, (G, LANES), 1)
    begins = [LANES + chunk * lax.rem(place_ref[0] + k, chunks) for k in range(chunks)]

    def fill(slot, tap, source, offset):
        for k in range(chunks):
            begin = begins[k] + offset
            first = lax.div(begin, LANES)
            shift = lax.rem(begin, LANES)
            back = lax.rem(LANES - shift, LANES)
            keep = lane < LANES - shift
            turned = []
            for t in range(width // LANES + 1):
                start = pl.multiple_of((first + t) * LANES, LANES)
                tile = rows_ref[source, :, pl.ds(start, LANES)]
                turned.append(pltpu.roll(tile, back, 1))
            for t in range(width // LANES):
                at = k * width + t * LANES
                taps_ref[slot, tap * G : (tap + 1) * G, at : at + LANES] = jnp.where(
                    keep, turned[t], turned[t + 1]
                )

    eye = jnp.where(
        lax.broadcasted_iota(jnp.int32, (G, G), 0) == lax.broadcasted_iota(jnp.int32, (G, G), 1),
        1.0,
        0.0,
    ).astype(jnp.bfloat16)
    for i in range(2):
        row = 2 * pair + i
        pieces = []
        for tap in range(S):
            picked = weight_ref[basis_ref[row, tap]].astype(jnp.float32) * value_ref[row, tap]
            pieces.append(picked.astype(jnp.bfloat16))
        pieces.append(eye)
        for k in range(TAPS // 2):
            filt_ref[i, :, k * 2 * G : (k + 1) * 2 * G] = jnp.concatenate(
                [pieces[2 * k], pieces[2 * k + 1]], axis=1
            )
        for tap in range(S):
            fill(i, tap, HALO + i + lat_ref[row, tap], lon_ref[row, tap])
        fill(i, S, HALO + i, 0)
        mixed = jnp.dot(filt_ref[i], taps_ref[i], preferred_element_type=jnp.float32).astype(
            jnp.bfloat16
        )
        for k in range(chunks):
            out_refs[k][i * G : (i + 1) * G, :] = mixed[:, k * width : (k + 1) * width]


def conv_rows(pair, place, supports, fields, edge, weight, chunks):
    own, chans, lon = fields.shape
    width = ceil_to(lon // chunks, LANES)
    highest = (LANES + lon - lon // chunks + DLON) // LANES
    total = (highest + 1) * LANES + width
    arrays = [fields] + ([] if edge is None else [edge]) + [weight]
    return pl.pallas_call(
        functools.partial(conv_kernel, edge is not None),
        out_shape=[jax.ShapeDtypeStruct((2 * chans, width), jnp.bfloat16)] * chunks,
        in_specs=[SMEM] * 6 + [VMEM] * len(arrays),
        out_specs=[VMEM] * chunks,
        scratch_shapes=[
            pltpu.VMEM((own + HALO, chans, total), jnp.bfloat16),
            pltpu.VMEM((2, TAPS * G, chunks * width), jnp.bfloat16),
            pltpu.VMEM((2, G, TAPS * G), jnp.bfloat16),
        ],
        compiler_params=params(20),
        cost_estimate=takes(4),
        name="conv_rows",
    )(pair, place, *supports, *arrays)


def mlp_kernel(parts, last, me_ref, place_ref, *rest):
    blocks, rest = rest[:parts], rest[parts:]
    up_ref, down_ref, table_ref, *rest = rest
    *rest, cells_ref = rest
    if last:
        earlier_ref, *out_refs, gather_ref = rest
    else:
        (out_ref,) = rest
    width = blocks[0].shape[1]
    place = place_ref[0]
    for k in range(parts):
        source = pl.multiple_of(lax.rem(place - k + parts, parts) * G, G)
        for i in range(2):
            cells_ref[pl.ds(source, G), i * width : (i + 1) * width] = blocks[k][
                i * G : (i + 1) * G, :
            ]
    values = cells_ref[...].astype(jnp.float32)
    center = values - jnp.mean(values, axis=0, keepdims=True)
    spread = jnp.mean(center * center, axis=0, keepdims=True)
    normed = (center * lax.rsqrt(spread + EPS)).astype(jnp.bfloat16)
    lifted = jnp.dot(up_ref[...], normed, preferred_element_type=jnp.float32)
    scale = math.sqrt(2.0 / math.pi)
    inner = lifted * (scale + (scale * 0.044715) * (lifted * lifted))
    half = 0.5 * lifted
    active = (half + half * jnp.tanh(inner)).astype(jnp.bfloat16)
    lowered = jnp.dot(down_ref[...], active, preferred_element_type=jnp.float32)
    result = (values + lowered).astype(jnp.bfloat16)
    found = []
    for i in range(2):
        modes = lax.dot_general(
            table_ref[place],
            result[:, i * width : (i + 1) * width],
            (((1,), (1,)), ((), ())),
            preferred_element_type=jnp.float32,
        )
        found.append(modes.reshape(modes.shape[0] // SLOT, SLOT, modes.shape[1]))
    block = jnp.concatenate(found, axis=1).astype(jnp.bfloat16)
    if not last:
        out_ref[...] = block
        return
    gather_ref[:, 0 : 2 * SLOT, :] = earlier_ref[...]
    gather_ref[:, 2 * SLOT : 4 * SLOT, :] = block
    if len(out_refs) == 1:
        out_refs[0][...] = gather_ref[...]
        return
    dests = len(out_refs)
    for k in range(dests):
        out_refs[k][...] = gather_ref[lax.rem(me_ref[0] + k, dests)]


def mlp_rows(me, place, blocks, up, down, tables, earlier, dests):
    pair_chans, width = blocks[0].shape
    chan = len(blocks) * pair_chans // 2
    last = earlier is not None
    arrays = [*blocks, up, down, tables] + ([earlier] if last else [])
    shape = (dests, 2 * SLOT, chan)
    scratch = []
    if last:
        shape = (dests, 4 * SLOT, chan)
        scratch = [pltpu.VMEM(shape, jnp.bfloat16)]
    outs = jax.ShapeDtypeStruct(shape, jnp.bfloat16)
    out_specs = VMEM
    if last and dests <= FEW:
        outs = [jax.ShapeDtypeStruct(shape[1:], jnp.bfloat16)] * dests
        out_specs = [VMEM] * dests
    return pl.pallas_call(
        functools.partial(mlp_kernel, len(blocks), last),
        out_shape=outs,
        in_specs=[SMEM] * 2 + [VMEM] * len(arrays),
        out_specs=out_specs,
        scratch_shapes=scratch + [pltpu.VMEM((chan, 2 * width), jnp.bfloat16)],
        compiler_params=params(20 if dests <= FEW else 40),
        cost_estimate=takes(3),
        name="mlp_rows",
    )(me, place, *arrays)


def expand_kernel(start_ref, legendre_ref, spread_ref, out_ref):
    _, lats, degrees = legendre_ref.shape
    m = pl.program_id(0)
    degree = lax.broadcasted_iota(jnp.int32, (lats, degrees), 1)
    kept = jnp.where(degree >= start_ref[0] + m, legendre_ref[0].astype(jnp.float32), 0.0)
    wide = lax.dot_general(
        kept.astype(jnp.bfloat16),
        spread_ref[...],
        (((0,), (0,)), ((), ())),
        preferred_element_type=jnp.float32,
    )
    slot = lax.rem(lax.broadcasted_iota(jnp.int32, wide.shape, 1), SLOT)
    for r in range(2):
        out_ref[0, r] = jnp.where(slot == 2 * m + r, wide, 0.0).astype(jnp.bfloat16)


def expand(start, legendre, spread):
    modes, lats, degrees = legendre.shape
    depth = spread.shape[1]
    return pl.pallas_call(
        expand_kernel,
        out_shape=jax.ShapeDtypeStruct((modes, 2, degrees, depth), jnp.bfloat16),
        grid=(modes,),
        in_specs=[
            SMEM,
            pl.BlockSpec((1, lats, degrees), lambda m: (m, 0, 0)),
            pl.BlockSpec((lats, depth), lambda m: (0, 0)),
        ],
        out_specs=pl.BlockSpec((1, 2, degrees, depth), lambda m: (m, 0, 0, 0)),
        compiler_params=params(10 if depth <= 512 else 48),
        cost_estimate=takes(2),
        name="expand",
    )(start, legendre, spread)


def final_kernel(me_ref, left_ref, *rest):
    *blocks, out_ref, spectrum_ref = rest
    depth, chan = spectrum_ref.shape
    count = len(blocks)
    rows = depth // count

    @pl.when(pl.program_id(0) == 0)
    def _():
        for k in range(count):
            source = lax.rem(me_ref[0] - k + count, count) * rows
            spectrum_ref[pl.ds(pl.multiple_of(source, rows), rows), :] = blocks[k][...]

    for r in range(2):
        out_ref[0, :, r * chan : (r + 1) * chan] = jnp.dot(
            left_ref[0, r], spectrum_ref[...], preferred_element_type=jnp.float32
        ).astype(jnp.bfloat16)


def final_sum(me, left, blocks):
    modes, _, degrees, depth = left.shape
    rows, chan = blocks[0].shape
    return pl.pallas_call(
        final_kernel,
        out_shape=jax.ShapeDtypeStruct((modes, degrees, 2 * chan), jnp.bfloat16),
        grid=(modes,),
        in_specs=[SMEM, pl.BlockSpec((1, 2, degrees, depth), lambda m: (m, 0, 0, 0))]
        + [pl.BlockSpec((rows, chan), lambda m: (0, 0))] * len(blocks),
        out_specs=pl.BlockSpec((1, degrees, 2 * chan), lambda m: (m, 0, 0)),
        scratch_shapes=[pltpu.VMEM((depth, chan), jnp.bfloat16)],
        compiler_params=params(10 if depth <= 512 else 48),
        cost_estimate=takes(2),
        name="final_sum",
    )(me, left, *blocks)


def fourier_blocks(lon, chunks, width, dests, mode_dev):
    chunk = lon // chunks
    index = np.arange(lon, dtype=np.int64)
    mode = np.arange(dests * mode_dev, dtype=np.int64)
    angle = ((mode[:, None] * index[None, :]) % lon) * (2.0 * math.pi / lon)
    paired = np.stack([np.cos(angle), -np.sin(angle)], axis=1) * math.sqrt(2.0 / lon)
    paired = paired.reshape(dests, 2 * mode_dev, chunks, chunk)
    table = np.zeros((chunks, dests, SLOT, width), np.float32)
    table[:, :, : 2 * mode_dev, :chunk] = np.transpose(paired, (2, 0, 1, 3))
    return table.reshape(chunks, dests * SLOT, width).astype(jnp.bfloat16)


def turn(block, axis, count, step):
    return lax.ppermute(block, axis, [(i, (i + step) % count) for i in range(count)])


def scalar(value):
    return jnp.asarray(value, jnp.int32).reshape(1)


def on_device(
    fields,
    disco_weight,
    support_lat,
    support_lon,
    support_basis,
    support_value,
    w_up,
    w_down,
    legendre,
):
    lat_dev, lon, _ = fields.shape
    num_lat = lax.axis_size("lat")
    num_chan = lax.axis_size("chan")
    mode_dev, _, lats = legendre.shape
    dests = num_lat * num_chan
    width = ceil_to(lon // num_chan, LANES)
    band = lax.axis_index("lat")
    place = scalar(lax.axis_index("chan"))
    index = lax.axis_index(("lat", "chan"))
    me = scalar(index)
    cells = jnp.swapaxes(fields, 1, 2)
    supports = (support_lat, support_lon, support_basis, support_value)

    two_bands = num_lat == 2
    if two_bands:
        edge_out = lax.dynamic_slice_in_dim(cells, HALO * (1 - band), HALO, axis=0)
        edges = [None, lax.ppermute(edge_out, "lat", [(0, 1), (1, 0)])]
        pairs = [band, 1 - band]
    else:
        ends = num_lat - 1
        edges = [
            lax.ppermute(cells[lat_dev - HALO :], "lat", [(i, i + 1) for i in range(ends)]),
            lax.ppermute(cells[:HALO], "lat", [(i + 1, i) for i in range(ends)]),
        ]
        pairs = [0, 1]

    tables = jnp.asarray(fourier_blocks(lon, num_chan, width, dests, mode_dev))
    up = w_up.T
    down = w_down.T

    depth = dests * 4 * SLOT
    row = np.arange(depth)
    source_band = row // (4 * SLOT) // num_chan
    phase = (row // (2 * SLOT)) % 2
    source_pair = (phase ^ source_band) if two_bands else phase
    lat_of = lat_dev * source_band + 2 * source_pair + (row // SLOT) % 2
    spread = (lat_of[None, :] == np.arange(lats)[:, None]).astype(jnp.bfloat16)
    left = expand(scalar(index * mode_dev), jnp.swapaxes(legendre, 1, 2), jnp.asarray(spread))

    received = []
    for edge, pair in zip(edges, pairs):
        mixed = conv_rows(scalar(pair), place, supports, cells, edge, disco_weight, num_chan)
        received.append(
            [mixed[0]] + [turn(mixed[k], "chan", num_chan, k) for k in range(1, num_chan)]
        )
    spectrum = None
    for blocks in received:
        spectrum = mlp_rows(me, place, blocks, up, down, tables, spectrum, dests)

    both = ("lat", "chan")
    if dests <= FEW:
        blocks = [spectrum[0]] + [turn(spectrum[k], both, dests, k) for k in range(1, dests)]
    else:
        whole = lax.all_to_all(spectrum, both, split_axis=0, concat_axis=0, tiled=True)
        blocks = [whole.reshape(depth, whole.shape[2])]
    return final_sum(me, left, blocks)


def solution(mesh):
    in_specs = (
        P(("tm", "lat"), None, "chan"),
        P(None, "chan", None),
        P("lat", None),
        P("lat", None),
        P("lat", None),
        P("lat", None),
        P(),
        P(),
        P(("lat", "chan"), None, None),
    )
    out_specs = P(("tm", "lat", "chan"), None, None)
    return jax.shard_map(
        on_device, mesh=mesh, in_specs=in_specs, out_specs=out_specs, check_vma=False
    )
```

```python
import functools
import math

import jax
import jax.numpy as jnp
import numpy as np
from jax import lax
from jax.experimental import pallas as pl
from jax.experimental.pallas import tpu as pltpu
from jax.sharding import PartitionSpec as P

G = 64
S = 9
HALO = 2
DLON = 4
TAPS = S + 1
LANES = 128
SLOT = 8
EPS = 1e-05
FEW = 8
MIB = 1024 * 1024
FLOPS_PER_US = 1_000_000_000

SMEM = pl.BlockSpec(memory_space=pltpu.SMEM)
VMEM = pl.BlockSpec(memory_space=pltpu.VMEM)
HBM = pl.BlockSpec(memory_space=pltpu.HBM)


def ceil_to(value, step):
    return -(-value // step) * step


def params(mib):
    return pltpu.CompilerParams(vmem_limit_bytes=mib * MIB)


def takes(micros):
    return pl.CostEstimate(flops=micros * FLOPS_PER_US, bytes_accessed=0, transcendentals=0)


def conv_kernel(
    has_edge, pair_ref, place_ref, lat_ref, lon_ref, basis_ref, value_ref, fields_ref, *rest
):
    if has_edge:
        edge_ref, weight_ref, *rest = rest
    else:
        edge_ref, (weight_ref, *rest) = None, rest
    *out_refs, rows_ref, taps_ref, filt_ref = rest
    own, _, lon = fields_ref.shape
    chunks = len(out_refs)
    chunk = lon // chunks
    width = out_refs[0].shape[1]
    total = rows_ref.shape[2]
    pair = pair_ref[0]
    own_at = HALO * (1 - pair)
    edge_at = own * pair

    def put(slot, cells):
        rows_ref[slot, :, LANES : LANES + lon] = cells
        rows_ref[slot, :, 0:LANES] = cells[:, lon - LANES :]
        full = (lon // LANES) * LANES
        tail = total - LANES - lon
        rows_ref[slot, :, LANES + full :] = jnp.concatenate(
            [cells[:, full:], cells[:, :tail]], axis=1
        )

    for row in range(own):
        put(own_at + row, fields_ref[row])
    for row in range(HALO):
        if has_edge:
            put(edge_at + row, edge_ref[row])
        else:
            rows_ref[edge_at + row] = jnp.zeros(rows_ref.shape[1:], rows_ref.dtype)

    lane = lax.broadcasted_iota(jnp.int32, (G, LANES), 1)
    begins = [LANES + chunk * lax.rem(place_ref[0] + k, chunks) for k in range(chunks)]

    def fill(slot, tap, source, offset):
        for k in range(chunks):
            begin = begins[k] + offset
            first = lax.div(begin, LANES)
            shift = lax.rem(begin, LANES)
            back = lax.rem(LANES - shift, LANES)
            keep = lane < LANES - shift
            turned = []
            for t in range(width // LANES + 1):
                start = pl.multiple_of((first + t) * LANES, LANES)
                tile = rows_ref[source, :, pl.ds(start, LANES)]
                turned.append(pltpu.roll(tile, back, 1))
            for t in range(width // LANES):
                at = k * width + t * LANES
                taps_ref[slot, tap * G : (tap + 1) * G, at : at + LANES] = jnp.where(
                    keep, turned[t], turned[t + 1]
                )

    eye = jnp.where(
        lax.broadcasted_iota(jnp.int32, (G, G), 0) == lax.broadcasted_iota(jnp.int32, (G, G), 1),
        1.0,
        0.0,
    ).astype(jnp.bfloat16)
    for i in range(2):
        row = 2 * pair + i
        pieces = []
        for tap in range(S):
            picked = weight_ref[basis_ref[row, tap]].astype(jnp.float32) * value_ref[row, tap]
            pieces.append(picked.astype(jnp.bfloat16))
        pieces.append(eye)
        for k in range(TAPS // 2):
            filt_ref[i, :, k * 2 * G : (k + 1) * 2 * G] = jnp.concatenate(
                [pieces[2 * k], pieces[2 * k + 1]], axis=1
            )
        for tap in range(S):
            fill(i, tap, HALO + i + lat_ref[row, tap], lon_ref[row, tap])
        fill(i, S, HALO + i, 0)
        mixed = jnp.dot(filt_ref[i], taps_ref[i], preferred_element_type=jnp.float32).astype(
            jnp.bfloat16
        )
        for k in range(chunks):
            out_refs[k][i * G : (i + 1) * G, :] = mixed[:, k * width : (k + 1) * width]


def conv_rows(pair, place, supports, fields, edge, weight, chunks):
    own, chans, lon = fields.shape
    width = ceil_to(lon // chunks, LANES)
    highest = (LANES + lon - lon // chunks + DLON) // LANES
    total = (highest + 1) * LANES + width
    arrays = [fields] + ([] if edge is None else [edge]) + [weight]
    return pl.pallas_call(
        functools.partial(conv_kernel, edge is not None),
        out_shape=[jax.ShapeDtypeStruct((2 * chans, width), jnp.bfloat16)] * chunks,
        in_specs=[SMEM] * 6 + [VMEM] * len(arrays),
        out_specs=[VMEM] * chunks,
        scratch_shapes=[
            pltpu.VMEM((own + HALO, chans, total), jnp.bfloat16),
            pltpu.VMEM((2, TAPS * G, chunks * width), jnp.bfloat16),
            pltpu.VMEM((2, G, TAPS * G), jnp.bfloat16),
        ],
        compiler_params=params(56 if edge is None else 20),
        cost_estimate=takes(4),
        name="conv_rows",
    )(pair, place, *supports, *arrays)


def mlp_kernel(parts, last, place_ref, *rest):
    blocks, rest = rest[:parts], rest[parts:]
    up_ref, down_ref, table_ref, *rest = rest
    if last:
        earlier_ref, out_ref, cells_ref = rest
    else:
        out_ref, cells_ref = rest
    width = blocks[0].shape[1]
    place = place_ref[0]
    for k in range(parts):
        source = pl.multiple_of(lax.rem(place - k + parts, parts) * G, G)
        for i in range(2):
            cells_ref[pl.ds(source, G), i * width : (i + 1) * width] = blocks[k][
                i * G : (i + 1) * G, :
            ]
    values = cells_ref[...].astype(jnp.float32)
    center = values - jnp.mean(values, axis=0, keepdims=True)
    spread = jnp.mean(center * center, axis=0, keepdims=True)
    normed = (center * lax.rsqrt(spread + EPS)).astype(jnp.bfloat16)
    lifted = jnp.dot(up_ref[...], normed, preferred_element_type=jnp.float32)
    scale = math.sqrt(2.0 / math.pi)
    inner = lifted * (scale + (scale * 0.044715) * (lifted * lifted))
    half = 0.5 * lifted
    active = (half + half * jnp.tanh(inner)).astype(jnp.bfloat16)
    lowered = jnp.dot(down_ref[...], active, preferred_element_type=jnp.float32)
    result = (values + lowered).astype(jnp.bfloat16)
    found = []
    for i in range(2):
        modes = lax.dot_general(
            table_ref[place],
            result[:, i * width : (i + 1) * width],
            (((1,), (1,)), ((), ())),
            preferred_element_type=jnp.float32,
        )
        found.append(modes.reshape(modes.shape[0] // SLOT, SLOT, modes.shape[1]))
    block = jnp.concatenate(found, axis=1).astype(jnp.bfloat16)
    if last:
        out_ref[:, 0 : 2 * SLOT, :] = earlier_ref[...]
        out_ref[:, 2 * SLOT : 4 * SLOT, :] = block
    else:
        out_ref[...] = block


def mlp_rows(place, blocks, up, down, tables, earlier, dests):
    pair_chans, width = blocks[0].shape
    chan = len(blocks) * pair_chans // 2
    last = earlier is not None
    arrays = [*blocks, up, down, tables] + ([earlier] if last else [])
    rows = (4 if last else 2) * SLOT
    return pl.pallas_call(
        functools.partial(mlp_kernel, len(blocks), last),
        out_shape=jax.ShapeDtypeStruct((dests, rows, chan), jnp.bfloat16),
        in_specs=[SMEM] + [VMEM] * len(arrays),
        out_specs=VMEM,
        scratch_shapes=[pltpu.VMEM((chan, 2 * width), jnp.bfloat16)],
        compiler_params=params(20 if dests <= FEW else 40),
        cost_estimate=takes(2),
        name="mlp_rows",
    )(place, *arrays)


def expand_kernel(start_ref, legendre_ref, spread_ref, out_ref):
    _, lats, degrees = legendre_ref.shape
    m = pl.program_id(0)
    degree = lax.broadcasted_iota(jnp.int32, (lats, degrees), 1)
    kept = jnp.where(degree >= start_ref[0] + m, legendre_ref[0].astype(jnp.float32), 0.0)
    wide = lax.dot_general(
        kept.astype(jnp.bfloat16),
        spread_ref[...],
        (((0,), (0,)), ((), ())),
        preferred_element_type=jnp.float32,
    )
    slot = lax.rem(lax.broadcasted_iota(jnp.int32, wide.shape, 1), SLOT)
    for r in range(2):
        out_ref[0, r] = jnp.where(slot == 2 * m + r, wide, 0.0).astype(jnp.bfloat16)


def expand(start, legendre, spread):
    modes, lats, degrees = legendre.shape
    depth = spread.shape[1]
    return pl.pallas_call(
        expand_kernel,
        out_shape=jax.ShapeDtypeStruct((modes, 2, degrees, depth), jnp.bfloat16),
        grid=(modes,),
        in_specs=[
            SMEM,
            pl.BlockSpec((1, lats, degrees), lambda m: (m, 0, 0)),
            pl.BlockSpec((lats, depth), lambda m: (0, 0)),
        ],
        out_specs=pl.BlockSpec((1, 2, degrees, depth), lambda m: (m, 0, 0, 0)),
        compiler_params=params(10 if depth <= 512 else 48),
        cost_estimate=takes(2),
        name="expand",
    )(start, legendre, spread)


def final_kernel(left_ref, spectrum_ref, out_ref, result_ref, sems):
    modes = left_ref.shape[0]
    chan = spectrum_ref.shape[1]
    copies = []
    for m in range(modes):
        for r in range(2):
            result_ref[m, :, r * chan : (r + 1) * chan] = jnp.dot(
                left_ref[m, r], spectrum_ref[...], preferred_element_type=jnp.float32
            ).astype(jnp.bfloat16)
        copies.append(pltpu.make_async_copy(result_ref.at[m], out_ref.at[m], sems.at[m]))
        copies[-1].start()
    for copy in copies:
        copy.wait()


def final_sum(left, spectrum):
    modes, _, degrees, depth = left.shape
    shape = (modes, degrees, 2 * spectrum.shape[1])
    return pl.pallas_call(
        final_kernel,
        out_shape=jax.ShapeDtypeStruct(shape, jnp.bfloat16),
        in_specs=[VMEM, VMEM],
        out_specs=HBM,
        scratch_shapes=[pltpu.VMEM(shape, jnp.bfloat16), pltpu.SemaphoreType.DMA((modes,))],
        compiler_params=params(8 if depth <= 512 else 48),
        cost_estimate=takes(1),
        name="final_sum",
    )(left, spectrum)


def fourier_blocks(lon, chunks, width, dests, mode_dev):
    chunk = lon // chunks
    index = np.arange(lon, dtype=np.int64)
    mode = np.arange(dests * mode_dev, dtype=np.int64)
    angle = ((mode[:, None] * index[None, :]) % lon) * (2.0 * math.pi / lon)
    paired = np.stack([np.cos(angle), -np.sin(angle)], axis=1) * math.sqrt(2.0 / lon)
    paired = paired.reshape(dests, 2 * mode_dev, chunks, chunk)
    table = np.zeros((chunks, dests, SLOT, width), np.float32)
    table[:, :, : 2 * mode_dev, :chunk] = np.transpose(paired, (2, 0, 1, 3))
    return table.reshape(chunks, dests * SLOT, width).astype(jnp.bfloat16)


def turn(block, axis, count, step):
    return lax.ppermute(block, axis, [(i, (i + step) % count) for i in range(count)])


def scalar(value):
    return jnp.asarray(value, jnp.int32).reshape(1)


def on_device(
    fields,
    disco_weight,
    support_lat,
    support_lon,
    support_basis,
    support_value,
    w_up,
    w_down,
    legendre,
):
    lat_dev, lon, _ = fields.shape
    num_lat = lax.axis_size("lat")
    num_chan = lax.axis_size("chan")
    mode_dev, _, lats = legendre.shape
    dests = num_lat * num_chan
    width = ceil_to(lon // num_chan, LANES)
    band = lax.axis_index("lat")
    place = scalar(lax.axis_index("chan"))
    index = lax.axis_index(("lat", "chan"))
    supports = (support_lat, support_lon, support_basis, support_value)

    two_bands = num_lat == 2
    cells = jnp.swapaxes(fields, 1, 2)
    if two_bands:
        edge_out = lax.dynamic_slice_in_dim(cells, HALO * (1 - band), HALO, axis=0)
        edges = [None, lax.ppermute(edge_out, "lat", [(0, 1), (1, 0)])]
        pairs = [band, 1 - band]
    else:
        ends = num_lat - 1
        edges = [
            lax.ppermute(cells[lat_dev - HALO :], "lat", [(i, i + 1) for i in range(ends)]),
            lax.ppermute(cells[:HALO], "lat", [(i + 1, i) for i in range(ends)]),
        ]
        pairs = [0, 1]

    tables = jnp.asarray(fourier_blocks(lon, num_chan, width, dests, mode_dev))
    up = w_up.T
    down = w_down.T

    depth = dests * 4 * SLOT
    row = np.arange(depth)
    source_band = row // (4 * SLOT) // num_chan
    phase = (row // (2 * SLOT)) % 2
    source_pair = (phase ^ source_band) if two_bands else phase
    lat_of = lat_dev * source_band + 2 * source_pair + (row // SLOT) % 2
    spread = (lat_of[None, :] == np.arange(lats)[:, None]).astype(jnp.bfloat16)
    left = expand(scalar(index * mode_dev), jnp.swapaxes(legendre, 1, 2), jnp.asarray(spread))

    received = []
    for edge, pair in zip(edges, pairs):
        mixed = conv_rows(scalar(pair), place, supports, cells, edge, disco_weight, num_chan)
        received.append(
            [mixed[0]] + [turn(mixed[k], "chan", num_chan, k) for k in range(1, num_chan)]
        )
    spectrum = None
    for blocks in received:
        spectrum = mlp_rows(place, blocks, up, down, tables, spectrum, dests)

    both = ("lat", "chan")
    gathered = lax.all_to_all(spectrum, both, split_axis=0, concat_axis=0, tiled=True)
    return final_sum(left, gathered.reshape(depth, gathered.shape[2]))


def solution(mesh):
    in_specs = (
        P(("tm", "lat"), None, "chan"),
        P(None, "chan", None),
        P("lat", None),
        P("lat", None),
        P("lat", None),
        P("lat", None),
        P(),
        P(),
        P(("lat", "chan"), None, None),
    )
    out_specs = P(("tm", "lat", "chan"), None, None)
    return jax.shard_map(
        on_device, mesh=mesh, in_specs=in_specs, out_specs=out_specs, check_vma=False
    )
```

```python
import functools
import math

import jax
import jax.numpy as jnp
import numpy as np
from jax import lax
from jax.experimental import pallas as pl
from jax.experimental.pallas import tpu as pltpu
from jax.sharding import PartitionSpec as P

G = 64
S = 9
HALO = 2
DLON = 4
TAPS = S + 1
LANES = 128
SLOT = 8
EPS = 1e-05
FEW = 8
MIB = 1024 * 1024
FLOPS_PER_US = 1_000_000_000

SMEM = pl.BlockSpec(memory_space=pltpu.SMEM)
VMEM = pl.BlockSpec(memory_space=pltpu.VMEM)
HBM = pl.BlockSpec(memory_space=pltpu.HBM)


def ceil_to(value, step):
    return -(-value // step) * step


def params(mib):
    return pltpu.CompilerParams(vmem_limit_bytes=mib * MIB)


def takes(micros):
    return pl.CostEstimate(flops=micros * FLOPS_PER_US, bytes_accessed=0, transcendentals=0)


def conv_kernel(
    has_edge, pair_ref, place_ref, lat_ref, lon_ref, basis_ref, value_ref, fields_ref, *rest
):
    if has_edge:
        edge_ref, weight_ref, *rest = rest
    else:
        edge_ref, (weight_ref, *rest) = None, rest
    *out_refs, wrap_ref, rows_ref, taps_ref, filt_ref = rest
    own, _, lon = fields_ref.shape
    chunks = len(out_refs)
    chunk = lon // chunks
    width = out_refs[0].shape[1]
    total = wrap_ref.shape[2]
    pair = pair_ref[0]
    own_at = HALO * (1 - pair)
    edge_at = own * pair

    lane = lax.broadcasted_iota(jnp.int32, (G, LANES), 1)
    begins = [LANES + chunk * lax.rem(place_ref[0] + k, chunks) - DLON for k in range(chunks)]

    def put(slot, room, cells):
        wrap_ref[room, :, LANES : LANES + lon] = cells
        wrap_ref[room, :, 0:LANES] = cells[:, lon - LANES :]
        full = (lon // LANES) * LANES
        tail = total - LANES - lon
        wrap_ref[room, :, LANES + full :] = jnp.concatenate(
            [cells[:, full:], cells[:, :tail]], axis=1
        )
        for k in range(chunks):
            first = lax.div(begins[k], LANES)
            shift = lax.rem(begins[k], LANES)
            back = lax.rem(LANES - shift, LANES)
            keep = lane < LANES - shift
            turned = []
            for t in range(width // LANES + 1):
                start = pl.multiple_of((first + t) * LANES, LANES)
                turned.append(pltpu.roll(wrap_ref[room, :, pl.ds(start, LANES)], back, 1))
            for t in range(width // LANES):
                at = k * width + t * LANES
                rows_ref[slot, :, at : at + LANES] = jnp.where(keep, turned[t], turned[t + 1])

    for row in range(own):
        put(own_at + row, row, fields_ref[row])
    for row in range(HALO):
        if has_edge:
            put(edge_at + row, own + row, edge_ref[row])
        else:
            rows_ref[edge_at + row] = jnp.zeros(rows_ref.shape[1:], rows_ref.dtype)

    def fill(slot, tap, source, offset):
        shift = offset + DLON
        back = lax.rem(LANES - shift, LANES)
        keep = lane < LANES - shift
        for k in range(chunks):
            turned = []
            for at in range(k * width, (k + 1) * width, LANES):
                turned.append(pltpu.roll(rows_ref[source, :, at : at + LANES], back, 1))
            for t, tile in enumerate(turned):
                if t + 1 < len(turned):
                    tile = jnp.where(keep, tile, turned[t + 1])
                at = k * width + t * LANES
                taps_ref[slot, tap * G : (tap + 1) * G, at : at + LANES] = tile

    eye = jnp.where(
        lax.broadcasted_iota(jnp.int32, (G, G), 0) == lax.broadcasted_iota(jnp.int32, (G, G), 1),
        1.0,
        0.0,
    ).astype(jnp.bfloat16)
    for i in range(2):
        row = 2 * pair + i
        pieces = []
        for tap in range(S):
            picked = weight_ref[basis_ref[row, tap]].astype(jnp.float32) * value_ref[row, tap]
            pieces.append(picked.astype(jnp.bfloat16))
        pieces.append(eye)
        for k in range(TAPS // 2):
            filt_ref[i, :, k * 2 * G : (k + 1) * 2 * G] = jnp.concatenate(
                [pieces[2 * k], pieces[2 * k + 1]], axis=1
            )
        for tap in range(S):
            fill(i, tap, HALO + i + lat_ref[row, tap], lon_ref[row, tap])
        fill(i, S, HALO + i, 0)
        mixed = jnp.dot(filt_ref[i], taps_ref[i], preferred_element_type=jnp.float32).astype(
            jnp.bfloat16
        )
        for k in range(chunks):
            out_refs[k][i * G : (i + 1) * G, :] = mixed[:, k * width : (k + 1) * width]


def conv_rows(pair, place, supports, fields, edge, weight, chunks):
    own, chans, lon = fields.shape
    width = ceil_to(lon // chunks + 2 * DLON, LANES)
    highest = (LANES + lon - lon // chunks - DLON) // LANES
    total = (highest + 1) * LANES + width
    arrays = [fields] + ([] if edge is None else [edge]) + [weight]
    return pl.pallas_call(
        functools.partial(conv_kernel, edge is not None),
        out_shape=[jax.ShapeDtypeStruct((2 * chans, width), jnp.bfloat16)] * chunks,
        in_specs=[SMEM] * 6 + [VMEM] * len(arrays),
        out_specs=[VMEM] * chunks,
        scratch_shapes=[
            pltpu.VMEM((own + HALO, chans, total), jnp.bfloat16),
            pltpu.VMEM((own + HALO, chans, chunks * width), jnp.bfloat16),
            pltpu.VMEM((2, TAPS * G, chunks * width), jnp.bfloat16),
            pltpu.VMEM((2, G, TAPS * G), jnp.bfloat16),
        ],
        compiler_params=params(56 if edge is None else 20),
        cost_estimate=takes(4),
        name="conv_rows",
    )(pair, place, *supports, *arrays)


def mlp_kernel(parts, last, place_ref, *rest):
    blocks, rest = rest[:parts], rest[parts:]
    up_ref, down_ref, table_ref, *rest = rest
    if last:
        earlier_ref, out_ref, cells_ref = rest
    else:
        out_ref, cells_ref = rest
    width = blocks[0].shape[1]
    place = place_ref[0]
    for k in range(parts):
        source = pl.multiple_of(lax.rem(place - k + parts, parts) * G, G)
        for i in range(2):
            cells_ref[pl.ds(source, G), i * width : (i + 1) * width] = blocks[k][
                i * G : (i + 1) * G, :
            ]
    values = cells_ref[...].astype(jnp.float32)
    center = values - jnp.mean(values, axis=0, keepdims=True)
    spread = jnp.mean(center * center, axis=0, keepdims=True)
    normed = (center * lax.rsqrt(spread + EPS)).astype(jnp.bfloat16)
    lifted = jnp.dot(up_ref[...], normed, preferred_element_type=jnp.float32)
    scale = math.sqrt(2.0 / math.pi)
    inner = lifted * (scale + (scale * 0.044715) * (lifted * lifted))
    half = 0.5 * lifted
    active = (half + half * jnp.tanh(inner)).astype(jnp.bfloat16)
    lowered = jnp.dot(down_ref[...], active, preferred_element_type=jnp.float32)
    result = (values + lowered).astype(jnp.bfloat16)
    found = []
    for i in range(2):
        modes = lax.dot_general(
            table_ref[place],
            result[:, i * width : (i + 1) * width],
            (((1,), (1,)), ((), ())),
            preferred_element_type=jnp.float32,
        )
        found.append(modes.reshape(modes.shape[0] // SLOT, SLOT, modes.shape[1]))
    block = jnp.concatenate(found, axis=1).astype(jnp.bfloat16)
    if last:
        out_ref[:, 0 : 2 * SLOT, :] = earlier_ref[...]
        out_ref[:, 2 * SLOT : 4 * SLOT, :] = block
    else:
        out_ref[...] = block


def mlp_rows(place, blocks, up, down, tables, earlier, dests):
    pair_chans, width = blocks[0].shape
    chan = len(blocks) * pair_chans // 2
    last = earlier is not None
    arrays = [*blocks, up, down, tables] + ([earlier] if last else [])
    rows = (4 if last else 2) * SLOT
    return pl.pallas_call(
        functools.partial(mlp_kernel, len(blocks), last),
        out_shape=jax.ShapeDtypeStruct((dests, rows, chan), jnp.bfloat16),
        in_specs=[SMEM] + [VMEM] * len(arrays),
        out_specs=VMEM,
        scratch_shapes=[pltpu.VMEM((chan, 2 * width), jnp.bfloat16)],
        compiler_params=params(20 if dests <= FEW else 40),
        cost_estimate=takes(2),
        name="mlp_rows",
    )(place, *arrays)


def expand_kernel(start_ref, legendre_ref, spread_ref, out_ref):
    _, lats, degrees = legendre_ref.shape
    m = pl.program_id(0)
    degree = lax.broadcasted_iota(jnp.int32, (lats, degrees), 1)
    kept = jnp.where(degree >= start_ref[0] + m, legendre_ref[0].astype(jnp.float32), 0.0)
    wide = lax.dot_general(
        kept.astype(jnp.bfloat16),
        spread_ref[...],
        (((0,), (0,)), ((), ())),
        preferred_element_type=jnp.float32,
    )
    slot = lax.rem(lax.broadcasted_iota(jnp.int32, wide.shape, 1), SLOT)
    for r in range(2):
        out_ref[0, r] = jnp.where(slot == 2 * m + r, wide, 0.0).astype(jnp.bfloat16)


def expand(start, legendre, spread):
    modes, lats, degrees = legendre.shape
    depth = spread.shape[1]
    return pl.pallas_call(
        expand_kernel,
        out_shape=jax.ShapeDtypeStruct((modes, 2, degrees, depth), jnp.bfloat16),
        grid=(modes,),
        in_specs=[
            SMEM,
            pl.BlockSpec((1, lats, degrees), lambda m: (m, 0, 0)),
            pl.BlockSpec((lats, depth), lambda m: (0, 0)),
        ],
        out_specs=pl.BlockSpec((1, 2, degrees, depth), lambda m: (m, 0, 0, 0)),
        compiler_params=params(10 if depth <= 512 else 48),
        cost_estimate=takes(2),
        name="expand",
    )(start, legendre, spread)


def final_kernel(left_ref, spectrum_ref, out_ref, result_ref, sems):
    modes = left_ref.shape[0]
    chan = spectrum_ref.shape[1]
    copies = []
    for m in range(modes):
        for r in range(2):
            result_ref[m, :, r * chan : (r + 1) * chan] = jnp.dot(
                left_ref[m, r], spectrum_ref[...], preferred_element_type=jnp.float32
            ).astype(jnp.bfloat16)
        copies.append(pltpu.make_async_copy(result_ref.at[m], out_ref.at[m], sems.at[m]))
        copies[-1].start()
    for copy in copies:
        copy.wait()


def final_sum(left, spectrum):
    modes, _, degrees, depth = left.shape
    shape = (modes, degrees, 2 * spectrum.shape[1])
    return pl.pallas_call(
        final_kernel,
        out_shape=jax.ShapeDtypeStruct(shape, jnp.bfloat16),
        in_specs=[VMEM, VMEM],
        out_specs=HBM,
        scratch_shapes=[pltpu.VMEM(shape, jnp.bfloat16), pltpu.SemaphoreType.DMA((modes,))],
        compiler_params=params(8 if depth <= 512 else 48),
        cost_estimate=takes(1),
        name="final_sum",
    )(left, spectrum)


def fourier_blocks(lon, chunks, width, dests, mode_dev):
    chunk = lon // chunks
    index = np.arange(lon, dtype=np.int64)
    mode = np.arange(dests * mode_dev, dtype=np.int64)
    angle = ((mode[:, None] * index[None, :]) % lon) * (2.0 * math.pi / lon)
    paired = np.stack([np.cos(angle), -np.sin(angle)], axis=1) * math.sqrt(2.0 / lon)
    paired = paired.reshape(dests, 2 * mode_dev, chunks, chunk)
    table = np.zeros((chunks, dests, SLOT, width), np.float32)
    table[:, :, : 2 * mode_dev, :chunk] = np.transpose(paired, (2, 0, 1, 3))
    return table.reshape(chunks, dests * SLOT, width).astype(jnp.bfloat16)


def turn(block, axis, count, step):
    return lax.ppermute(block, axis, [(i, (i + step) % count) for i in range(count)])


def scalar(value):
    return jnp.asarray(value, jnp.int32).reshape(1)


def on_device(
    fields,
    disco_weight,
    support_lat,
    support_lon,
    support_basis,
    support_value,
    w_up,
    w_down,
    legendre,
):
    lat_dev, lon, _ = fields.shape
    num_lat = lax.axis_size("lat")
    num_chan = lax.axis_size("chan")
    mode_dev, _, lats = legendre.shape
    dests = num_lat * num_chan
    width = ceil_to(lon // num_chan + 2 * DLON, LANES)
    band = lax.axis_index("lat")
    place = scalar(lax.axis_index("chan"))
    index = lax.axis_index(("lat", "chan"))
    supports = (support_lat, support_lon, support_basis, support_value)

    two_bands = num_lat == 2
    cells = jnp.swapaxes(fields, 1, 2)
    if two_bands:
        edge_out = lax.dynamic_slice_in_dim(cells, HALO * (1 - band), HALO, axis=0)
        edges = [None, lax.ppermute(edge_out, "lat", [(0, 1), (1, 0)])]
        pairs = [band, 1 - band]
    else:
        ends = num_lat - 1
        edges = [
            lax.ppermute(cells[lat_dev - HALO :], "lat", [(i, i + 1) for i in range(ends)]),
            lax.ppermute(cells[:HALO], "lat", [(i + 1, i) for i in range(ends)]),
        ]
        pairs = [0, 1]

    tables = jnp.asarray(fourier_blocks(lon, num_chan, width, dests, mode_dev))
    up = w_up.T
    down = w_down.T

    depth = dests * 4 * SLOT
    row = np.arange(depth)
    source_band = row // (4 * SLOT) // num_chan
    phase = (row // (2 * SLOT)) % 2
    source_pair = (phase ^ source_band) if two_bands else phase
    lat_of = lat_dev * source_band + 2 * source_pair + (row // SLOT) % 2
    spread = (lat_of[None, :] == np.arange(lats)[:, None]).astype(jnp.bfloat16)
    left = expand(scalar(index * mode_dev), jnp.swapaxes(legendre, 1, 2), jnp.asarray(spread))

    received = []
    for edge, pair in zip(edges, pairs):
        mixed = conv_rows(scalar(pair), place, supports, cells, edge, disco_weight, num_chan)
        received.append(
            [mixed[0]] + [turn(mixed[k], "chan", num_chan, k) for k in range(1, num_chan)]
        )
    spectrum = None
    for blocks in received:
        spectrum = mlp_rows(place, blocks, up, down, tables, spectrum, dests)

    both = ("lat", "chan")
    gathered = lax.all_to_all(spectrum, both, split_axis=0, concat_axis=0, tiled=True)
    return final_sum(left, gathered.reshape(depth, gathered.shape[2]))


def solution(mesh):
    in_specs = (
        P(("tm", "lat"), None, "chan"),
        P(None, "chan", None),
        P("lat", None),
        P("lat", None),
        P("lat", None),
        P("lat", None),
        P(),
        P(),
        P(("lat", "chan"), None, None),
    )
    out_specs = P(("tm", "lat", "chan"), None, None)
    return jax.shard_map(
        on_device, mesh=mesh, in_specs=in_specs, out_specs=out_specs, check_vma=False
    )
```

```python
import functools
import math

import jax
import jax.numpy as jnp
import numpy as np
from jax import lax
from jax.experimental import pallas as pl
from jax.experimental.pallas import tpu as pltpu
from jax.sharding import PartitionSpec as P

G = 64
S = 9
HALO = 2
DLON = 4
TAPS = S + 1
LANES = 128
SLOT = 8
EPS = 1e-05
FEW = 8
MIB = 1024 * 1024
FLOPS_PER_US = 100_000_000

SMEM = pl.BlockSpec(memory_space=pltpu.SMEM)
VMEM = pl.BlockSpec(memory_space=pltpu.VMEM)
ANY = pl.BlockSpec(memory_space=pl.ANY)
HBM = pl.BlockSpec(memory_space=pltpu.HBM)


def ceil_to(value, step):
    return -(-value // step) * step


def params(mib):
    return pltpu.CompilerParams(vmem_limit_bytes=mib * MIB)


def takes(micros):
    return pl.CostEstimate(flops=int(micros * FLOPS_PER_US), bytes_accessed=0, transcendentals=0)


def conv_kernel(
    step,
    edges,
    emit,
    after,
    pair_ref,
    place_ref,
    lat_ref,
    lon_ref,
    basis_ref,
    value_ref,
    fields_ref,
    weight_ref,
    *rest,
):
    edge_refs, rest = rest[:edges], rest[edges + after :]
    *out_refs, rows_ref, taps_ref, filt_ref = rest
    own, _, lon = fields_ref.shape
    pair = pair_ref[0]
    if emit:
        *out_refs, near_ref, far_ref = out_refs
        near_ref[...] = fields_ref[(own - 1) * (1 - pair)]
        far_ref[...] = fields_ref[(own - 2) * (1 - pair) + pair]
    chunks = len(out_refs)
    chunk = lon // chunks
    width = out_refs[0].shape[1]
    total = rows_ref.shape[2]
    own_at = HALO * (1 - pair)
    edge_at = [own * pair + 1 - pair, (own + 1) * pair]
    if edges == 0:
        i = step
    elif step == 0:
        i = 1 - pair
    else:
        i = pair
    row = 2 * pair + i

    def put(slot, cells):
        rows_ref[slot, :, LANES : LANES + lon] = cells
        rows_ref[slot, :, 0:LANES] = cells[:, lon - LANES :]
        full = (lon // LANES) * LANES
        tail = total - LANES - lon
        rows_ref[slot, :, LANES + full :] = jnp.concatenate(
            [cells[:, full:], cells[:, :tail]], axis=1
        )

    for k in range(own):
        put(own_at + k, fields_ref[k])
    for k in range(HALO):
        if k < edges:
            put(edge_at[k], edge_refs[k][...])
        else:
            rows_ref[edge_at[k]] = jnp.zeros(rows_ref.shape[1:], rows_ref.dtype)

    lane = lax.broadcasted_iota(jnp.int32, (G, LANES), 1)
    begins = [LANES + chunk * lax.rem(place_ref[0] + k, chunks) for k in range(chunks)]

    def fill(tap, source, offset):
        for k in range(chunks):
            begin = begins[k] + offset
            first = lax.div(begin, LANES)
            shift = lax.rem(begin, LANES)
            back = lax.rem(LANES - shift, LANES)
            keep = lane < LANES - shift
            turned = []
            for t in range(width // LANES + 1):
                start = pl.multiple_of((first + t) * LANES, LANES)
                tile = rows_ref[source, :, pl.ds(start, LANES)]
                turned.append(pltpu.roll(tile, back, 1))
            for t in range(width // LANES):
                at = k * width + t * LANES
                taps_ref[tap * G : (tap + 1) * G, at : at + LANES] = jnp.where(
                    keep, turned[t], turned[t + 1]
                )

    eye = jnp.where(
        lax.broadcasted_iota(jnp.int32, (G, G), 0) == lax.broadcasted_iota(jnp.int32, (G, G), 1),
        1.0,
        0.0,
    ).astype(jnp.bfloat16)
    pieces = []
    for tap in range(S):
        picked = weight_ref[basis_ref[row, tap]].astype(jnp.float32) * value_ref[row, tap]
        pieces.append(picked.astype(jnp.bfloat16))
    pieces.append(eye)
    for k in range(TAPS // 2):
        filt_ref[:, k * 2 * G : (k + 1) * 2 * G] = jnp.concatenate(
            [pieces[2 * k], pieces[2 * k + 1]], axis=1
        )
    for tap in range(S):
        fill(tap, HALO + i + lat_ref[row, tap], lon_ref[row, tap])
    fill(S, HALO + i, 0)
    mixed = jnp.dot(filt_ref[...], taps_ref[...], preferred_element_type=jnp.float32).astype(
        jnp.bfloat16
    )
    for k in range(chunks):
        out_refs[k][...] = mixed[:, k * width : (k + 1) * width]


def conv_row(step, emit, pair, place, supports, fields, weight, edges, after, chunks):
    own, chans, lon = fields.shape
    width = ceil_to(lon // chunks, LANES)
    highest = (LANES + lon - lon // chunks + DLON) // LANES
    total = (highest + 1) * LANES + width
    outs = [jax.ShapeDtypeStruct((chans, width), jnp.bfloat16)] * chunks
    if emit:
        outs += [jax.ShapeDtypeStruct((chans, lon), jnp.bfloat16)] * HALO
    return pl.pallas_call(
        functools.partial(conv_kernel, step, len(edges), emit, len(after)),
        out_shape=outs,
        in_specs=[SMEM] * 6 + [VMEM] * (2 + len(edges)) + [ANY] * len(after),
        out_specs=[VMEM] * len(outs),
        scratch_shapes=[
            pltpu.VMEM((own + HALO, chans, total), jnp.bfloat16),
            pltpu.VMEM((TAPS * G, chunks * width), jnp.bfloat16),
            pltpu.VMEM((G, TAPS * G), jnp.bfloat16),
        ],
        compiler_params=params(56 if emit else 16),
        cost_estimate=takes(2),
        name="conv_row",
    )(pair, place, *supports, fields, weight, *edges, *after)


def mlp_kernel(parts, rows, joins, wide, place_ref, *rest):
    blocks, rest = rest[: parts * rows], rest[parts * rows :]
    up_ref, down_ref, table_ref, *rest = rest
    earlier, (out_ref, cells_ref) = rest[:joins], rest[-2:]
    width = blocks[0].shape[1]
    place = place_ref[0]
    for k in range(parts):
        source = pl.multiple_of(lax.rem(place - k + parts, parts) * G, G)
        for i in range(rows):
            cells_ref[pl.ds(source, G), i * width : (i + 1) * width] = blocks[i * parts + k][...]
    values = cells_ref[...].astype(jnp.float32)
    center = values - jnp.mean(values, axis=0, keepdims=True)
    spread = jnp.mean(center * center, axis=0, keepdims=True)
    normed = (center * lax.rsqrt(spread + EPS)).astype(jnp.bfloat16)
    lifted = jnp.dot(up_ref[...], normed, preferred_element_type=jnp.float32)
    scale = math.sqrt(2.0 / math.pi)
    inner = lifted * (scale + (scale * 0.044715) * (lifted * lifted))
    half = 0.5 * lifted
    active = (half + half * jnp.tanh(inner)).astype(jnp.bfloat16)
    lowered = jnp.dot(down_ref[...], active, preferred_element_type=jnp.float32)
    result = (values + lowered).astype(jnp.bfloat16)
    found = []
    for i in range(rows):
        modes = lax.dot_general(
            table_ref[place],
            result[:, i * width : (i + 1) * width],
            (((1,), (1,)), ((), ())),
            preferred_element_type=jnp.float32,
        )
        found.append(modes.reshape(modes.shape[0] // SLOT, SLOT, modes.shape[1]))
    if wide:
        out_ref[...] = found[0]
    elif joins:
        first_ref, second_ref = earlier
        out_ref[:, 0 : 2 * SLOT, :] = first_ref[...]
        out_ref[:, 2 * SLOT : 4 * SLOT, :] = jnp.concatenate(
            [second_ref[...], *found], axis=1
        ).astype(jnp.bfloat16)
    else:
        out_ref[...] = jnp.concatenate(found, axis=1).astype(jnp.bfloat16)


def mlp_rows(place, rows, up, down, tables, earlier, wide, after=()):
    parts = len(rows[0])
    chans, width = rows[0][0].shape
    chan = parts * chans
    dests = tables.shape[1] // SLOT
    arrays = [*(block for row in rows for block in row), up, down, tables, *earlier]
    slots = 4 if earlier else len(rows)
    kind = jnp.float32 if wide else jnp.bfloat16
    return pl.pallas_call(
        functools.partial(mlp_kernel, parts, len(rows), len(earlier), wide),
        out_shape=jax.ShapeDtypeStruct((dests, slots * SLOT, chan), kind),
        in_specs=[SMEM] + [VMEM] * len(arrays) + [ANY] * len(after),
        out_specs=VMEM,
        scratch_shapes=[pltpu.VMEM((chan, len(rows) * width), jnp.bfloat16)],
        compiler_params=params(20 if dests <= FEW else 40),
        cost_estimate=takes(1),
        name="mlp_rows",
    )(place, *arrays, *after)


def expand_kernel(start_ref, legendre_ref, spread_ref, out_ref):
    _, lats, degrees = legendre_ref.shape
    m = pl.program_id(0)
    degree = lax.broadcasted_iota(jnp.int32, (lats, degrees), 1)
    kept = jnp.where(degree >= start_ref[0] + m, legendre_ref[0].astype(jnp.float32), 0.0)
    wide = lax.dot_general(
        kept.astype(jnp.bfloat16),
        spread_ref[...],
        (((0,), (0,)), ((), ())),
        preferred_element_type=jnp.float32,
    )
    slot = lax.rem(lax.broadcasted_iota(jnp.int32, wide.shape, 1), SLOT)
    for r in range(2):
        out_ref[0, r] = jnp.where(slot == 2 * m + r, wide, 0.0).astype(jnp.bfloat16)


def expand(start, legendre, spread):
    modes, lats, degrees = legendre.shape
    depth = spread.shape[1]
    return pl.pallas_call(
        expand_kernel,
        out_shape=jax.ShapeDtypeStruct((modes, 2, degrees, depth), jnp.bfloat16),
        grid=(modes,),
        in_specs=[
            SMEM,
            pl.BlockSpec((1, lats, degrees), lambda m: (m, 0, 0)),
            pl.BlockSpec((lats, depth), lambda m: (0, 0)),
        ],
        out_specs=pl.BlockSpec((1, 2, degrees, depth), lambda m: (m, 0, 0, 0)),
        compiler_params=params(10 if depth <= 512 else 48),
        cost_estimate=takes(2),
        name="expand",
    )(start, legendre, spread)


def final_kernel(left_ref, spectrum_ref, out_ref, result_ref, sems):
    modes = left_ref.shape[0]
    chan = spectrum_ref.shape[1]
    copies = []
    for m in range(modes):
        for r in range(2):
            result_ref[m, :, r * chan : (r + 1) * chan] = jnp.dot(
                left_ref[m, r], spectrum_ref[...], preferred_element_type=jnp.float32
            ).astype(jnp.bfloat16)
        copies.append(pltpu.make_async_copy(result_ref.at[m], out_ref.at[m], sems.at[m]))
        copies[-1].start()
    for copy in copies:
        copy.wait()


def final_sum(left, spectrum):
    modes, _, degrees, depth = left.shape
    shape = (modes, degrees, 2 * spectrum.shape[1])
    return pl.pallas_call(
        final_kernel,
        out_shape=jax.ShapeDtypeStruct(shape, jnp.bfloat16),
        in_specs=[VMEM, VMEM],
        out_specs=HBM,
        scratch_shapes=[pltpu.VMEM(shape, jnp.bfloat16), pltpu.SemaphoreType.DMA((modes,))],
        compiler_params=params(8 if depth <= 512 else 48),
        cost_estimate=takes(1),
        name="final_sum",
    )(left, spectrum)


def fourier_blocks(lon, chunks, width, dests, mode_dev):
    chunk = lon // chunks
    index = np.arange(lon, dtype=np.int64)
    mode = np.arange(dests * mode_dev, dtype=np.int64)
    angle = ((mode[:, None] * index[None, :]) % lon) * (2.0 * math.pi / lon)
    paired = np.stack([np.cos(angle), -np.sin(angle)], axis=1) * math.sqrt(2.0 / lon)
    paired = paired.reshape(dests, 2 * mode_dev, chunks, chunk)
    table = np.zeros((chunks, dests, SLOT, width), np.float32)
    table[:, :, : 2 * mode_dev, :chunk] = np.transpose(paired, (2, 0, 1, 3))
    return table.reshape(chunks, dests * SLOT, width).astype(jnp.bfloat16)


def turn(block, axis, count, step):
    return lax.ppermute(block, axis, [(i, (i + step) % count) for i in range(count)])


def scalar(value):
    return jnp.asarray(value, jnp.int32).reshape(1)


def on_device(
    fields,
    disco_weight,
    support_lat,
    support_lon,
    support_basis,
    support_value,
    w_up,
    w_down,
    legendre,
):
    lat_dev, lon, _ = fields.shape
    num_lat = lax.axis_size("lat")
    num_chan = lax.axis_size("chan")
    mode_dev, _, lats = legendre.shape
    dests = num_lat * num_chan
    width = ceil_to(lon // num_chan, LANES)
    band = lax.axis_index("lat")
    place = scalar(lax.axis_index("chan"))
    index = lax.axis_index(("lat", "chan"))
    supports = (support_lat, support_lon, support_basis, support_value)

    two_bands = num_lat == 2
    cells = jnp.swapaxes(fields, 1, 2)
    two_bands = num_lat == 2

    tables = jnp.asarray(fourier_blocks(lon, num_chan, width, dests, mode_dev))
    up = w_up.T
    down = w_down.T

    depth = dests * 4 * SLOT
    row = np.arange(depth)
    source_band = row // (4 * SLOT) // num_chan
    step = (row // SLOT) % 2
    phase = (row // (2 * SLOT)) % 2
    source_pair = (phase ^ source_band) if two_bands else phase
    edged = (phase == 1) if two_bands else np.ones_like(phase, bool)
    source_row = np.where(edged, np.where(step == 0, 1 - source_pair, source_pair), step)
    lat_of = lat_dev * source_band + 2 * source_pair + source_row
    spread = (lat_of[None, :] == np.arange(lats)[:, None]).astype(jnp.bfloat16)
    left = expand(scalar(index * mode_dev), jnp.swapaxes(legendre, 1, 2), jnp.asarray(spread))

    def send(step, pair, edges, emit=False, after=()):
        outs = conv_row(
            step, emit, scalar(pair), place, supports, cells, disco_weight, edges, after, num_chan
        )
        outs = list(outs)
        row = outs[:1] + [turn(outs[k], "chan", num_chan, k) for k in range(1, num_chan)]
        return (row, *outs[num_chan:])

    if two_bands:
        row_a, near, far = send(0, band, [], emit=True)
        edges = [lax.ppermute(edge, "lat", [(0, 1), (1, 0)]) for edge in (near, far)]
        (row_b,) = send(1, band, [], after=[near])
        last = 1 - band
    else:
        ends = num_lat - 1
        up_edges = [
            lax.ppermute(cells[lat_dev - 1 - k], "lat", [(i, i + 1) for i in range(ends)])
            for k in range(HALO)
        ]
        edges = [
            lax.ppermute(cells[k], "lat", [(i + 1, i) for i in range(ends)]) for k in range(HALO)
        ]
        (row_a,) = send(0, 0, up_edges[:1])
        (row_b,) = send(1, 0, up_edges)
        last = 1
    (row_c,) = send(0, last, edges[:1], after=row_a[1:])
    (row_d,) = send(1, last, edges)
    first = mlp_rows(
        place, [row_a, row_b], up, down, tables, [], False, after=[row_c[0], edges[1]]
    )
    second = mlp_rows(place, [row_c], up, down, tables, [], True)
    spectrum = mlp_rows(place, [row_d], up, down, tables, [first, second], False)

    both = ("lat", "chan")
    gathered = lax.all_to_all(spectrum, both, split_axis=0, concat_axis=0, tiled=True)
    return final_sum(left, gathered.reshape(depth, gathered.shape[2]))


def solution(mesh):
    in_specs = (
        P(("tm", "lat"), None, "chan"),
        P(None, "chan", None),
        P("lat", None),
        P("lat", None),
        P("lat", None),
        P("lat", None),
        P(),
        P(),
        P(("lat", "chan"), None, None),
    )
    out_specs = P(("tm", "lat", "chan"), None, None)
    return jax.shard_map(
        on_device, mesh=mesh, in_specs=in_specs, out_specs=out_specs, check_vma=False
    )
```

```python
import functools
import math

import jax
import jax.numpy as jnp
import numpy as np
from jax import lax
from jax.experimental import pallas as pl
from jax.experimental.pallas import tpu as pltpu
from jax.sharding import PartitionSpec as P

G = 64
S = 9
HALO = 2
DLON = 4
TAPS = S + 1
LANES = 128
SLOT = 8
EPS = 1e-05
FEW = 8
MIB = 1024 * 1024
FLOPS_PER_US = 1_000_000_000

SMEM = pl.BlockSpec(memory_space=pltpu.SMEM)
VMEM = pl.BlockSpec(memory_space=pltpu.VMEM)
ANY = pl.BlockSpec(memory_space=pl.ANY)
HBM = pl.BlockSpec(memory_space=pltpu.HBM)


def ceil_to(value, step):
    return -(-value // step) * step


def params(mib):
    return pltpu.CompilerParams(vmem_limit_bytes=mib * MIB)


def takes(micros):
    return pl.CostEstimate(flops=int(micros * FLOPS_PER_US), bytes_accessed=0, transcendentals=0)


def conv_kernel(
    steps,
    edges,
    emit,
    after,
    pair_ref,
    place_ref,
    lat_ref,
    lon_ref,
    basis_ref,
    value_ref,
    fields_ref,
    weight_ref,
    *rest,
):
    edge_refs, rest = rest[:edges], rest[edges + after :]
    *out_refs, rows_ref, taps_ref, filt_ref = rest
    own, _, lon = fields_ref.shape
    pair = pair_ref[0]
    if emit:
        *out_refs, near_ref, far_ref = out_refs
        near_ref[...] = fields_ref[(own - 1) * (1 - pair)]
        far_ref[...] = fields_ref[(own - 2) * (1 - pair) + pair]
    chunks = len(out_refs)
    chunk = lon // chunks
    width = out_refs[0].shape[1]
    total = rows_ref.shape[2]
    own_at = HALO * (1 - pair)
    edge_at = [own * pair + 1 - pair, (own + 1) * pair]
    def put(slot, cells):
        rows_ref[slot, :, LANES : LANES + lon] = cells
        rows_ref[slot, :, 0:LANES] = cells[:, lon - LANES :]
        full = (lon // LANES) * LANES
        tail = total - LANES - lon
        rows_ref[slot, :, LANES + full :] = jnp.concatenate(
            [cells[:, full:], cells[:, :tail]], axis=1
        )

    for k in range(own):
        put(own_at + k, fields_ref[k])
    for k in range(HALO):
        if k < edges:
            put(edge_at[k], edge_refs[k][...])
        else:
            rows_ref[edge_at[k]] = jnp.zeros(rows_ref.shape[1:], rows_ref.dtype)

    lane = lax.broadcasted_iota(jnp.int32, (G, LANES), 1)
    begins = [LANES + chunk * lax.rem(place_ref[0] + k, chunks) for k in range(chunks)]

    def fill(slot, tap, source, offset):
        for k in range(chunks):
            begin = begins[k] + offset
            first = lax.div(begin, LANES)
            shift = lax.rem(begin, LANES)
            back = lax.rem(LANES - shift, LANES)
            keep = lane < LANES - shift
            turned = []
            for t in range(width // LANES + 1):
                start = pl.multiple_of((first + t) * LANES, LANES)
                tile = rows_ref[source, :, pl.ds(start, LANES)]
                turned.append(pltpu.roll(tile, back, 1))
            for t in range(width // LANES):
                at = k * width + t * LANES
                taps_ref[slot, tap * G : (tap + 1) * G, at : at + LANES] = jnp.where(
                    keep, turned[t], turned[t + 1]
                )

    eye = jnp.where(
        lax.broadcasted_iota(jnp.int32, (G, G), 0) == lax.broadcasted_iota(jnp.int32, (G, G), 1),
        1.0,
        0.0,
    ).astype(jnp.bfloat16)
    for n, step in enumerate(steps):
        i = step
        if edges:
            i = pair if step else 1 - pair
        row = 2 * pair + i
        pieces = []
        for tap in range(S):
            picked = weight_ref[basis_ref[row, tap]].astype(jnp.float32) * value_ref[row, tap]
            pieces.append(picked.astype(jnp.bfloat16))
        pieces.append(eye)
        for k in range(TAPS // 2):
            filt_ref[n, :, k * 2 * G : (k + 1) * 2 * G] = jnp.concatenate(
                [pieces[2 * k], pieces[2 * k + 1]], axis=1
            )
        for tap in range(S):
            fill(n, tap, HALO + i + lat_ref[row, tap], lon_ref[row, tap])
        fill(n, S, HALO + i, 0)
        mixed = jnp.dot(filt_ref[n], taps_ref[n], preferred_element_type=jnp.float32).astype(
            jnp.bfloat16
        )
        for k in range(chunks):
            out_refs[k][n * G : (n + 1) * G, :] = mixed[:, k * width : (k + 1) * width]


def conv_rows(steps, emit, pair, place, supports, fields, weight, edges, after, chunks):
    own, chans, lon = fields.shape
    width = ceil_to(lon // chunks, LANES)
    highest = (LANES + lon - lon // chunks + DLON) // LANES
    total = (highest + 1) * LANES + width
    count = len(steps)
    outs = [jax.ShapeDtypeStruct((count * chans, width), jnp.bfloat16)] * chunks
    if emit:
        outs += [jax.ShapeDtypeStruct((chans, lon), jnp.bfloat16)] * HALO
    return pl.pallas_call(
        functools.partial(conv_kernel, steps, len(edges), emit, len(after)),
        out_shape=outs,
        in_specs=[SMEM] * 6 + [VMEM] * (2 + len(edges)) + [ANY] * len(after),
        out_specs=[VMEM] * len(outs),
        scratch_shapes=[
            pltpu.VMEM((own + HALO, chans, total), jnp.bfloat16),
            pltpu.VMEM((count, TAPS * G, chunks * width), jnp.bfloat16),
            pltpu.VMEM((count, G, TAPS * G), jnp.bfloat16),
        ],
        compiler_params=params(56 if emit else 16),
        cost_estimate=takes(2),
        name="conv_rows",
    )(pair, place, *supports, fields, weight, *edges, *after)


def mlp_kernel(parts, rows, joins, wide, place_ref, *rest):
    blocks, rest = rest[:parts], rest[parts:]
    up_ref, down_ref, table_ref, *rest = rest
    earlier, (out_ref, cells_ref) = rest[:joins], rest[-2:]
    width = blocks[0].shape[1]
    place = place_ref[0]
    for k in range(parts):
        source = pl.multiple_of(lax.rem(place - k + parts, parts) * G, G)
        for i in range(rows):
            cells_ref[pl.ds(source, G), i * width : (i + 1) * width] = blocks[k][
                i * G : (i + 1) * G, :
            ]
    values = cells_ref[...].astype(jnp.float32)
    center = values - jnp.mean(values, axis=0, keepdims=True)
    spread = jnp.mean(center * center, axis=0, keepdims=True)
    normed = (center * lax.rsqrt(spread + EPS)).astype(jnp.bfloat16)
    lifted = jnp.dot(up_ref[...], normed, preferred_element_type=jnp.float32)
    scale = math.sqrt(2.0 / math.pi)
    inner = lifted * (scale + (scale * 0.044715) * (lifted * lifted))
    half = 0.5 * lifted
    active = (half + half * jnp.tanh(inner)).astype(jnp.bfloat16)
    lowered = jnp.dot(down_ref[...], active, preferred_element_type=jnp.float32)
    result = (values + lowered).astype(jnp.bfloat16)
    found = []
    for i in range(rows):
        modes = lax.dot_general(
            table_ref[place],
            result[:, i * width : (i + 1) * width],
            (((1,), (1,)), ((), ())),
            preferred_element_type=jnp.float32,
        )
        found.append(modes.reshape(modes.shape[0] // SLOT, SLOT, modes.shape[1]))
    if wide:
        out_ref[...] = found[0]
    elif joins:
        first_ref, second_ref = earlier
        out_ref[:, 0 : 2 * SLOT, :] = first_ref[...]
        out_ref[:, 2 * SLOT : 4 * SLOT, :] = jnp.concatenate(
            [second_ref[...], *found], axis=1
        ).astype(jnp.bfloat16)
    else:
        out_ref[...] = jnp.concatenate(found, axis=1).astype(jnp.bfloat16)


def mlp_rows(place, blocks, up, down, tables, earlier, wide, after=()):
    parts = len(blocks)
    chans, width = blocks[0].shape
    rows = chans // G
    chan = parts * G
    dests = tables.shape[1] // SLOT
    arrays = [*blocks, up, down, tables, *earlier]
    slots = 4 if earlier else rows
    kind = jnp.float32 if wide else jnp.bfloat16
    return pl.pallas_call(
        functools.partial(mlp_kernel, parts, rows, len(earlier), wide),
        out_shape=jax.ShapeDtypeStruct((dests, slots * SLOT, chan), kind),
        in_specs=[SMEM] + [VMEM] * len(arrays) + [ANY] * len(after),
        out_specs=VMEM,
        scratch_shapes=[pltpu.VMEM((chan, rows * width), jnp.bfloat16)],
        compiler_params=params(20 if dests <= FEW else 40),
        cost_estimate=takes(1),
        name="mlp_rows",
    )(place, *arrays, *after)


def expand_kernel(start_ref, legendre_ref, spread_ref, out_ref):
    _, lats, degrees = legendre_ref.shape
    m = pl.program_id(0)
    degree = lax.broadcasted_iota(jnp.int32, (lats, degrees), 1)
    kept = jnp.where(degree >= start_ref[0] + m, legendre_ref[0].astype(jnp.float32), 0.0)
    wide = lax.dot_general(
        kept.astype(jnp.bfloat16),
        spread_ref[...],
        (((0,), (0,)), ((), ())),
        preferred_element_type=jnp.float32,
    )
    slot = lax.rem(lax.broadcasted_iota(jnp.int32, wide.shape, 1), SLOT)
    for r in range(2):
        out_ref[0, r] = jnp.where(slot == 2 * m + r, wide, 0.0).astype(jnp.bfloat16)


def expand(start, legendre, spread):
    modes, lats, degrees = legendre.shape
    depth = spread.shape[1]
    return pl.pallas_call(
        expand_kernel,
        out_shape=jax.ShapeDtypeStruct((modes, 2, degrees, depth), jnp.bfloat16),
        grid=(modes,),
        in_specs=[
            SMEM,
            pl.BlockSpec((1, lats, degrees), lambda m: (m, 0, 0)),
            pl.BlockSpec((lats, depth), lambda m: (0, 0)),
        ],
        out_specs=pl.BlockSpec((1, 2, degrees, depth), lambda m: (m, 0, 0, 0)),
        compiler_params=params(10 if depth <= 512 else 48),
        cost_estimate=takes(2),
        name="expand",
    )(start, legendre, spread)


def final_kernel(left_ref, spectrum_ref, out_ref, result_ref, sems):
    modes = left_ref.shape[0]
    chan = spectrum_ref.shape[1]
    copies = []
    for m in range(modes):
        for r in range(2):
            result_ref[m, :, r * chan : (r + 1) * chan] = jnp.dot(
                left_ref[m, r], spectrum_ref[...], preferred_element_type=jnp.float32
            ).astype(jnp.bfloat16)
        copies.append(pltpu.make_async_copy(result_ref.at[m], out_ref.at[m], sems.at[m]))
        copies[-1].start()
    for copy in copies:
        copy.wait()


def final_sum(left, spectrum):
    modes, _, degrees, depth = left.shape
    shape = (modes, degrees, 2 * spectrum.shape[1])
    return pl.pallas_call(
        final_kernel,
        out_shape=jax.ShapeDtypeStruct(shape, jnp.bfloat16),
        in_specs=[VMEM, VMEM],
        out_specs=HBM,
        scratch_shapes=[pltpu.VMEM(shape, jnp.bfloat16), pltpu.SemaphoreType.DMA((modes,))],
        compiler_params=params(8 if depth <= 512 else 48),
        cost_estimate=takes(1),
        name="final_sum",
    )(left, spectrum)


def fourier_blocks(lon, chunks, width, dests, mode_dev):
    chunk = lon // chunks
    index = np.arange(lon, dtype=np.int64)
    mode = np.arange(dests * mode_dev, dtype=np.int64)
    angle = ((mode[:, None] * index[None, :]) % lon) * (2.0 * math.pi / lon)
    paired = np.stack([np.cos(angle), -np.sin(angle)], axis=1) * math.sqrt(2.0 / lon)
    paired = paired.reshape(dests, 2 * mode_dev, chunks, chunk)
    table = np.zeros((chunks, dests, SLOT, width), np.float32)
    table[:, :, : 2 * mode_dev, :chunk] = np.transpose(paired, (2, 0, 1, 3))
    return table.reshape(chunks, dests * SLOT, width).astype(jnp.bfloat16)


def turn(block, axis, count, step):
    return lax.ppermute(block, axis, [(i, (i + step) % count) for i in range(count)])


def scalar(value):
    return jnp.asarray(value, jnp.int32).reshape(1)


def on_device(
    fields,
    disco_weight,
    support_lat,
    support_lon,
    support_basis,
    support_value,
    w_up,
    w_down,
    legendre,
):
    lat_dev, lon, _ = fields.shape
    num_lat = lax.axis_size("lat")
    num_chan = lax.axis_size("chan")
    mode_dev, _, lats = legendre.shape
    dests = num_lat * num_chan
    width = ceil_to(lon // num_chan, LANES)
    band = lax.axis_index("lat")
    place = scalar(lax.axis_index("chan"))
    index = lax.axis_index(("lat", "chan"))
    supports = (support_lat, support_lon, support_basis, support_value)

    two_bands = num_lat == 2
    cells = jnp.swapaxes(fields, 1, 2)
    two_bands = num_lat == 2

    tables = jnp.asarray(fourier_blocks(lon, num_chan, width, dests, mode_dev))
    up = w_up.T
    down = w_down.T

    depth = dests * 4 * SLOT
    row = np.arange(depth)
    source_band = row // (4 * SLOT) // num_chan
    step = (row // SLOT) % 2
    phase = (row // (2 * SLOT)) % 2
    source_pair = (phase ^ source_band) if two_bands else phase
    plain = (phase == 0) if two_bands else np.zeros_like(phase, bool)
    source_row = np.where(plain, step, np.where(step == 0, 1 - source_pair, source_pair))
    lat_of = lat_dev * source_band + 2 * source_pair + source_row
    spread = (lat_of[None, :] == np.arange(lats)[:, None]).astype(jnp.bfloat16)
    left = expand(scalar(index * mode_dev), jnp.swapaxes(legendre, 1, 2), jnp.asarray(spread))

    def send(steps, pair, edges, emit=False, after=()):
        outs = list(
            conv_rows(
                steps, emit, scalar(pair), place, supports, cells, disco_weight, edges, after, num_chan
            )
        )
        blocks = outs[:1] + [turn(outs[k], "chan", num_chan, k) for k in range(1, num_chan)]
        return (blocks, *outs[num_chan:])

    if two_bands:
        blocks, near, far = send((0, 1), band, [], emit=True)
        edges = [lax.ppermute(edge, "lat", [(0, 1), (1, 0)]) for edge in (near, far)]
        last = 1 - band
    else:
        ends = num_lat - 1
        up_edges = [
            lax.ppermute(cells[lat_dev - 1 - k], "lat", [(i, i + 1) for i in range(ends)])
            for k in range(HALO)
        ]
        edges = [
            lax.ppermute(cells[k], "lat", [(i + 1, i) for i in range(ends)]) for k in range(HALO)
        ]
        (blocks,) = send((0, 1), 0, up_edges)
        last = 1
    (row_c,) = send((0,), last, edges[:1])
    (row_d,) = send((1,), last, edges, after=blocks[1:])
    first = mlp_rows(place, blocks, up, down, tables, [], False, after=row_c[:1])
    second = mlp_rows(place, row_c, up, down, tables, [], True)
    spectrum = mlp_rows(place, row_d, up, down, tables, [first, second], False)

    both = ("lat", "chan")
    gathered = lax.all_to_all(spectrum, both, split_axis=0, concat_axis=0, tiled=True)
    return final_sum(left, gathered.reshape(depth, gathered.shape[2]))


def solution(mesh):
    in_specs = (
        P(("tm", "lat"), None, "chan"),
        P(None, "chan", None),
        P("lat", None),
        P("lat", None),
        P("lat", None),
        P("lat", None),
        P(),
        P(),
        P(("lat", "chan"), None, None),
    )
    out_specs = P(("tm", "lat", "chan"), None, None)
    return jax.shard_map(
        on_device, mesh=mesh, in_specs=in_specs, out_specs=out_specs, check_vma=False
    )
```

```python
import functools
import math

import jax
import jax.numpy as jnp
import numpy as np
from jax import lax
from jax.experimental import pallas as pl
from jax.experimental.pallas import tpu as pltpu
from jax.sharding import PartitionSpec as P

G = 64
S = 9
HALO = 2
DLON = 4
TAPS = S + 1
LANES = 128
SLOT = 8
EPS = 1e-05
FEW = 8
MIB = 1024 * 1024
FLOPS_PER_US = 1_000_000_000

SMEM = pl.BlockSpec(memory_space=pltpu.SMEM)
VMEM = pl.BlockSpec(memory_space=pltpu.VMEM)
ANY = pl.BlockSpec(memory_space=pl.ANY)
HBM = pl.BlockSpec(memory_space=pltpu.HBM)


def ceil_to(value, step):
    return -(-value // step) * step


def params(mib):
    return pltpu.CompilerParams(vmem_limit_bytes=mib * MIB)


def takes(micros):
    return pl.CostEstimate(flops=int(micros * FLOPS_PER_US), bytes_accessed=0, transcendentals=0)


def edge_kernel(start_ref, fields_ref, out_ref, sem):
    copy = pltpu.make_async_copy(fields_ref.at[pl.ds(start_ref[0], HALO)], out_ref, sem)
    copy.start()
    copy.wait()


def edge_rows(start, fields):
    return pl.pallas_call(
        edge_kernel,
        out_shape=jax.ShapeDtypeStruct((HALO, *fields.shape[1:]), fields.dtype),
        in_specs=[SMEM, ANY],
        out_specs=ANY,
        scratch_shapes=[pltpu.SemaphoreType.DMA],
        compiler_params=params(56),
        cost_estimate=takes(1),
        name="edge_rows",
    )(start, fields)


def conv_kernel(
    chunks, picks, has_edge, after, pair_ref, place_ref, lat_ref, lon_ref, basis_ref, value_ref, fields_ref, *rest
):
    if has_edge:
        edge_ref, weight_ref, *rest = rest
    else:
        edge_ref, (weight_ref, *rest) = None, rest
    *out_refs, rows_ref, taps_ref, filt_ref = rest[after:]
    own, _, lon = fields_ref.shape
    chunk = lon // chunks
    width = out_refs[0].shape[1]
    total = rows_ref.shape[2]
    pair = pair_ref[0]
    own_at = HALO * (1 - pair)
    edge_at = own * pair

    def put(slot, cells):
        rows_ref[slot, :, LANES : LANES + lon] = cells
        rows_ref[slot, :, 0:LANES] = cells[:, lon - LANES :]
        full = (lon // LANES) * LANES
        tail = total - LANES - lon
        rows_ref[slot, :, LANES + full :] = jnp.concatenate(
            [cells[:, full:], cells[:, :tail]], axis=1
        )

    for row in range(own):
        put(own_at + row, fields_ref[row])
    for row in range(HALO):
        if has_edge:
            put(edge_at + row, edge_ref[row])
        else:
            rows_ref[edge_at + row] = jnp.zeros(rows_ref.shape[1:], rows_ref.dtype)

    lane = lax.broadcasted_iota(jnp.int32, (G, LANES), 1)
    begins = [LANES + chunk * lax.rem(place_ref[0] + k, chunks) for k in picks]

    def fill(slot, tap, source, offset):
        for k, origin in enumerate(begins):
            begin = origin + offset
            first = lax.div(begin, LANES)
            shift = lax.rem(begin, LANES)
            back = lax.rem(LANES - shift, LANES)
            keep = lane < LANES - shift
            turned = []
            for t in range(width // LANES + 1):
                start = pl.multiple_of((first + t) * LANES, LANES)
                tile = rows_ref[source, :, pl.ds(start, LANES)]
                turned.append(pltpu.roll(tile, back, 1))
            for t in range(width // LANES):
                at = k * width + t * LANES
                taps_ref[slot, tap * G : (tap + 1) * G, at : at + LANES] = jnp.where(
                    keep, turned[t], turned[t + 1]
                )

    eye = jnp.where(
        lax.broadcasted_iota(jnp.int32, (G, G), 0) == lax.broadcasted_iota(jnp.int32, (G, G), 1),
        1.0,
        0.0,
    ).astype(jnp.bfloat16)
    for i in range(2):
        row = 2 * pair + i
        pieces = []
        for tap in range(S):
            picked = weight_ref[basis_ref[row, tap]].astype(jnp.float32) * value_ref[row, tap]
            pieces.append(picked.astype(jnp.bfloat16))
        pieces.append(eye)
        for k in range(TAPS // 2):
            filt_ref[i, :, k * 2 * G : (k + 1) * 2 * G] = jnp.concatenate(
                [pieces[2 * k], pieces[2 * k + 1]], axis=1
            )
        for tap in range(S):
            fill(i, tap, HALO + i + lat_ref[row, tap], lon_ref[row, tap])
        fill(i, S, HALO + i, 0)
        mixed = jnp.dot(filt_ref[i], taps_ref[i], preferred_element_type=jnp.float32).astype(
            jnp.bfloat16
        )
        for k in range(len(picks)):
            out_refs[k][i * G : (i + 1) * G, :] = mixed[:, k * width : (k + 1) * width]


def conv_rows(pair, place, supports, fields, edge, weight, chunks, picks, after, roomy):
    own, chans, lon = fields.shape
    width = ceil_to(lon // chunks, LANES)
    highest = (LANES + lon - lon // chunks + DLON) // LANES
    total = (highest + 1) * LANES + width
    arrays = [fields] + ([] if edge is None else [edge]) + [weight]
    return pl.pallas_call(
        functools.partial(conv_kernel, chunks, picks, edge is not None, len(after)),
        out_shape=[jax.ShapeDtypeStruct((2 * chans, width), jnp.bfloat16)] * len(picks),
        in_specs=[SMEM] * 6 + [VMEM] * len(arrays) + [ANY] * len(after),
        out_specs=[VMEM] * len(picks),
        scratch_shapes=[
            pltpu.VMEM((own + HALO, chans, total), jnp.bfloat16),
            pltpu.VMEM((2, TAPS * G, len(picks) * width), jnp.bfloat16),
            pltpu.VMEM((2, G, TAPS * G), jnp.bfloat16),
        ],
        compiler_params=params(56 if roomy else 20),
        cost_estimate=takes(1 if len(picks) > 1 else 0.2),
        name="conv_rows",
    )(pair, place, *supports, *arrays, *after)


def mlp_kernel(parts, last, after, place_ref, *rest):
    blocks, rest = rest[:parts], rest[parts:]
    up_ref, down_ref, table_ref, *rest = rest
    rest = rest[after:]
    if last:
        earlier_ref, out_ref, cells_ref = rest
    else:
        out_ref, cells_ref = rest
    width = blocks[0].shape[1]
    place = place_ref[0]
    for k in range(parts):
        source = pl.multiple_of(lax.rem(place - k + parts, parts) * G, G)
        for i in range(2):
            cells_ref[pl.ds(source, G), i * width : (i + 1) * width] = blocks[k][
                i * G : (i + 1) * G, :
            ]
    values = cells_ref[...].astype(jnp.float32)
    center = values - jnp.mean(values, axis=0, keepdims=True)
    spread = jnp.mean(center * center, axis=0, keepdims=True)
    normed = (center * lax.rsqrt(spread + EPS)).astype(jnp.bfloat16)
    lifted = jnp.dot(up_ref[...], normed, preferred_element_type=jnp.float32)
    scale = math.sqrt(2.0 / math.pi)
    inner = lifted * (scale + (scale * 0.044715) * (lifted * lifted))
    half = 0.5 * lifted
    active = (half + half * jnp.tanh(inner)).astype(jnp.bfloat16)
    lowered = jnp.dot(down_ref[...], active, preferred_element_type=jnp.float32)
    result = (values + lowered).astype(jnp.bfloat16)
    found = []
    for i in range(2):
        modes = lax.dot_general(
            table_ref[place],
            result[:, i * width : (i + 1) * width],
            (((1,), (1,)), ((), ())),
            preferred_element_type=jnp.float32,
        )
        found.append(modes.reshape(modes.shape[0] // SLOT, SLOT, modes.shape[1]))
    block = jnp.concatenate(found, axis=1).astype(jnp.bfloat16)
    if last:
        out_ref[:, 0 : 2 * SLOT, :] = earlier_ref[...]
        out_ref[:, 2 * SLOT : 4 * SLOT, :] = block
    else:
        out_ref[...] = block


def mlp_rows(place, blocks, up, down, tables, earlier, dests, after):
    pair_chans, width = blocks[0].shape
    chan = len(blocks) * pair_chans // 2
    last = earlier is not None
    arrays = [*blocks, up, down, tables, *after] + ([earlier] if last else [])
    rows = (4 if last else 2) * SLOT
    return pl.pallas_call(
        functools.partial(mlp_kernel, len(blocks), last, len(after)),
        out_shape=jax.ShapeDtypeStruct((dests, rows, chan), jnp.bfloat16),
        in_specs=[SMEM]
        + [VMEM] * (len(blocks) + 3)
        + [ANY] * len(after)
        + [VMEM] * last,
        out_specs=VMEM,
        scratch_shapes=[pltpu.VMEM((chan, 2 * width), jnp.bfloat16)],
        compiler_params=params(20 if dests <= FEW else 40),
        cost_estimate=takes(1),
        name="mlp_rows",
    )(place, *arrays)


def expand_kernel(start_ref, legendre_ref, spread_ref, out_ref):
    _, lats, degrees = legendre_ref.shape
    m = pl.program_id(0)
    degree = lax.broadcasted_iota(jnp.int32, (lats, degrees), 1)
    kept = jnp.where(degree >= start_ref[0] + m, legendre_ref[0].astype(jnp.float32), 0.0)
    wide = lax.dot_general(
        kept.astype(jnp.bfloat16),
        spread_ref[...],
        (((0,), (0,)), ((), ())),
        preferred_element_type=jnp.float32,
    )
    slot = lax.rem(lax.broadcasted_iota(jnp.int32, wide.shape, 1), SLOT)
    for r in range(2):
        out_ref[0, r] = jnp.where(slot == 2 * m + r, wide, 0.0).astype(jnp.bfloat16)


def expand(start, legendre, spread):
    modes, lats, degrees = legendre.shape
    depth = spread.shape[1]
    return pl.pallas_call(
        expand_kernel,
        out_shape=jax.ShapeDtypeStruct((modes, 2, degrees, depth), jnp.bfloat16),
        grid=(modes,),
        in_specs=[
            SMEM,
            pl.BlockSpec((1, lats, degrees), lambda m: (m, 0, 0)),
            pl.BlockSpec((lats, depth), lambda m: (0, 0)),
        ],
        out_specs=pl.BlockSpec((1, 2, degrees, depth), lambda m: (m, 0, 0, 0)),
        compiler_params=params(10 if depth <= 512 else 48),
        cost_estimate=takes(0.2),
        name="expand",
    )(start, legendre, spread)


def final_kernel(left_ref, spectrum_ref, out_ref, result_ref, sems):
    modes = left_ref.shape[0]
    chan = spectrum_ref.shape[1]
    copies = []
    for m in range(modes):
        for r in range(2):
            result_ref[m, :, r * chan : (r + 1) * chan] = jnp.dot(
                left_ref[m, r], spectrum_ref[...], preferred_element_type=jnp.float32
            ).astype(jnp.bfloat16)
        copies.append(pltpu.make_async_copy(result_ref.at[m], out_ref.at[m], sems.at[m]))
        copies[-1].start()
    for copy in copies:
        copy.wait()


def final_sum(left, spectrum):
    modes, _, degrees, depth = left.shape
    shape = (modes, degrees, 2 * spectrum.shape[1])
    return pl.pallas_call(
        final_kernel,
        out_shape=jax.ShapeDtypeStruct(shape, jnp.bfloat16),
        in_specs=[VMEM, VMEM],
        out_specs=HBM,
        scratch_shapes=[pltpu.VMEM(shape, jnp.bfloat16), pltpu.SemaphoreType.DMA((modes,))],
        compiler_params=params(8 if depth <= 512 else 48),
        cost_estimate=takes(1),
        name="final_sum",
    )(left, spectrum)


def fourier_blocks(lon, chunks, width, dests, mode_dev):
    chunk = lon // chunks
    index = np.arange(lon, dtype=np.int64)
    mode = np.arange(dests * mode_dev, dtype=np.int64)
    angle = ((mode[:, None] * index[None, :]) % lon) * (2.0 * math.pi / lon)
    paired = np.stack([np.cos(angle), -np.sin(angle)], axis=1) * math.sqrt(2.0 / lon)
    paired = paired.reshape(dests, 2 * mode_dev, chunks, chunk)
    table = np.zeros((chunks, dests, SLOT, width), np.float32)
    table[:, :, : 2 * mode_dev, :chunk] = np.transpose(paired, (2, 0, 1, 3))
    return table.reshape(chunks, dests * SLOT, width).astype(jnp.bfloat16)


def turn(block, axis, count, step):
    return lax.ppermute(block, axis, [(i, (i + step) % count) for i in range(count)])


def scalar(value):
    return jnp.asarray(value, jnp.int32).reshape(1)


def on_device(
    fields,
    disco_weight,
    support_lat,
    support_lon,
    support_basis,
    support_value,
    w_up,
    w_down,
    legendre,
):
    lat_dev, lon, _ = fields.shape
    num_lat = lax.axis_size("lat")
    num_chan = lax.axis_size("chan")
    mode_dev, _, lats = legendre.shape
    dests = num_lat * num_chan
    width = ceil_to(lon // num_chan, LANES)
    band = lax.axis_index("lat")
    place = scalar(lax.axis_index("chan"))
    index = lax.axis_index(("lat", "chan"))
    supports = (support_lat, support_lon, support_basis, support_value)

    two_bands = num_lat == 2
    cells = jnp.swapaxes(fields, 1, 2)
    if two_bands:
        edge_out = edge_rows(scalar(HALO * (1 - band)), cells)
        edges = [None, lax.ppermute(edge_out, "lat", [(0, 1), (1, 0)])]
        pairs = [band, 1 - band]
    else:
        ends = num_lat - 1
        edges = [
            lax.ppermute(cells[lat_dev - HALO :], "lat", [(i, i + 1) for i in range(ends)]),
            lax.ppermute(cells[:HALO], "lat", [(i + 1, i) for i in range(ends)]),
        ]
        pairs = [0, 1]

    tables = jnp.asarray(fourier_blocks(lon, num_chan, width, dests, mode_dev))
    up = w_up.T
    down = w_down.T

    depth = dests * 4 * SLOT
    row = np.arange(depth)
    source_band = row // (4 * SLOT) // num_chan
    phase = (row // (2 * SLOT)) % 2
    source_pair = (phase ^ source_band) if two_bands else phase
    lat_of = lat_dev * source_band + 2 * source_pair + (row // SLOT) % 2
    spread = (lat_of[None, :] == np.arange(lats)[:, None]).astype(jnp.bfloat16)
    left = expand(scalar(index * mode_dev), jnp.swapaxes(legendre, 1, 2), jnp.asarray(spread))

    received = []
    after = [edge_out] if two_bands else []
    for edge, pair in zip(edges, pairs):
        shared = (scalar(pair), place, supports, cells, edge, disco_weight, num_chan)
        sent = conv_rows(*shared, tuple(range(1, num_chan)), after, edge is None)
        kept = conv_rows(*shared, (0,), sent[:1], False)
        received.append(
            list(kept) + [turn(block, "chan", num_chan, k + 1) for k, block in enumerate(sent)]
        )
        after = kept
    spectrum = None
    after = list(after)
    for blocks in received:
        spectrum = mlp_rows(place, blocks, up, down, tables, spectrum, dests, after)
        after = []

    both = ("lat", "chan")
    gathered = lax.all_to_all(spectrum, both, split_axis=0, concat_axis=0, tiled=True)
    return final_sum(left, gathered.reshape(depth, gathered.shape[2]))


def solution(mesh):
    in_specs = (
        P(("tm", "lat"), None, "chan"),
        P(None, "chan", None),
        P("lat", None),
        P("lat", None),
        P("lat", None),
        P("lat", None),
        P(),
        P(),
        P(("lat", "chan"), None, None),
    )
    out_specs = P(("tm", "lat", "chan"), None, None)
    return jax.shard_map(
        on_device, mesh=mesh, in_specs=in_specs, out_specs=out_specs, check_vma=False
    )
```

```python
import functools
import math

import jax
import jax.numpy as jnp
import numpy as np
from jax import lax
from jax.experimental import pallas as pl
from jax.experimental.pallas import tpu as pltpu
from jax.sharding import PartitionSpec as P

G = 64
S = 9
HALO = 2
DLON = 4
TAPS = S + 1
LANES = 128
SLOT = 8
EPS = 1e-05
FEW = 8
MIB = 1024 * 1024
FLOPS_PER_US = 1_000_000_000

SMEM = pl.BlockSpec(memory_space=pltpu.SMEM)
VMEM = pl.BlockSpec(memory_space=pltpu.VMEM)
ANY = pl.BlockSpec(memory_space=pl.ANY)
HBM = pl.BlockSpec(memory_space=pltpu.HBM)


def ceil_to(value, step):
    return -(-value // step) * step


def params(mib):
    return pltpu.CompilerParams(vmem_limit_bytes=mib * MIB)


def takes(micros):
    return pl.CostEstimate(flops=int(micros * FLOPS_PER_US), bytes_accessed=0, transcendentals=0)


def conv_kernel(
    chunks, picks, has_edge, after, pair_ref, place_ref, lat_ref, lon_ref, basis_ref, value_ref, fields_ref, *rest
):
    if has_edge:
        edge_ref, weight_ref, *rest = rest
    else:
        edge_ref, (weight_ref, *rest) = None, rest
    *out_refs, rows_ref, taps_ref, filt_ref = rest[after:]
    own, _, lon = fields_ref.shape
    chunk = lon // chunks
    width = out_refs[0].shape[1]
    total = rows_ref.shape[2]
    pair = pair_ref[0]
    own_at = HALO * (1 - pair)
    edge_at = own * pair

    def put(slot, cells):
        rows_ref[slot, :, LANES : LANES + lon] = cells
        rows_ref[slot, :, 0:LANES] = cells[:, lon - LANES :]
        full = (lon // LANES) * LANES
        tail = total - LANES - lon
        rows_ref[slot, :, LANES + full :] = jnp.concatenate(
            [cells[:, full:], cells[:, :tail]], axis=1
        )

    for row in range(own):
        put(own_at + row, fields_ref[row])
    for row in range(HALO):
        if has_edge:
            put(edge_at + row, edge_ref[row])
        else:
            rows_ref[edge_at + row] = jnp.zeros(rows_ref.shape[1:], rows_ref.dtype)

    lane = lax.broadcasted_iota(jnp.int32, (G, LANES), 1)
    begins = [LANES + chunk * lax.rem(place_ref[0] + k, chunks) for k in picks]

    def fill(slot, tap, source, offset):
        for k, origin in enumerate(begins):
            begin = origin + offset
            first = lax.div(begin, LANES)
            shift = lax.rem(begin, LANES)
            back = lax.rem(LANES - shift, LANES)
            keep = lane < LANES - shift
            turned = []
            for t in range(width // LANES + 1):
                start = pl.multiple_of((first + t) * LANES, LANES)
                tile = rows_ref[source, :, pl.ds(start, LANES)]
                turned.append(pltpu.roll(tile, back, 1))
            for t in range(width // LANES):
                at = k * width + t * LANES
                taps_ref[slot, tap * G : (tap + 1) * G, at : at + LANES] = jnp.where(
                    keep, turned[t], turned[t + 1]
                )

    eye = jnp.where(
        lax.broadcasted_iota(jnp.int32, (G, G), 0) == lax.broadcasted_iota(jnp.int32, (G, G), 1),
        1.0,
        0.0,
    ).astype(jnp.bfloat16)
    for i in range(2):
        row = 2 * pair + i
        pieces = []
        for tap in range(S):
            picked = weight_ref[basis_ref[row, tap]].astype(jnp.float32) * value_ref[row, tap]
            pieces.append(picked.astype(jnp.bfloat16))
        pieces.append(eye)
        for k in range(TAPS // 2):
            filt_ref[i, :, k * 2 * G : (k + 1) * 2 * G] = jnp.concatenate(
                [pieces[2 * k], pieces[2 * k + 1]], axis=1
            )
        for tap in range(S):
            fill(i, tap, HALO + i + lat_ref[row, tap], lon_ref[row, tap])
        fill(i, S, HALO + i, 0)
        mixed = jnp.dot(filt_ref[i], taps_ref[i], preferred_element_type=jnp.float32).astype(
            jnp.bfloat16
        )
        for k in range(len(picks)):
            out_refs[k][i * G : (i + 1) * G, :] = mixed[:, k * width : (k + 1) * width]


def conv_rows(pair, place, supports, fields, edge, weight, chunks, picks, after, roomy):
    own, chans, lon = fields.shape
    width = ceil_to(lon // chunks, LANES)
    highest = (LANES + lon - lon // chunks + DLON) // LANES
    total = (highest + 1) * LANES + width
    arrays = [fields] + ([] if edge is None else [edge]) + [weight]
    return pl.pallas_call(
        functools.partial(conv_kernel, chunks, picks, edge is not None, len(after)),
        out_shape=[jax.ShapeDtypeStruct((2 * chans, width), jnp.bfloat16)] * len(picks),
        in_specs=[SMEM] * 6 + [VMEM] * len(arrays) + [ANY] * len(after),
        out_specs=[VMEM] * len(picks),
        scratch_shapes=[
            pltpu.VMEM((own + HALO, chans, total), jnp.bfloat16),
            pltpu.VMEM((2, TAPS * G, len(picks) * width), jnp.bfloat16),
            pltpu.VMEM((2, G, TAPS * G), jnp.bfloat16),
        ],
        compiler_params=params(56 if roomy else 20),
        cost_estimate=takes(1 if len(picks) > 1 else 0.2),
        name="conv_rows",
    )(pair, place, *supports, *arrays, *after)


def mlp_kernel(parts, last, after, place_ref, *rest):
    blocks, rest = rest[:parts], rest[parts:]
    up_ref, down_ref, table_ref, *rest = rest
    rest = rest[after:]
    if last:
        earlier_ref, out_ref, cells_ref = rest
    else:
        out_ref, cells_ref = rest
    width = blocks[0].shape[1]
    place = place_ref[0]
    for k in range(parts):
        source = pl.multiple_of(lax.rem(place - k + parts, parts) * G, G)
        for i in range(2):
            cells_ref[pl.ds(source, G), i * width : (i + 1) * width] = blocks[k][
                i * G : (i + 1) * G, :
            ]
    values = cells_ref[...].astype(jnp.float32)
    center = values - jnp.mean(values, axis=0, keepdims=True)
    spread = jnp.mean(center * center, axis=0, keepdims=True)
    normed = (center * lax.rsqrt(spread + EPS)).astype(jnp.bfloat16)
    lifted = jnp.dot(up_ref[...], normed, preferred_element_type=jnp.float32)
    scale = math.sqrt(2.0 / math.pi)
    inner = lifted * (scale + (scale * 0.044715) * (lifted * lifted))
    half = 0.5 * lifted
    active = (half + half * jnp.tanh(inner)).astype(jnp.bfloat16)
    lowered = jnp.dot(down_ref[...], active, preferred_element_type=jnp.float32)
    result = (values + lowered).astype(jnp.bfloat16)
    found = []
    for i in range(2):
        modes = lax.dot_general(
            table_ref[place],
            result[:, i * width : (i + 1) * width],
            (((1,), (1,)), ((), ())),
            preferred_element_type=jnp.float32,
        )
        found.append(modes.reshape(modes.shape[0] // SLOT, SLOT, modes.shape[1]))
    block = jnp.concatenate(found, axis=1).astype(jnp.bfloat16)
    if last:
        out_ref[:, 0 : 2 * SLOT, :] = earlier_ref[...]
        out_ref[:, 2 * SLOT : 4 * SLOT, :] = block
    else:
        out_ref[...] = block


def mlp_rows(place, blocks, up, down, tables, earlier, dests, after):
    pair_chans, width = blocks[0].shape
    chan = len(blocks) * pair_chans // 2
    last = earlier is not None
    arrays = [*blocks, up, down, tables, *after] + ([earlier] if last else [])
    rows = (4 if last else 2) * SLOT
    return pl.pallas_call(
        functools.partial(mlp_kernel, len(blocks), last, len(after)),
        out_shape=jax.ShapeDtypeStruct((dests, rows, chan), jnp.bfloat16),
        in_specs=[SMEM]
        + [VMEM] * (len(blocks) + 3)
        + [ANY] * len(after)
        + [VMEM] * last,
        out_specs=VMEM,
        scratch_shapes=[pltpu.VMEM((chan, 2 * width), jnp.bfloat16)],
        compiler_params=params(20 if dests <= FEW else 40),
        cost_estimate=takes(1),
        name="mlp_rows",
    )(place, *arrays)


def expand_kernel(start_ref, legendre_ref, spread_ref, out_ref):
    _, lats, degrees = legendre_ref.shape
    m = pl.program_id(0)
    degree = lax.broadcasted_iota(jnp.int32, (lats, degrees), 1)
    kept = jnp.where(degree >= start_ref[0] + m, legendre_ref[0].astype(jnp.float32), 0.0)
    wide = lax.dot_general(
        kept.astype(jnp.bfloat16),
        spread_ref[...],
        (((0,), (0,)), ((), ())),
        preferred_element_type=jnp.float32,
    )
    slot = lax.rem(lax.broadcasted_iota(jnp.int32, wide.shape, 1), SLOT)
    for r in range(2):
        out_ref[0, r] = jnp.where(slot == 2 * m + r, wide, 0.0).astype(jnp.bfloat16)


def expand(start, legendre, spread):
    modes, lats, degrees = legendre.shape
    depth = spread.shape[1]
    return pl.pallas_call(
        expand_kernel,
        out_shape=jax.ShapeDtypeStruct((modes, 2, degrees, depth), jnp.bfloat16),
        grid=(modes,),
        in_specs=[
            SMEM,
            pl.BlockSpec((1, lats, degrees), lambda m: (m, 0, 0)),
            pl.BlockSpec((lats, depth), lambda m: (0, 0)),
        ],
        out_specs=pl.BlockSpec((1, 2, degrees, depth), lambda m: (m, 0, 0, 0)),
        compiler_params=params(10 if depth <= 512 else 48),
        cost_estimate=takes(0.2),
        name="expand",
    )(start, legendre, spread)


def final_kernel(left_ref, spectrum_ref, out_ref, result_ref, sems):
    modes = left_ref.shape[0]
    chan = spectrum_ref.shape[1]
    copies = []
    for m in range(modes):
        for r in range(2):
            result_ref[m, :, r * chan : (r + 1) * chan] = jnp.dot(
                left_ref[m, r], spectrum_ref[...], preferred_element_type=jnp.float32
            ).astype(jnp.bfloat16)
        copies.append(pltpu.make_async_copy(result_ref.at[m], out_ref.at[m], sems.at[m]))
        copies[-1].start()
    for copy in copies:
        copy.wait()


def final_sum(left, spectrum):
    modes, _, degrees, depth = left.shape
    shape = (modes, degrees, 2 * spectrum.shape[1])
    return pl.pallas_call(
        final_kernel,
        out_shape=jax.ShapeDtypeStruct(shape, jnp.bfloat16),
        in_specs=[VMEM, VMEM],
        out_specs=HBM,
        scratch_shapes=[pltpu.VMEM(shape, jnp.bfloat16), pltpu.SemaphoreType.DMA((modes,))],
        compiler_params=params(8 if depth <= 512 else 48),
        cost_estimate=takes(1),
        name="final_sum",
    )(left, spectrum)


def fourier_blocks(lon, chunks, width, dests, mode_dev):
    chunk = lon // chunks
    index = np.arange(lon, dtype=np.int64)
    mode = np.arange(dests * mode_dev, dtype=np.int64)
    angle = ((mode[:, None] * index[None, :]) % lon) * (2.0 * math.pi / lon)
    paired = np.stack([np.cos(angle), -np.sin(angle)], axis=1) * math.sqrt(2.0 / lon)
    paired = paired.reshape(dests, 2 * mode_dev, chunks, chunk)
    table = np.zeros((chunks, dests, SLOT, width), np.float32)
    table[:, :, : 2 * mode_dev, :chunk] = np.transpose(paired, (2, 0, 1, 3))
    return table.reshape(chunks, dests * SLOT, width).astype(jnp.bfloat16)


def turn(block, axis, count, step):
    return lax.ppermute(block, axis, [(i, (i + step) % count) for i in range(count)])


def scalar(value):
    return jnp.asarray(value, jnp.int32).reshape(1)


def on_device(
    fields,
    disco_weight,
    support_lat,
    support_lon,
    support_basis,
    support_value,
    w_up,
    w_down,
    legendre,
):
    lat_dev, lon, _ = fields.shape
    num_lat = lax.axis_size("lat")
    num_chan = lax.axis_size("chan")
    mode_dev, _, lats = legendre.shape
    dests = num_lat * num_chan
    width = ceil_to(lon // num_chan, LANES)
    band = lax.axis_index("lat")
    place = scalar(lax.axis_index("chan"))
    index = lax.axis_index(("lat", "chan"))
    supports = (support_lat, support_lon, support_basis, support_value)

    two_bands = num_lat == 2
    cells = jnp.swapaxes(fields, 1, 2)
    if two_bands:
        edge_out = lax.dynamic_slice_in_dim(cells, HALO * (1 - band), HALO, axis=0)
        edges = [None, lax.ppermute(edge_out, "lat", [(0, 1), (1, 0)])]
        pairs = [band, 1 - band]
    else:
        ends = num_lat - 1
        edges = [
            lax.ppermute(cells[lat_dev - HALO :], "lat", [(i, i + 1) for i in range(ends)]),
            lax.ppermute(cells[:HALO], "lat", [(i + 1, i) for i in range(ends)]),
        ]
        pairs = [0, 1]

    tables = jnp.asarray(fourier_blocks(lon, num_chan, width, dests, mode_dev))
    up = w_up.T
    down = w_down.T

    depth = dests * 4 * SLOT
    row = np.arange(depth)
    source_band = row // (4 * SLOT) // num_chan
    phase = (row // (2 * SLOT)) % 2
    source_pair = (phase ^ source_band) if two_bands else phase
    lat_of = lat_dev * source_band + 2 * source_pair + (row // SLOT) % 2
    spread = (lat_of[None, :] == np.arange(lats)[:, None]).astype(jnp.bfloat16)
    left = expand(scalar(index * mode_dev), jnp.swapaxes(legendre, 1, 2), jnp.asarray(spread))

    received = []
    after = []
    for edge, pair in zip(edges, pairs):
        shared = (scalar(pair), place, supports, cells, edge, disco_weight, num_chan)
        sent = conv_rows(*shared, tuple(range(1, num_chan)), after, edge is None)
        moved = [turn(block, "chan", num_chan, k + 1) for k, block in enumerate(sent)]
        kept = conv_rows(*shared, (0,), sent[-1:], False)
        received.append([*kept, *moved])
        after = kept
    spectrum = None
    after = list(after)
    for blocks in received:
        spectrum = mlp_rows(place, blocks, up, down, tables, spectrum, dests, after)
        after = []

    both = ("lat", "chan")
    gathered = lax.all_to_all(spectrum, both, split_axis=0, concat_axis=0, tiled=True)
    return final_sum(left, gathered.reshape(depth, gathered.shape[2]))


def solution(mesh):
    in_specs = (
        P(("tm", "lat"), None, "chan"),
        P(None, "chan", None),
        P("lat", None),
        P("lat", None),
        P("lat", None),
        P("lat", None),
        P(),
        P(),
        P(("lat", "chan"), None, None),
    )
    out_specs = P(("tm", "lat", "chan"), None, None)
    return jax.shard_map(
        on_device, mesh=mesh, in_specs=in_specs, out_specs=out_specs, check_vma=False
    )
```

```python
import functools
import math

import jax
import jax.numpy as jnp
import numpy as np
from jax import lax
from jax.experimental import pallas as pl
from jax.experimental.pallas import tpu as pltpu
from jax.sharding import PartitionSpec as P

G = 64
S = 9
HALO = 2
DLON = 4
TAPS = S + 1
LANES = 128
SLOT = 8
EPS = 1e-05
FEW = 8
MIB = 1024 * 1024
FLOPS_PER_US = 1_000_000_000

SMEM = pl.BlockSpec(memory_space=pltpu.SMEM)
VMEM = pl.BlockSpec(memory_space=pltpu.VMEM)
ANY = pl.BlockSpec(memory_space=pl.ANY)
HBM = pl.BlockSpec(memory_space=pltpu.HBM)


def ceil_to(value, step):
    return -(-value // step) * step


def params(mib):
    return pltpu.CompilerParams(vmem_limit_bytes=mib * MIB)


def takes(micros):
    return pl.CostEstimate(flops=int(micros * FLOPS_PER_US), bytes_accessed=0, transcendentals=0)


def paired(count):
    return count & (count - 1) == 0


def target(place, k, count):
    return place ^ k if paired(count) else (place + k) % count


def source(place, k, count):
    return place ^ k if paired(count) else (place - k + count) % count


def issue_order(count):
    return [*range(2, count), 1] if paired(count) else list(range(1, count))


def conv_kernel(
    chunks, picks, has_edge, after, pair_ref, place_ref, lat_ref, lon_ref, basis_ref, value_ref, fields_ref, *rest
):
    if has_edge:
        edge_ref, weight_ref, *rest = rest
    else:
        edge_ref, (weight_ref, *rest) = None, rest
    *out_refs, rows_ref, taps_ref, filt_ref = rest[after:]
    own, _, lon = fields_ref.shape
    chunk = lon // chunks
    width = out_refs[0].shape[1]
    total = rows_ref.shape[2]
    pair = pair_ref[0]
    own_at = HALO * (1 - pair)
    edge_at = own * pair

    def put(slot, cells):
        rows_ref[slot, :, LANES : LANES + lon] = cells
        rows_ref[slot, :, 0:LANES] = cells[:, lon - LANES :]
        full = (lon // LANES) * LANES
        tail = total - LANES - lon
        rows_ref[slot, :, LANES + full :] = jnp.concatenate(
            [cells[:, full:], cells[:, :tail]], axis=1
        )

    for row in range(own):
        put(own_at + row, fields_ref[row])
    for row in range(HALO):
        if has_edge:
            put(edge_at + row, edge_ref[row])
        else:
            rows_ref[edge_at + row] = jnp.zeros(rows_ref.shape[1:], rows_ref.dtype)

    lane = lax.broadcasted_iota(jnp.int32, (G, LANES), 1)
    begins = [LANES + chunk * target(place_ref[0], k, chunks) for k in picks]

    def fill(slot, tap, source, offset):
        for k, origin in enumerate(begins):
            begin = origin + offset
            first = lax.div(begin, LANES)
            shift = lax.rem(begin, LANES)
            back = lax.rem(LANES - shift, LANES)
            keep = lane < LANES - shift
            turned = []
            for t in range(width // LANES + 1):
                start = pl.multiple_of((first + t) * LANES, LANES)
                tile = rows_ref[source, :, pl.ds(start, LANES)]
                turned.append(pltpu.roll(tile, back, 1))
            for t in range(width // LANES):
                at = k * width + t * LANES
                taps_ref[slot, tap * G : (tap + 1) * G, at : at + LANES] = jnp.where(
                    keep, turned[t], turned[t + 1]
                )

    eye = jnp.where(
        lax.broadcasted_iota(jnp.int32, (G, G), 0) == lax.broadcasted_iota(jnp.int32, (G, G), 1),
        1.0,
        0.0,
    ).astype(jnp.bfloat16)
    for i in range(2):
        row = 2 * pair + i
        pieces = []
        for tap in range(S):
            picked = weight_ref[basis_ref[row, tap]].astype(jnp.float32) * value_ref[row, tap]
            pieces.append(picked.astype(jnp.bfloat16))
        pieces.append(eye)
        for k in range(TAPS // 2):
            filt_ref[i, :, k * 2 * G : (k + 1) * 2 * G] = jnp.concatenate(
                [pieces[2 * k], pieces[2 * k + 1]], axis=1
            )
        for tap in range(S):
            fill(i, tap, HALO + i + lat_ref[row, tap], lon_ref[row, tap])
        fill(i, S, HALO + i, 0)
        mixed = jnp.dot(filt_ref[i], taps_ref[i], preferred_element_type=jnp.float32).astype(
            jnp.bfloat16
        )
        for k in range(len(picks)):
            out_refs[k][i * G : (i + 1) * G, :] = mixed[:, k * width : (k + 1) * width]


def conv_rows(pair, place, supports, fields, edge, weight, chunks, picks, after, roomy):
    own, chans, lon = fields.shape
    width = ceil_to(lon // chunks, LANES)
    highest = (LANES + lon - lon // chunks + DLON) // LANES
    total = (highest + 1) * LANES + width
    arrays = [fields] + ([] if edge is None else [edge]) + [weight]
    return pl.pallas_call(
        functools.partial(conv_kernel, chunks, picks, edge is not None, len(after)),
        out_shape=[jax.ShapeDtypeStruct((2 * chans, width), jnp.bfloat16)] * len(picks),
        in_specs=[SMEM] * 6 + [VMEM] * len(arrays) + [ANY] * len(after),
        out_specs=[VMEM] * len(picks),
        scratch_shapes=[
            pltpu.VMEM((own + HALO, chans, total), jnp.bfloat16),
            pltpu.VMEM((2, TAPS * G, len(picks) * width), jnp.bfloat16),
            pltpu.VMEM((2, G, TAPS * G), jnp.bfloat16),
        ],
        compiler_params=params(56 if roomy else 20),
        cost_estimate=takes(1 if len(picks) > 1 else 0.2),
        name="conv_rows",
    )(pair, place, *supports, *arrays, *after)


def mlp_kernel(parts, last, after, place_ref, *rest):
    blocks, rest = rest[:parts], rest[parts:]
    up_ref, down_ref, table_ref, *rest = rest
    rest = rest[after:]
    if last:
        earlier_ref, out_ref, cells_ref = rest
    else:
        out_ref, cells_ref = rest
    width = blocks[0].shape[1]
    place = place_ref[0]
    for block, k in zip(blocks, [0, *issue_order(parts)]):
        origin = pl.multiple_of(source(place, k, parts) * G, G)
        for i in range(2):
            cells_ref[pl.ds(origin, G), i * width : (i + 1) * width] = block[
                i * G : (i + 1) * G, :
            ]
    values = cells_ref[...].astype(jnp.float32)
    center = values - jnp.mean(values, axis=0, keepdims=True)
    spread = jnp.mean(center * center, axis=0, keepdims=True)
    normed = (center * lax.rsqrt(spread + EPS)).astype(jnp.bfloat16)
    lifted = jnp.dot(up_ref[...], normed, preferred_element_type=jnp.float32)
    scale = math.sqrt(2.0 / math.pi)
    inner = lifted * (scale + (scale * 0.044715) * (lifted * lifted))
    half = 0.5 * lifted
    active = (half + half * jnp.tanh(inner)).astype(jnp.bfloat16)
    lowered = jnp.dot(down_ref[...], active, preferred_element_type=jnp.float32)
    result = (values + lowered).astype(jnp.bfloat16)
    found = []
    for i in range(2):
        modes = lax.dot_general(
            table_ref[place],
            result[:, i * width : (i + 1) * width],
            (((1,), (1,)), ((), ())),
            preferred_element_type=jnp.float32,
        )
        found.append(modes.reshape(modes.shape[0] // SLOT, SLOT, modes.shape[1]))
    block = jnp.concatenate(found, axis=1).astype(jnp.bfloat16)
    if last:
        out_ref[:, 0 : 2 * SLOT, :] = earlier_ref[...]
        out_ref[:, 2 * SLOT : 4 * SLOT, :] = block
    else:
        out_ref[...] = block


def mlp_rows(place, blocks, up, down, tables, earlier, dests, after):
    pair_chans, width = blocks[0].shape
    chan = len(blocks) * pair_chans // 2
    last = earlier is not None
    arrays = [*blocks, up, down, tables, *after] + ([earlier] if last else [])
    rows = (4 if last else 2) * SLOT
    return pl.pallas_call(
        functools.partial(mlp_kernel, len(blocks), last, len(after)),
        out_shape=jax.ShapeDtypeStruct((dests, rows, chan), jnp.bfloat16),
        in_specs=[SMEM]
        + [VMEM] * (len(blocks) + 3)
        + [ANY] * len(after)
        + [VMEM] * last,
        out_specs=VMEM,
        scratch_shapes=[pltpu.VMEM((chan, 2 * width), jnp.bfloat16)],
        compiler_params=params(20 if dests <= FEW else 40),
        cost_estimate=takes(1),
        name="mlp_rows",
    )(place, *arrays)


def expand_kernel(start_ref, legendre_ref, spread_ref, out_ref):
    _, lats, degrees = legendre_ref.shape
    m = pl.program_id(0)
    degree = lax.broadcasted_iota(jnp.int32, (lats, degrees), 1)
    kept = jnp.where(degree >= start_ref[0] + m, legendre_ref[0].astype(jnp.float32), 0.0)
    wide = lax.dot_general(
        kept.astype(jnp.bfloat16),
        spread_ref[...],
        (((0,), (0,)), ((), ())),
        preferred_element_type=jnp.float32,
    )
    slot = lax.rem(lax.broadcasted_iota(jnp.int32, wide.shape, 1), SLOT)
    for r in range(2):
        out_ref[0, r] = jnp.where(slot == 2 * m + r, wide, 0.0).astype(jnp.bfloat16)


def expand(start, legendre, spread):
    modes, lats, degrees = legendre.shape
    depth = spread.shape[1]
    return pl.pallas_call(
        expand_kernel,
        out_shape=jax.ShapeDtypeStruct((modes, 2, degrees, depth), jnp.bfloat16),
        grid=(modes,),
        in_specs=[
            SMEM,
            pl.BlockSpec((1, lats, degrees), lambda m: (m, 0, 0)),
            pl.BlockSpec((lats, depth), lambda m: (0, 0)),
        ],
        out_specs=pl.BlockSpec((1, 2, degrees, depth), lambda m: (m, 0, 0, 0)),
        compiler_params=params(10 if depth <= 512 else 48),
        cost_estimate=takes(0.2),
        name="expand",
    )(start, legendre, spread)


def final_kernel(left_ref, spectrum_ref, out_ref, result_ref, sems):
    modes = left_ref.shape[0]
    chan = spectrum_ref.shape[1]
    copies = []
    for m in range(modes):
        for r in range(2):
            result_ref[m, :, r * chan : (r + 1) * chan] = jnp.dot(
                left_ref[m, r], spectrum_ref[...], preferred_element_type=jnp.float32
            ).astype(jnp.bfloat16)
        copies.append(pltpu.make_async_copy(result_ref.at[m], out_ref.at[m], sems.at[m]))
        copies[-1].start()
    for copy in copies:
        copy.wait()


def final_sum(left, spectrum):
    modes, _, degrees, depth = left.shape
    shape = (modes, degrees, 2 * spectrum.shape[1])
    return pl.pallas_call(
        final_kernel,
        out_shape=jax.ShapeDtypeStruct(shape, jnp.bfloat16),
        in_specs=[VMEM, VMEM],
        out_specs=HBM,
        scratch_shapes=[pltpu.VMEM(shape, jnp.bfloat16), pltpu.SemaphoreType.DMA((modes,))],
        compiler_params=params(8 if depth <= 512 else 48),
        cost_estimate=takes(1),
        name="final_sum",
    )(left, spectrum)


def fourier_blocks(lon, chunks, width, dests, mode_dev):
    chunk = lon // chunks
    index = np.arange(lon, dtype=np.int64)
    mode = np.arange(dests * mode_dev, dtype=np.int64)
    angle = ((mode[:, None] * index[None, :]) % lon) * (2.0 * math.pi / lon)
    paired = np.stack([np.cos(angle), -np.sin(angle)], axis=1) * math.sqrt(2.0 / lon)
    paired = paired.reshape(dests, 2 * mode_dev, chunks, chunk)
    table = np.zeros((chunks, dests, SLOT, width), np.float32)
    table[:, :, : 2 * mode_dev, :chunk] = np.transpose(paired, (2, 0, 1, 3))
    return table.reshape(chunks, dests * SLOT, width).astype(jnp.bfloat16)


def turn(block, axis, count, k):
    return lax.ppermute(block, axis, [(i, target(i, k, count)) for i in range(count)])


def scalar(value):
    return jnp.asarray(value, jnp.int32).reshape(1)


def on_device(
    fields,
    disco_weight,
    support_lat,
    support_lon,
    support_basis,
    support_value,
    w_up,
    w_down,
    legendre,
):
    lat_dev, lon, _ = fields.shape
    num_lat = lax.axis_size("lat")
    num_chan = lax.axis_size("chan")
    mode_dev, _, lats = legendre.shape
    dests = num_lat * num_chan
    width = ceil_to(lon // num_chan, LANES)
    band = lax.axis_index("lat")
    place = scalar(lax.axis_index("chan"))
    index = lax.axis_index(("lat", "chan"))
    supports = (support_lat, support_lon, support_basis, support_value)

    two_bands = num_lat == 2
    cells = jnp.swapaxes(fields, 1, 2)
    if two_bands:
        edge_out = lax.dynamic_slice_in_dim(cells, HALO * (1 - band), HALO, axis=0)
        edges = [None, lax.ppermute(edge_out, "lat", [(0, 1), (1, 0)])]
        pairs = [band, 1 - band]
    else:
        ends = num_lat - 1
        edges = [
            lax.ppermute(cells[lat_dev - HALO :], "lat", [(i, i + 1) for i in range(ends)]),
            lax.ppermute(cells[:HALO], "lat", [(i + 1, i) for i in range(ends)]),
        ]
        pairs = [0, 1]

    tables = jnp.asarray(fourier_blocks(lon, num_chan, width, dests, mode_dev))
    up = w_up.T
    down = w_down.T

    depth = dests * 4 * SLOT
    row = np.arange(depth)
    source_band = row // (4 * SLOT) // num_chan
    phase = (row // (2 * SLOT)) % 2
    source_pair = (phase ^ source_band) if two_bands else phase
    lat_of = lat_dev * source_band + 2 * source_pair + (row // SLOT) % 2
    spread = (lat_of[None, :] == np.arange(lats)[:, None]).astype(jnp.bfloat16)
    left = expand(scalar(index * mode_dev), jnp.swapaxes(legendre, 1, 2), jnp.asarray(spread))

    received = []
    after = []
    order = issue_order(num_chan)
    for edge, pair in zip(edges, pairs):
        shared = (scalar(pair), place, supports, cells, edge, disco_weight, num_chan)
        sent = conv_rows(*shared, order, after, edge is None)
        moved = [turn(block, "chan", num_chan, k) for k, block in zip(order, sent)]
        kept = conv_rows(*shared, (0,), sent[-1:], False)
        received.append([*kept, *moved])
        after = kept
    spectrum = None
    after = list(after)
    for blocks in received:
        spectrum = mlp_rows(place, blocks, up, down, tables, spectrum, dests, after)
        after = []

    both = ("lat", "chan")
    gathered = lax.all_to_all(spectrum, both, split_axis=0, concat_axis=0, tiled=True)
    return final_sum(left, gathered.reshape(depth, gathered.shape[2]))


def solution(mesh):
    in_specs = (
        P(("tm", "lat"), None, "chan"),
        P(None, "chan", None),
        P("lat", None),
        P("lat", None),
        P("lat", None),
        P("lat", None),
        P(),
        P(),
        P(("lat", "chan"), None, None),
    )
    out_specs = P(("tm", "lat", "chan"), None, None)
    return jax.shard_map(
        on_device, mesh=mesh, in_specs=in_specs, out_specs=out_specs, check_vma=False
    )
```

```python
import functools
import math

import jax
import jax.numpy as jnp
import numpy as np
from jax import lax
from jax.experimental import pallas as pl
from jax.experimental.pallas import tpu as pltpu
from jax.sharding import PartitionSpec as P

G = 64
S = 9
HALO = 2
DLON = 4
TAPS = S + 1
LANES = 128
SLOT = 8
EPS = 1e-05
FEW = 8
MIB = 1024 * 1024
FLOPS_PER_US = 1_000_000_000

SMEM = pl.BlockSpec(memory_space=pltpu.SMEM)
VMEM = pl.BlockSpec(memory_space=pltpu.VMEM)
ANY = pl.BlockSpec(memory_space=pl.ANY)
HBM = pl.BlockSpec(memory_space=pltpu.HBM)


def ceil_to(value, step):
    return -(-value // step) * step


def params(mib):
    return pltpu.CompilerParams(vmem_limit_bytes=mib * MIB)


def takes(micros):
    return pl.CostEstimate(flops=int(micros * FLOPS_PER_US), bytes_accessed=0, transcendentals=0)


def paired(count):
    return count & (count - 1) == 0


def target(place, k, count):
    return place ^ k if paired(count) else (place + k) % count


def source(place, k, count):
    return place ^ k if paired(count) else (place - k + count) % count


def issue_order(count):
    return [*range(2, count), 1] if paired(count) else list(range(1, count))


def conv_kernel(
    chunks, picks, has_edge, after, pair_ref, place_ref, lat_ref, lon_ref, basis_ref, value_ref, fields_ref, *rest
):
    if has_edge:
        edge_ref, weight_ref, *rest = rest
    else:
        edge_ref, (weight_ref, *rest) = None, rest
    *out_refs, rows_ref, taps_ref, filt_ref = rest[after:]
    own, _, lon = fields_ref.shape
    chunk = lon // chunks
    width = out_refs[0].shape[1]
    total = rows_ref.shape[2]
    pair = pair_ref[0]
    own_at = HALO * (1 - pair)
    edge_at = own * pair

    def put(slot, cells):
        rows_ref[slot, :, LANES : LANES + lon] = cells
        rows_ref[slot, :, 0:LANES] = cells[:, lon - LANES :]
        full = (lon // LANES) * LANES
        tail = total - LANES - lon
        rows_ref[slot, :, LANES + full :] = jnp.concatenate(
            [cells[:, full:], cells[:, :tail]], axis=1
        )

    for row in range(own):
        put(own_at + row, fields_ref[row])
    for row in range(HALO):
        if has_edge:
            put(edge_at + row, edge_ref[row])
        else:
            rows_ref[edge_at + row] = jnp.zeros(rows_ref.shape[1:], rows_ref.dtype)

    lane = lax.broadcasted_iota(jnp.int32, (G, LANES), 1)
    begins = [LANES + chunk * target(place_ref[0], k, chunks) for k in picks]

    def fill(slot, tap, source, offset):
        for k, origin in enumerate(begins):
            begin = origin + offset
            first = lax.div(begin, LANES)
            shift = lax.rem(begin, LANES)
            back = lax.rem(LANES - shift, LANES)
            keep = lane < LANES - shift
            turned = []
            for t in range(width // LANES + 1):
                start = pl.multiple_of((first + t) * LANES, LANES)
                tile = rows_ref[source, :, pl.ds(start, LANES)]
                turned.append(pltpu.roll(tile, back, 1))
            for t in range(width // LANES):
                at = k * width + t * LANES
                taps_ref[slot, tap * G : (tap + 1) * G, at : at + LANES] = jnp.where(
                    keep, turned[t], turned[t + 1]
                )

    eye = jnp.where(
        lax.broadcasted_iota(jnp.int32, (G, G), 0) == lax.broadcasted_iota(jnp.int32, (G, G), 1),
        1.0,
        0.0,
    ).astype(jnp.bfloat16)
    for i in range(2):
        row = 2 * pair + i
        pieces = []
        for tap in range(S):
            picked = weight_ref[basis_ref[row, tap]].astype(jnp.float32) * value_ref[row, tap]
            pieces.append(picked.astype(jnp.bfloat16))
        pieces.append(eye)
        for k in range(TAPS // 2):
            filt_ref[i, :, k * 2 * G : (k + 1) * 2 * G] = jnp.concatenate(
                [pieces[2 * k], pieces[2 * k + 1]], axis=1
            )
        for tap in range(S):
            fill(i, tap, HALO + i + lat_ref[row, tap], lon_ref[row, tap])
        fill(i, S, HALO + i, 0)
        mixed = jnp.dot(filt_ref[i], taps_ref[i], preferred_element_type=jnp.float32).astype(
            jnp.bfloat16
        )
        for k in range(len(picks)):
            out_refs[k][i * G : (i + 1) * G, :] = mixed[:, k * width : (k + 1) * width]


def conv_rows(pair, place, supports, fields, edge, weight, chunks, picks, after, roomy):
    own, chans, lon = fields.shape
    width = ceil_to(lon // chunks, LANES)
    highest = (LANES + lon - lon // chunks + DLON) // LANES
    total = (highest + 1) * LANES + width
    arrays = [fields] + ([] if edge is None else [edge]) + [weight]
    return pl.pallas_call(
        functools.partial(conv_kernel, chunks, picks, edge is not None, len(after)),
        out_shape=[jax.ShapeDtypeStruct((2 * chans, width), jnp.bfloat16)] * len(picks),
        in_specs=[SMEM] * 6 + [VMEM] * len(arrays) + [ANY] * len(after),
        out_specs=[VMEM] * len(picks),
        scratch_shapes=[
            pltpu.VMEM((own + HALO, chans, total), jnp.bfloat16),
            pltpu.VMEM((2, TAPS * G, len(picks) * width), jnp.bfloat16),
            pltpu.VMEM((2, G, TAPS * G), jnp.bfloat16),
        ],
        compiler_params=params(56 if roomy else 20),
        cost_estimate=takes(1 if len(picks) > 1 else 0.2),
        name="conv_rows",
    )(pair, place, *supports, *arrays, *after)


def mlp_kernel(parts, last, after, place_ref, *rest):
    blocks, rest = rest[:parts], rest[parts:]
    up_ref, down_ref, table_ref, *rest = rest
    rest = rest[after:]
    if last:
        earlier_ref, out_ref, cells_ref = rest
    else:
        out_ref, cells_ref = rest
    width = blocks[0].shape[1]
    place = place_ref[0]
    for block, k in zip(blocks, [0, *issue_order(parts)]):
        origin = pl.multiple_of(source(place, k, parts) * G, G)
        for i in range(2):
            cells_ref[pl.ds(origin, G), i * width : (i + 1) * width] = block[
                i * G : (i + 1) * G, :
            ]
    values = cells_ref[...].astype(jnp.float32)
    center = values - jnp.mean(values, axis=0, keepdims=True)
    spread = jnp.mean(center * center, axis=0, keepdims=True)
    normed = (center * lax.rsqrt(spread + EPS)).astype(jnp.bfloat16)
    lifted = jnp.dot(up_ref[...], normed, preferred_element_type=jnp.float32)
    scale = math.sqrt(2.0 / math.pi)
    inner = lifted * (scale + (scale * 0.044715) * (lifted * lifted))
    half = 0.5 * lifted
    active = (half + half * jnp.tanh(inner)).astype(jnp.bfloat16)
    lowered = jnp.dot(down_ref[...], active, preferred_element_type=jnp.float32)
    result = (values + lowered).astype(jnp.bfloat16)
    found = []
    for i in range(2):
        modes = lax.dot_general(
            table_ref[place],
            result[:, i * width : (i + 1) * width],
            (((1,), (1,)), ((), ())),
            preferred_element_type=jnp.float32,
        )
        found.append(modes.reshape(modes.shape[0] // SLOT, SLOT, modes.shape[1]))
    block = jnp.concatenate(found, axis=1).astype(jnp.bfloat16)
    if last:
        out_ref[:, 0 : 2 * SLOT, :] = earlier_ref[...]
        out_ref[:, 2 * SLOT : 4 * SLOT, :] = block
    else:
        out_ref[...] = block


def mlp_rows(place, blocks, up, down, tables, earlier, dests, after):
    pair_chans, width = blocks[0].shape
    chan = len(blocks) * pair_chans // 2
    last = earlier is not None
    arrays = [*blocks, up, down, tables, *after] + ([earlier] if last else [])
    rows = (4 if last else 2) * SLOT
    return pl.pallas_call(
        functools.partial(mlp_kernel, len(blocks), last, len(after)),
        out_shape=jax.ShapeDtypeStruct((dests, rows, chan), jnp.bfloat16),
        in_specs=[SMEM]
        + [VMEM] * (len(blocks) + 3)
        + [ANY] * len(after)
        + [VMEM] * last,
        out_specs=VMEM,
        scratch_shapes=[pltpu.VMEM((chan, 2 * width), jnp.bfloat16)],
        compiler_params=params(20 if dests <= FEW else 40),
        cost_estimate=takes(1),
        name="mlp_rows",
    )(place, *arrays)


def expand_kernel(start_ref, legendre_ref, spread_ref, out_ref):
    _, lats, degrees = legendre_ref.shape
    m = pl.program_id(0)
    degree = lax.broadcasted_iota(jnp.int32, (lats, degrees), 1)
    kept = jnp.where(degree >= start_ref[0] + m, legendre_ref[0].astype(jnp.float32), 0.0)
    wide = lax.dot_general(
        kept.astype(jnp.bfloat16),
        spread_ref[...],
        (((0,), (0,)), ((), ())),
        preferred_element_type=jnp.float32,
    )
    slot = lax.rem(lax.broadcasted_iota(jnp.int32, wide.shape, 1), SLOT)
    for r in range(2):
        out_ref[0, r] = jnp.where(slot == 2 * m + r, wide, 0.0).astype(jnp.bfloat16)


def expand(start, legendre, spread):
    modes, lats, degrees = legendre.shape
    depth = spread.shape[1]
    return pl.pallas_call(
        expand_kernel,
        out_shape=jax.ShapeDtypeStruct((modes, 2, degrees, depth), jnp.bfloat16),
        grid=(modes,),
        in_specs=[
            SMEM,
            pl.BlockSpec((1, lats, degrees), lambda m: (m, 0, 0)),
            pl.BlockSpec((lats, depth), lambda m: (0, 0)),
        ],
        out_specs=pl.BlockSpec((1, 2, degrees, depth), lambda m: (m, 0, 0, 0)),
        compiler_params=params(10 if depth <= 512 else 48),
        cost_estimate=takes(0.2),
        name="expand",
    )(start, legendre, spread)


def final_kernel(left_ref, spectrum_ref, out_ref, result_ref, sems):
    modes = left_ref.shape[0]
    chan = spectrum_ref.shape[1]
    copies = []
    for m in range(modes):
        for r in range(2):
            result_ref[m, :, r * chan : (r + 1) * chan] = jnp.dot(
                left_ref[m, r], spectrum_ref[...], preferred_element_type=jnp.float32
            ).astype(jnp.bfloat16)
        copies.append(pltpu.make_async_copy(result_ref.at[m], out_ref.at[m], sems.at[m]))
        copies[-1].start()
    for copy in copies:
        copy.wait()


def final_sum(left, spectrum):
    modes, _, degrees, depth = left.shape
    shape = (modes, degrees, 2 * spectrum.shape[1])
    return pl.pallas_call(
        final_kernel,
        out_shape=jax.ShapeDtypeStruct(shape, jnp.bfloat16),
        in_specs=[VMEM, VMEM],
        out_specs=HBM,
        scratch_shapes=[pltpu.VMEM(shape, jnp.bfloat16), pltpu.SemaphoreType.DMA((modes,))],
        compiler_params=params(8 if depth <= 512 else 48),
        cost_estimate=takes(1),
        name="final_sum",
    )(left, spectrum)


def fourier_blocks(lon, chunks, width, dests, mode_dev):
    chunk = lon // chunks
    index = np.arange(lon, dtype=np.int64)
    mode = np.arange(dests * mode_dev, dtype=np.int64)
    angle = ((mode[:, None] * index[None, :]) % lon) * (2.0 * math.pi / lon)
    paired = np.stack([np.cos(angle), -np.sin(angle)], axis=1) * math.sqrt(2.0 / lon)
    paired = paired.reshape(dests, 2 * mode_dev, chunks, chunk)
    table = np.zeros((chunks, dests, SLOT, width), np.float32)
    table[:, :, : 2 * mode_dev, :chunk] = np.transpose(paired, (2, 0, 1, 3))
    return table.reshape(chunks, dests * SLOT, width).astype(jnp.bfloat16)


def turn(block, axis, count, k):
    return lax.ppermute(block, axis, [(i, target(i, k, count)) for i in range(count)])


def scalar(value):
    return jnp.asarray(value, jnp.int32).reshape(1)


def on_device(
    fields,
    disco_weight,
    support_lat,
    support_lon,
    support_basis,
    support_value,
    w_up,
    w_down,
    legendre,
):
    lat_dev, lon, _ = fields.shape
    num_lat = lax.axis_size("lat")
    num_chan = lax.axis_size("chan")
    mode_dev, _, lats = legendre.shape
    dests = num_lat * num_chan
    width = ceil_to(lon // num_chan, LANES)
    band = lax.axis_index("lat")
    place = scalar(lax.axis_index("chan"))
    index = lax.axis_index(("lat", "chan"))
    supports = (support_lat, support_lon, support_basis, support_value)

    two_bands = num_lat == 2
    cells = jnp.swapaxes(fields, 1, 2)
    if two_bands:
        edge_out = lax.dynamic_slice_in_dim(cells, HALO * (1 - band), HALO, axis=0)
        edges = [None, lax.ppermute(edge_out, "lat", [(0, 1), (1, 0)])]
        pairs = [band, 1 - band]
    else:
        ends = num_lat - 1
        edges = [
            lax.ppermute(cells[lat_dev - HALO :], "lat", [(i, i + 1) for i in range(ends)]),
            lax.ppermute(cells[:HALO], "lat", [(i + 1, i) for i in range(ends)]),
        ]
        pairs = [0, 1]

    tables = jnp.asarray(fourier_blocks(lon, num_chan, width, dests, mode_dev))
    up = w_up.T
    down = w_down.T

    depth = dests * 4 * SLOT
    row = np.arange(depth)
    source_band = row // (4 * SLOT) // num_chan
    phase = (row // (2 * SLOT)) % 2
    source_pair = (phase ^ source_band) if two_bands else phase
    lat_of = lat_dev * source_band + 2 * source_pair + (row // SLOT) % 2
    spread = (lat_of[None, :] == np.arange(lats)[:, None]).astype(jnp.bfloat16)
    left = expand(scalar(index * mode_dev), jnp.swapaxes(legendre, 1, 2), jnp.asarray(spread))

    order = issue_order(num_chan)
    halves = [
        (scalar(pair), place, supports, cells, edge, disco_weight, num_chan)
        for edge, pair in zip(edges, pairs)
    ]
    received = []
    for half, edge in zip(halves, edges):
        sent = conv_rows(*half, order, received[0][:1] if received else [], edge is None)
        received.append([turn(block, "chan", num_chan, k) for k, block in zip(order, sent)])
    after = sent[-1:]
    for half, blocks in zip(halves, received):
        after = conv_rows(*half, (0,), after, False)
        blocks.insert(0, after[0])
    spectrum = None
    for blocks in received:
        spectrum = mlp_rows(place, blocks, up, down, tables, spectrum, dests, list(after))
        after = []

    both = ("lat", "chan")
    gathered = lax.all_to_all(spectrum, both, split_axis=0, concat_axis=0, tiled=True)
    return final_sum(left, gathered.reshape(depth, gathered.shape[2]))


def solution(mesh):
    in_specs = (
        P(("tm", "lat"), None, "chan"),
        P(None, "chan", None),
        P("lat", None),
        P("lat", None),
        P("lat", None),
        P("lat", None),
        P(),
        P(),
        P(("lat", "chan"), None, None),
    )
    out_specs = P(("tm", "lat", "chan"), None, None)
    return jax.shard_map(
        on_device, mesh=mesh, in_specs=in_specs, out_specs=out_specs, check_vma=False
    )
```

```python
import functools
import math

import jax
import jax.numpy as jnp
import numpy as np
from jax import lax
from jax.experimental import pallas as pl
from jax.experimental.pallas import tpu as pltpu
from jax.sharding import PartitionSpec as P

G = 64
S = 9
HALO = 2
DLON = 4
TAPS = S + 1
LANES = 128
SLOT = 8
EPS = 1e-05
FEW = 8
MIB = 1024 * 1024
FLOPS_PER_US = 1_000_000_000

SMEM = pl.BlockSpec(memory_space=pltpu.SMEM)
VMEM = pl.BlockSpec(memory_space=pltpu.VMEM)
ANY = pl.BlockSpec(memory_space=pl.ANY)
HBM = pl.BlockSpec(memory_space=pltpu.HBM)


def ceil_to(value, step):
    return -(-value // step) * step


def params(mib):
    return pltpu.CompilerParams(vmem_limit_bytes=mib * MIB)


def takes(micros):
    return pl.CostEstimate(flops=int(micros * FLOPS_PER_US), bytes_accessed=0, transcendentals=0)


def paired(count):
    return count & (count - 1) == 0


def target(place, k, count):
    return place ^ k if paired(count) else (place + k) % count


def source(place, k, count):
    return place ^ k if paired(count) else (place - k + count) % count


def issue_order(count):
    return [*range(2, count), 1] if paired(count) else list(range(1, count))


def conv_kernel(
    chunks, picks, has_edge, after, pair_ref, place_ref, lat_ref, lon_ref, basis_ref, value_ref, fields_ref, *rest
):
    if has_edge:
        edge_ref, weight_ref, *rest = rest
    else:
        edge_ref, (weight_ref, *rest) = None, rest
    *out_refs, rows_ref, taps_ref, filt_ref = rest[after:]
    own, _, lon = fields_ref.shape
    chunk = lon // chunks
    width = out_refs[0].shape[1]
    total = rows_ref.shape[2]
    pair = pair_ref[0]
    own_at = HALO * (1 - pair)
    edge_at = own * pair

    def put(slot, cells):
        rows_ref[slot, :, LANES : LANES + lon] = cells
        rows_ref[slot, :, 0:LANES] = cells[:, lon - LANES :]
        full = (lon // LANES) * LANES
        tail = total - LANES - lon
        rows_ref[slot, :, LANES + full :] = jnp.concatenate(
            [cells[:, full:], cells[:, :tail]], axis=1
        )

    for row in range(own):
        put(own_at + row, fields_ref[row])
    for row in range(HALO):
        if has_edge:
            put(edge_at + row, edge_ref[row])
        else:
            rows_ref[edge_at + row] = jnp.zeros(rows_ref.shape[1:], rows_ref.dtype)

    lane = lax.broadcasted_iota(jnp.int32, (G, LANES), 1)
    begins = [LANES + chunk * target(place_ref[0], k, chunks) for k in picks]

    def fill(slot, tap, source, offset):
        for k, origin in enumerate(begins):
            begin = origin + offset
            first = lax.div(begin, LANES)
            shift = lax.rem(begin, LANES)
            back = lax.rem(LANES - shift, LANES)
            keep = lane < LANES - shift
            turned = []
            for t in range(width // LANES + 1):
                start = pl.multiple_of((first + t) * LANES, LANES)
                tile = rows_ref[source, :, pl.ds(start, LANES)]
                turned.append(pltpu.roll(tile, back, 1))
            for t in range(width // LANES):
                at = k * width + t * LANES
                taps_ref[slot, tap * G : (tap + 1) * G, at : at + LANES] = jnp.where(
                    keep, turned[t], turned[t + 1]
                )

    eye = jnp.where(
        lax.broadcasted_iota(jnp.int32, (G, G), 0) == lax.broadcasted_iota(jnp.int32, (G, G), 1),
        1.0,
        0.0,
    ).astype(jnp.bfloat16)
    for i in range(2):
        row = 2 * pair + i
        pieces = []
        for tap in range(S):
            picked = weight_ref[basis_ref[row, tap]].astype(jnp.float32) * value_ref[row, tap]
            pieces.append(picked.astype(jnp.bfloat16))
        pieces.append(eye)
        for k in range(TAPS // 2):
            filt_ref[i, :, k * 2 * G : (k + 1) * 2 * G] = jnp.concatenate(
                [pieces[2 * k], pieces[2 * k + 1]], axis=1
            )
        for tap in range(S):
            fill(i, tap, HALO + i + lat_ref[row, tap], lon_ref[row, tap])
        fill(i, S, HALO + i, 0)
        mixed = jnp.dot(filt_ref[i], taps_ref[i], preferred_element_type=jnp.float32).astype(
            jnp.bfloat16
        )
        for k in range(len(picks)):
            out_refs[k][i * G : (i + 1) * G, :] = mixed[:, k * width : (k + 1) * width]


def conv_rows(pair, place, supports, fields, edge, weight, chunks, picks, after, roomy):
    own, chans, lon = fields.shape
    width = ceil_to(lon // chunks, LANES)
    highest = (LANES + lon - lon // chunks + DLON) // LANES
    total = (highest + 1) * LANES + width
    arrays = [fields] + ([] if edge is None else [edge]) + [weight]
    return pl.pallas_call(
        functools.partial(conv_kernel, chunks, picks, edge is not None, len(after)),
        out_shape=[jax.ShapeDtypeStruct((2 * chans, width), jnp.bfloat16)] * len(picks),
        in_specs=[SMEM] * 6 + [VMEM] * len(arrays) + [ANY] * len(after),
        out_specs=[VMEM] * len(picks),
        scratch_shapes=[
            pltpu.VMEM((own + HALO, chans, total), jnp.bfloat16),
            pltpu.VMEM((2, TAPS * G, len(picks) * width), jnp.bfloat16),
            pltpu.VMEM((2, G, TAPS * G), jnp.bfloat16),
        ],
        compiler_params=params(56 if roomy else 20),
        cost_estimate=takes(1 if len(picks) > 1 else 0.2),
        name="conv_rows",
    )(pair, place, *supports, *arrays, *after)


def mlp_kernel(parts, last, after, place_ref, *rest):
    blocks, rest = rest[:parts], rest[parts:]
    up_ref, down_ref, table_ref, *rest = rest
    rest = rest[after:]
    if last:
        earlier_ref, out_ref, cells_ref = rest
    else:
        out_ref, cells_ref = rest
    width = blocks[0].shape[1]
    place = place_ref[0]
    for block, k in zip(blocks, [0, *issue_order(parts)]):
        origin = pl.multiple_of(source(place, k, parts) * G, G)
        for i in range(2):
            cells_ref[pl.ds(origin, G), i * width : (i + 1) * width] = block[
                i * G : (i + 1) * G, :
            ]
    values = cells_ref[...].astype(jnp.float32)
    center = values - jnp.mean(values, axis=0, keepdims=True)
    spread = jnp.mean(center * center, axis=0, keepdims=True)
    normed = (center * lax.rsqrt(spread + EPS)).astype(jnp.bfloat16)
    lifted = jnp.dot(up_ref[...], normed, preferred_element_type=jnp.float32)
    scale = math.sqrt(2.0 / math.pi)
    inner = lifted * (scale + (scale * 0.044715) * (lifted * lifted))
    half = 0.5 * lifted
    active = (half + half * jnp.tanh(inner)).astype(jnp.bfloat16)
    lowered = jnp.dot(down_ref[...], active, preferred_element_type=jnp.float32)
    result = (values + lowered).astype(jnp.bfloat16)
    found = []
    for i in range(2):
        modes = lax.dot_general(
            table_ref[place],
            result[:, i * width : (i + 1) * width],
            (((1,), (1,)), ((), ())),
            preferred_element_type=jnp.float32,
        )
        found.append(modes.reshape(modes.shape[0] // SLOT, SLOT, modes.shape[1]))
    block = jnp.concatenate(found, axis=1).astype(jnp.bfloat16)
    if last:
        out_ref[:, 0 : 2 * SLOT, :] = earlier_ref[...]
        out_ref[:, 2 * SLOT : 4 * SLOT, :] = block
    else:
        out_ref[...] = block


def mlp_rows(place, blocks, up, down, tables, earlier, dests, after):
    pair_chans, width = blocks[0].shape
    chan = len(blocks) * pair_chans // 2
    last = earlier is not None
    arrays = [*blocks, up, down, tables, *after] + ([earlier] if last else [])
    rows = (4 if last else 2) * SLOT
    return pl.pallas_call(
        functools.partial(mlp_kernel, len(blocks), last, len(after)),
        out_shape=jax.ShapeDtypeStruct((dests, rows, chan), jnp.bfloat16),
        in_specs=[SMEM]
        + [VMEM] * (len(blocks) + 3)
        + [ANY] * len(after)
        + [VMEM] * last,
        out_specs=VMEM,
        scratch_shapes=[pltpu.VMEM((chan, 2 * width), jnp.bfloat16)],
        compiler_params=params(20 if dests <= FEW else 40),
        cost_estimate=takes(1),
        name="mlp_rows",
    )(place, *arrays)


def expand_kernel(start_ref, legendre_ref, spread_ref, out_ref):
    _, lats, degrees = legendre_ref.shape
    m = pl.program_id(0)
    degree = lax.broadcasted_iota(jnp.int32, (lats, degrees), 1)
    kept = jnp.where(degree >= start_ref[0] + m, legendre_ref[0].astype(jnp.float32), 0.0)
    wide = lax.dot_general(
        kept.astype(jnp.bfloat16),
        spread_ref[...],
        (((0,), (0,)), ((), ())),
        preferred_element_type=jnp.float32,
    )
    slot = lax.rem(lax.broadcasted_iota(jnp.int32, wide.shape, 1), SLOT)
    for r in range(2):
        out_ref[0, r] = jnp.where(slot == 2 * m + r, wide, 0.0).astype(jnp.bfloat16)


def expand(start, legendre, spread):
    modes, lats, degrees = legendre.shape
    depth = spread.shape[1]
    return pl.pallas_call(
        expand_kernel,
        out_shape=jax.ShapeDtypeStruct((modes, 2, degrees, depth), jnp.bfloat16),
        grid=(modes,),
        in_specs=[
            SMEM,
            pl.BlockSpec((1, lats, degrees), lambda m: (m, 0, 0)),
            pl.BlockSpec((lats, depth), lambda m: (0, 0)),
        ],
        out_specs=pl.BlockSpec((1, 2, degrees, depth), lambda m: (m, 0, 0, 0)),
        compiler_params=params(10 if depth <= 512 else 48),
        cost_estimate=takes(0.2),
        name="expand",
    )(start, legendre, spread)


def final_kernel(left_ref, spectrum_ref, out_ref, result_ref, sems):
    modes = left_ref.shape[0]
    chan = spectrum_ref.shape[1]
    copies = []
    for m in range(modes):
        for r in range(2):
            result_ref[m, :, r * chan : (r + 1) * chan] = jnp.dot(
                left_ref[m, r], spectrum_ref[...], preferred_element_type=jnp.float32
            ).astype(jnp.bfloat16)
        copies.append(pltpu.make_async_copy(result_ref.at[m], out_ref.at[m], sems.at[m]))
        copies[-1].start()
    for copy in copies:
        copy.wait()


def final_sum(left, spectrum):
    modes, _, degrees, depth = left.shape
    shape = (modes, degrees, 2 * spectrum.shape[1])
    return pl.pallas_call(
        final_kernel,
        out_shape=jax.ShapeDtypeStruct(shape, jnp.bfloat16),
        in_specs=[VMEM, VMEM],
        out_specs=HBM,
        scratch_shapes=[pltpu.VMEM(shape, jnp.bfloat16), pltpu.SemaphoreType.DMA((modes,))],
        compiler_params=params(8 if depth <= 512 else 48),
        cost_estimate=takes(1),
        name="final_sum",
    )(left, spectrum)


def fourier_blocks(lon, chunks, width, dests, mode_dev):
    chunk = lon // chunks
    index = np.arange(lon, dtype=np.int64)
    mode = np.arange(dests * mode_dev, dtype=np.int64)
    angle = ((mode[:, None] * index[None, :]) % lon) * (2.0 * math.pi / lon)
    paired = np.stack([np.cos(angle), -np.sin(angle)], axis=1) * math.sqrt(2.0 / lon)
    paired = paired.reshape(dests, 2 * mode_dev, chunks, chunk)
    table = np.zeros((chunks, dests, SLOT, width), np.float32)
    table[:, :, : 2 * mode_dev, :chunk] = np.transpose(paired, (2, 0, 1, 3))
    return table.reshape(chunks, dests * SLOT, width).astype(jnp.bfloat16)


def turn(block, axis, count, k):
    return lax.ppermute(block, axis, [(i, target(i, k, count)) for i in range(count)])


def scalar(value):
    return jnp.asarray(value, jnp.int32).reshape(1)


def on_device(
    fields,
    disco_weight,
    support_lat,
    support_lon,
    support_basis,
    support_value,
    w_up,
    w_down,
    legendre,
):
    lat_dev, lon, _ = fields.shape
    num_lat = lax.axis_size("lat")
    num_chan = lax.axis_size("chan")
    mode_dev, _, lats = legendre.shape
    dests = num_lat * num_chan
    width = ceil_to(lon // num_chan, LANES)
    band = lax.axis_index("lat")
    place = scalar(lax.axis_index("chan"))
    index = lax.axis_index(("lat", "chan"))
    supports = (support_lat, support_lon, support_basis, support_value)

    two_bands = num_lat == 2
    cells = jnp.swapaxes(fields, 1, 2)
    if two_bands:
        edge_out = lax.dynamic_slice_in_dim(cells, HALO * (1 - band), HALO, axis=0)
        edges = [None, lax.ppermute(edge_out, "lat", [(0, 1), (1, 0)])]
        pairs = [band, 1 - band]
    else:
        ends = num_lat - 1
        edges = [
            lax.ppermute(cells[lat_dev - HALO :], "lat", [(i, i + 1) for i in range(ends)]),
            lax.ppermute(cells[:HALO], "lat", [(i + 1, i) for i in range(ends)]),
        ]
        pairs = [0, 1]

    tables = jnp.asarray(fourier_blocks(lon, num_chan, width, dests, mode_dev))
    up = w_up.T
    down = w_down.T

    depth = dests * 4 * SLOT
    row = np.arange(depth)
    source_band = row // (4 * SLOT) // num_chan
    phase = (row // (2 * SLOT)) % 2
    source_pair = (phase ^ source_band) if two_bands else phase
    lat_of = lat_dev * source_band + 2 * source_pair + (row // SLOT) % 2
    spread = (lat_of[None, :] == np.arange(lats)[:, None]).astype(jnp.bfloat16)
    left = expand(scalar(index * mode_dev), jnp.swapaxes(legendre, 1, 2), jnp.asarray(spread))

    order = issue_order(num_chan)
    halves = [
        (scalar(pair), place, supports, cells, edge, disco_weight, num_chan)
        for edge, pair in zip(edges, pairs)
    ]
    received = []
    for half, edge in zip(halves, edges):
        sent = conv_rows(*half, order, [], edge is None)
        received.append([turn(block, "chan", num_chan, k) for k, block in zip(order, sent)])
    after = sent[1:2]
    for half, blocks in zip(halves, received):
        after = conv_rows(*half, (0,), after, False)
        blocks.insert(0, after[0])
    spectrum = None
    for blocks in received:
        spectrum = mlp_rows(place, blocks, up, down, tables, spectrum, dests, list(after))
        after = []

    both = ("lat", "chan")
    gathered = lax.all_to_all(spectrum, both, split_axis=0, concat_axis=0, tiled=True)
    return final_sum(left, gathered.reshape(depth, gathered.shape[2]))


def solution(mesh):
    in_specs = (
        P(("tm", "lat"), None, "chan"),
        P(None, "chan", None),
        P("lat", None),
        P("lat", None),
        P("lat", None),
        P("lat", None),
        P(),
        P(),
        P(("lat", "chan"), None, None),
    )
    out_specs = P(("tm", "lat", "chan"), None, None)
    return jax.shard_map(
        on_device, mesh=mesh, in_specs=in_specs, out_specs=out_specs, check_vma=False
    )
```

```python
import functools
import math

import jax
import jax.numpy as jnp
import numpy as np
from jax import lax
from jax.experimental import pallas as pl
from jax.experimental.pallas import tpu as pltpu
from jax.sharding import PartitionSpec as P

G = 64
S = 9
HALO = 2
DLON = 4
TAPS = S + 1
LANES = 128
SLOT = 8
EPS = 1e-05
FEW = 8
MIB = 1024 * 1024
FLOPS_PER_US = 1_000_000_000

SMEM = pl.BlockSpec(memory_space=pltpu.SMEM)
VMEM = pl.BlockSpec(memory_space=pltpu.VMEM)
ANY = pl.BlockSpec(memory_space=pl.ANY)
HBM = pl.BlockSpec(memory_space=pltpu.HBM)


def ceil_to(value, step):
    return -(-value // step) * step


def params(mib):
    return pltpu.CompilerParams(vmem_limit_bytes=mib * MIB)


def takes(micros):
    return pl.CostEstimate(flops=int(micros * FLOPS_PER_US), bytes_accessed=0, transcendentals=0)


def paired(count):
    return count & (count - 1) == 0


def target(place, k, count):
    return place ^ k if paired(count) else (place + k) % count


def source(place, k, count):
    return place ^ k if paired(count) else (place - k + count) % count


def issue_order(count):
    return [*range(2, count), 1] if paired(count) else list(range(1, count))


def conv_kernel(
    chunks, picks, has_edge, after, pair_ref, place_ref, lat_ref, lon_ref, basis_ref, value_ref, fields_ref, *rest
):
    if has_edge:
        edge_ref, weight_ref, *rest = rest
    else:
        edge_ref, (weight_ref, *rest) = None, rest
    *out_refs, rows_ref, taps_ref, filt_ref = rest[after:]
    own, _, lon = fields_ref.shape
    chunk = lon // chunks
    width = out_refs[0].shape[1]
    total = rows_ref.shape[2]
    pair = pair_ref[0]
    own_at = HALO * (1 - pair)
    edge_at = own * pair

    def put(slot, cells):
        rows_ref[slot, :, LANES : LANES + lon] = cells
        rows_ref[slot, :, 0:LANES] = cells[:, lon - LANES :]
        full = (lon // LANES) * LANES
        tail = total - LANES - lon
        rows_ref[slot, :, LANES + full :] = jnp.concatenate(
            [cells[:, full:], cells[:, :tail]], axis=1
        )

    for row in range(own):
        put(own_at + row, fields_ref[row])
    for row in range(HALO):
        if has_edge:
            put(edge_at + row, edge_ref[row])
        else:
            rows_ref[edge_at + row] = jnp.zeros(rows_ref.shape[1:], rows_ref.dtype)

    lane = lax.broadcasted_iota(jnp.int32, (G, LANES), 1)
    begins = [LANES + chunk * target(place_ref[0], k, chunks) for k in picks]

    def fill(slot, tap, source, offset):
        for k, origin in enumerate(begins):
            begin = origin + offset
            first = lax.div(begin, LANES)
            shift = lax.rem(begin, LANES)
            back = lax.rem(LANES - shift, LANES)
            keep = lane < LANES - shift
            turned = []
            for t in range(width // LANES + 1):
                start = pl.multiple_of((first + t) * LANES, LANES)
                tile = rows_ref[source, :, pl.ds(start, LANES)]
                turned.append(pltpu.roll(tile, back, 1))
            for t in range(width // LANES):
                at = k * width + t * LANES
                taps_ref[slot, tap * G : (tap + 1) * G, at : at + LANES] = jnp.where(
                    keep, turned[t], turned[t + 1]
                )

    eye = jnp.where(
        lax.broadcasted_iota(jnp.int32, (G, G), 0) == lax.broadcasted_iota(jnp.int32, (G, G), 1),
        1.0,
        0.0,
    ).astype(jnp.bfloat16)
    for i in range(2):
        row = 2 * pair + i
        pieces = []
        for tap in range(S):
            picked = weight_ref[basis_ref[row, tap]].astype(jnp.float32) * value_ref[row, tap]
            pieces.append(picked.astype(jnp.bfloat16))
        pieces.append(eye)
        for k in range(TAPS // 2):
            filt_ref[i, :, k * 2 * G : (k + 1) * 2 * G] = jnp.concatenate(
                [pieces[2 * k], pieces[2 * k + 1]], axis=1
            )
        for tap in range(S):
            fill(i, tap, HALO + i + lat_ref[row, tap], lon_ref[row, tap])
        fill(i, S, HALO + i, 0)
        mixed = jnp.dot(filt_ref[i], taps_ref[i], preferred_element_type=jnp.float32).astype(
            jnp.bfloat16
        )
        for k in range(len(picks)):
            out_refs[k][i * G : (i + 1) * G, :] = mixed[:, k * width : (k + 1) * width]


def conv_rows(pair, place, supports, fields, edge, weight, chunks, picks, after, roomy):
    own, chans, lon = fields.shape
    width = ceil_to(lon // chunks, LANES)
    highest = (LANES + lon - lon // chunks + DLON) // LANES
    total = (highest + 1) * LANES + width
    arrays = [fields] + ([] if edge is None else [edge]) + [weight]
    return pl.pallas_call(
        functools.partial(conv_kernel, chunks, picks, edge is not None, len(after)),
        out_shape=[jax.ShapeDtypeStruct((2 * chans, width), jnp.bfloat16)] * len(picks),
        in_specs=[SMEM] * 6 + [VMEM] * len(arrays) + [ANY] * len(after),
        out_specs=[VMEM] * len(picks),
        scratch_shapes=[
            pltpu.VMEM((own + HALO, chans, total), jnp.bfloat16),
            pltpu.VMEM((2, TAPS * G, len(picks) * width), jnp.bfloat16),
            pltpu.VMEM((2, G, TAPS * G), jnp.bfloat16),
        ],
        compiler_params=params(56 if roomy else 20),
        cost_estimate=takes(1 if len(picks) > 1 else 0.2),
        name="conv_rows",
    )(pair, place, *supports, *arrays, *after)


def mlp_kernel(parts, last, after, place_ref, *rest):
    blocks, rest = rest[:parts], rest[parts:]
    up_ref, down_ref, table_ref, *rest = rest
    rest = rest[after:]
    if last:
        earlier_ref, out_ref, cells_ref = rest
    else:
        out_ref, cells_ref = rest
    width = blocks[0].shape[1]
    place = place_ref[0]
    for block, k in zip(blocks, [0, *issue_order(parts)]):
        origin = pl.multiple_of(source(place, k, parts) * G, G)
        for i in range(2):
            cells_ref[pl.ds(origin, G), i * width : (i + 1) * width] = block[
                i * G : (i + 1) * G, :
            ]
    values = cells_ref[...].astype(jnp.float32)
    center = values - jnp.mean(values, axis=0, keepdims=True)
    spread = jnp.mean(center * center, axis=0, keepdims=True)
    normed = (center * lax.rsqrt(spread + EPS)).astype(jnp.bfloat16)
    lifted = jnp.dot(up_ref[...], normed, preferred_element_type=jnp.float32)
    scale = math.sqrt(2.0 / math.pi)
    inner = lifted * (scale + (scale * 0.044715) * (lifted * lifted))
    half = 0.5 * lifted
    active = (half + half * jnp.tanh(inner)).astype(jnp.bfloat16)
    lowered = jnp.dot(down_ref[...], active, preferred_element_type=jnp.float32)
    result = (values + lowered).astype(jnp.bfloat16)
    found = []
    for i in range(2):
        modes = lax.dot_general(
            table_ref[place],
            result[:, i * width : (i + 1) * width],
            (((1,), (1,)), ((), ())),
            preferred_element_type=jnp.float32,
        )
        found.append(modes.reshape(modes.shape[0] // SLOT, SLOT, modes.shape[1]))
    block = jnp.concatenate(found, axis=1).astype(jnp.bfloat16)
    if last:
        out_ref[:, 0 : 2 * SLOT, :] = earlier_ref[...]
        out_ref[:, 2 * SLOT : 4 * SLOT, :] = block
    else:
        out_ref[...] = block


def mlp_rows(place, blocks, up, down, tables, earlier, dests, after):
    pair_chans, width = blocks[0].shape
    chan = len(blocks) * pair_chans // 2
    last = earlier is not None
    arrays = [*blocks, up, down, tables, *after] + ([earlier] if last else [])
    rows = (4 if last else 2) * SLOT
    return pl.pallas_call(
        functools.partial(mlp_kernel, len(blocks), last, len(after)),
        out_shape=jax.ShapeDtypeStruct((dests, rows, chan), jnp.bfloat16),
        in_specs=[SMEM]
        + [VMEM] * (len(blocks) + 3)
        + [ANY] * len(after)
        + [VMEM] * last,
        out_specs=VMEM,
        scratch_shapes=[pltpu.VMEM((chan, 2 * width), jnp.bfloat16)],
        compiler_params=params(20 if dests <= FEW else 40),
        cost_estimate=takes(1),
        name="mlp_rows",
    )(place, *arrays)


def expand_kernel(start_ref, legendre_ref, spread_ref, out_ref):
    _, lats, degrees = legendre_ref.shape
    m = pl.program_id(0)
    degree = lax.broadcasted_iota(jnp.int32, (lats, degrees), 1)
    kept = jnp.where(degree >= start_ref[0] + m, legendre_ref[0].astype(jnp.float32), 0.0)
    wide = lax.dot_general(
        kept.astype(jnp.bfloat16),
        spread_ref[...],
        (((0,), (0,)), ((), ())),
        preferred_element_type=jnp.float32,
    )
    slot = lax.rem(lax.broadcasted_iota(jnp.int32, wide.shape, 1), SLOT)
    for r in range(2):
        out_ref[0, r] = jnp.where(slot == 2 * m + r, wide, 0.0).astype(jnp.bfloat16)


def expand(start, legendre, spread):
    modes, lats, degrees = legendre.shape
    depth = spread.shape[1]
    return pl.pallas_call(
        expand_kernel,
        out_shape=jax.ShapeDtypeStruct((modes, 2, degrees, depth), jnp.bfloat16),
        grid=(modes,),
        in_specs=[
            SMEM,
            pl.BlockSpec((1, lats, degrees), lambda m: (m, 0, 0)),
            pl.BlockSpec((lats, depth), lambda m: (0, 0)),
        ],
        out_specs=pl.BlockSpec((1, 2, degrees, depth), lambda m: (m, 0, 0, 0)),
        compiler_params=params(10 if depth <= 512 else 48),
        cost_estimate=takes(0.2),
        name="expand",
    )(start, legendre, spread)


def final_kernel(left_ref, spectrum_ref, out_ref, result_ref, sems):
    modes = left_ref.shape[0]
    chan = spectrum_ref.shape[1]
    copies = []
    for m in range(modes):
        for r in range(2):
            result_ref[m, :, r * chan : (r + 1) * chan] = jnp.dot(
                left_ref[m, r], spectrum_ref[...], preferred_element_type=jnp.float32
            ).astype(jnp.bfloat16)
        copies.append(pltpu.make_async_copy(result_ref.at[m], out_ref.at[m], sems.at[m]))
        copies[-1].start()
    for copy in copies:
        copy.wait()


def final_sum(left, spectrum):
    modes, _, degrees, depth = left.shape
    shape = (modes, degrees, 2 * spectrum.shape[1])
    return pl.pallas_call(
        final_kernel,
        out_shape=jax.ShapeDtypeStruct(shape, jnp.bfloat16),
        in_specs=[VMEM, VMEM],
        out_specs=HBM,
        scratch_shapes=[pltpu.VMEM(shape, jnp.bfloat16), pltpu.SemaphoreType.DMA((modes,))],
        compiler_params=params(8 if depth <= 512 else 48),
        cost_estimate=takes(1),
        name="final_sum",
    )(left, spectrum)


def fourier_blocks(lon, chunks, width, dests, mode_dev):
    chunk = lon // chunks
    index = np.arange(lon, dtype=np.int64)
    mode = np.arange(dests * mode_dev, dtype=np.int64)
    angle = ((mode[:, None] * index[None, :]) % lon) * (2.0 * math.pi / lon)
    paired = np.stack([np.cos(angle), -np.sin(angle)], axis=1) * math.sqrt(2.0 / lon)
    paired = paired.reshape(dests, 2 * mode_dev, chunks, chunk)
    table = np.zeros((chunks, dests, SLOT, width), np.float32)
    table[:, :, : 2 * mode_dev, :chunk] = np.transpose(paired, (2, 0, 1, 3))
    return table.reshape(chunks, dests * SLOT, width).astype(jnp.bfloat16)


def turn(block, axis, count, k):
    return lax.ppermute(block, axis, [(i, target(i, k, count)) for i in range(count)])


def scalar(value):
    return jnp.asarray(value, jnp.int32).reshape(1)


def on_device(
    fields,
    disco_weight,
    support_lat,
    support_lon,
    support_basis,
    support_value,
    w_up,
    w_down,
    legendre,
):
    lat_dev, lon, _ = fields.shape
    num_lat = lax.axis_size("lat")
    num_chan = lax.axis_size("chan")
    mode_dev, _, lats = legendre.shape
    dests = num_lat * num_chan
    width = ceil_to(lon // num_chan, LANES)
    band = lax.axis_index("lat")
    place = scalar(lax.axis_index("chan"))
    index = lax.axis_index(("lat", "chan"))
    supports = (support_lat, support_lon, support_basis, support_value)

    two_bands = num_lat == 2
    cells = jnp.swapaxes(fields, 1, 2)
    if two_bands:
        edge_out = lax.dynamic_slice_in_dim(cells, HALO * (1 - band), HALO, axis=0)
        edges = [None, lax.ppermute(edge_out, "lat", [(0, 1), (1, 0)])]
        pairs = [band, 1 - band]
    else:
        ends = num_lat - 1
        edges = [
            lax.ppermute(cells[lat_dev - HALO :], "lat", [(i, i + 1) for i in range(ends)]),
            lax.ppermute(cells[:HALO], "lat", [(i + 1, i) for i in range(ends)]),
        ]
        pairs = [0, 1]

    tables = jnp.asarray(fourier_blocks(lon, num_chan, width, dests, mode_dev))
    up = w_up.T
    down = w_down.T

    depth = dests * 4 * SLOT
    row = np.arange(depth)
    source_band = row // (4 * SLOT) // num_chan
    phase = (row // (2 * SLOT)) % 2
    source_pair = (phase ^ source_band) if two_bands else phase
    lat_of = lat_dev * source_band + 2 * source_pair + (row // SLOT) % 2
    spread = (lat_of[None, :] == np.arange(lats)[:, None]).astype(jnp.bfloat16)
    left = expand(scalar(index * mode_dev), jnp.swapaxes(legendre, 1, 2), jnp.asarray(spread))

    order = issue_order(num_chan)
    halves = [
        (scalar(pair), place, supports, cells, edge, disco_weight, num_chan)
        for edge, pair in zip(edges, pairs)
    ]
    received = []
    for half, edge in zip(halves, edges):
        if edge is None:
            sent = conv_rows(*half, order[:1], [], True)
            sent = [*sent, *conv_rows(*half, order[1:], sent, True)]
        else:
            sent = conv_rows(*half, order, [], False)
        received.append([turn(block, "chan", num_chan, k) for k, block in zip(order, sent)])
    after = sent[1:2]
    for half, blocks in zip(halves, received):
        after = conv_rows(*half, (0,), after, False)
        blocks.insert(0, after[0])
    spectrum = None
    for blocks in received:
        spectrum = mlp_rows(place, blocks, up, down, tables, spectrum, dests, list(after))
        after = []

    both = ("lat", "chan")
    gathered = lax.all_to_all(spectrum, both, split_axis=0, concat_axis=0, tiled=True)
    return final_sum(left, gathered.reshape(depth, gathered.shape[2]))


def solution(mesh):
    in_specs = (
        P(("tm", "lat"), None, "chan"),
        P(None, "chan", None),
        P("lat", None),
        P("lat", None),
        P("lat", None),
        P("lat", None),
        P(),
        P(),
        P(("lat", "chan"), None, None),
    )
    out_specs = P(("tm", "lat", "chan"), None, None)
    return jax.shard_map(
        on_device, mesh=mesh, in_specs=in_specs, out_specs=out_specs, check_vma=False
    )
```

```python
import functools
import math

import jax
import jax.numpy as jnp
import numpy as np
from jax import lax
from jax.experimental import pallas as pl
from jax.experimental.pallas import tpu as pltpu
from jax.sharding import PartitionSpec as P

G = 64
S = 9
HALO = 2
DLON = 4
TAPS = S + 1
LANES = 128
SLOT = 8
EPS = 1e-05
FEW = 8
MIB = 1024 * 1024
FLOPS_PER_US = 1_000_000_000

SMEM = pl.BlockSpec(memory_space=pltpu.SMEM)
VMEM = pl.BlockSpec(memory_space=pltpu.VMEM)
ANY = pl.BlockSpec(memory_space=pl.ANY)
HBM = pl.BlockSpec(memory_space=pltpu.HBM)


def ceil_to(value, step):
    return -(-value // step) * step


def params(mib):
    return pltpu.CompilerParams(vmem_limit_bytes=mib * MIB)


def takes(micros):
    return pl.CostEstimate(flops=int(micros * FLOPS_PER_US), bytes_accessed=0, transcendentals=0)


def paired(count):
    return count & (count - 1) == 0


def target(place, k, count):
    return place ^ k if paired(count) else (place + k) % count


def source(place, k, count):
    return place ^ k if paired(count) else (place - k + count) % count


def issue_order(count):
    return [*range(2, count), 1] if paired(count) else list(range(1, count))


def conv_kernel(
    chunks, picks, has_edge, after, pair_ref, place_ref, lat_ref, lon_ref, basis_ref, value_ref, fields_ref, *rest
):
    if has_edge:
        edge_ref, weight_ref, *rest = rest
    else:
        edge_ref, (weight_ref, *rest) = None, rest
    *out_refs, rows_ref, taps_ref, filt_ref = rest[after:]
    own, _, lon = fields_ref.shape
    chunk = lon // chunks
    width = out_refs[0].shape[1]
    total = rows_ref.shape[2]
    pair = pair_ref[0]
    own_at = HALO * (1 - pair)
    edge_at = own * pair

    def put(slot, cells):
        rows_ref[slot, :, LANES : LANES + lon] = cells
        rows_ref[slot, :, 0:LANES] = cells[:, lon - LANES :]
        full = (lon // LANES) * LANES
        tail = total - LANES - lon
        rows_ref[slot, :, LANES + full :] = jnp.concatenate(
            [cells[:, full:], cells[:, :tail]], axis=1
        )

    for row in range(own):
        put(own_at + row, fields_ref[row])
    for row in range(HALO):
        if has_edge:
            put(edge_at + row, edge_ref[row])
        else:
            rows_ref[edge_at + row] = jnp.zeros(rows_ref.shape[1:], rows_ref.dtype)

    lane = lax.broadcasted_iota(jnp.int32, (G, LANES), 1)
    begins = [LANES + chunk * target(place_ref[0], k, chunks) for k in picks]

    def fill(slot, tap, source, offset):
        for k, origin in enumerate(begins):
            begin = origin + offset
            first = lax.div(begin, LANES)
            shift = lax.rem(begin, LANES)
            back = lax.rem(LANES - shift, LANES)
            keep = lane < LANES - shift
            turned = []
            for t in range(width // LANES + 1):
                start = pl.multiple_of((first + t) * LANES, LANES)
                tile = rows_ref[source, :, pl.ds(start, LANES)]
                turned.append(pltpu.roll(tile, back, 1))
            for t in range(width // LANES):
                at = k * width + t * LANES
                taps_ref[slot, tap * G : (tap + 1) * G, at : at + LANES] = jnp.where(
                    keep, turned[t], turned[t + 1]
                )

    eye = jnp.where(
        lax.broadcasted_iota(jnp.int32, (G, G), 0) == lax.broadcasted_iota(jnp.int32, (G, G), 1),
        1.0,
        0.0,
    ).astype(jnp.bfloat16)
    for i in range(2):
        row = 2 * pair + i
        pieces = []
        for tap in range(S):
            picked = weight_ref[basis_ref[row, tap]].astype(jnp.float32) * value_ref[row, tap]
            pieces.append(picked.astype(jnp.bfloat16))
        pieces.append(eye)
        for k in range(TAPS // 2):
            filt_ref[i, :, k * 2 * G : (k + 1) * 2 * G] = jnp.concatenate(
                [pieces[2 * k], pieces[2 * k + 1]], axis=1
            )
        for tap in range(S):
            fill(i, tap, HALO + i + lat_ref[row, tap], lon_ref[row, tap])
        fill(i, S, HALO + i, 0)
        mixed = jnp.dot(filt_ref[i], taps_ref[i], preferred_element_type=jnp.float32).astype(
            jnp.bfloat16
        )
        for k in range(len(picks)):
            out_refs[k][i * G : (i + 1) * G, :] = mixed[:, k * width : (k + 1) * width]


def conv_rows(pair, place, supports, fields, edge, weight, chunks, picks, after, roomy):
    own, chans, lon = fields.shape
    width = ceil_to(lon // chunks, LANES)
    highest = (LANES + lon - lon // chunks + DLON) // LANES
    total = (highest + 1) * LANES + width
    arrays = [fields] + ([] if edge is None else [edge]) + [weight]
    return pl.pallas_call(
        functools.partial(conv_kernel, chunks, picks, edge is not None, len(after)),
        out_shape=[jax.ShapeDtypeStruct((2 * chans, width), jnp.bfloat16)] * len(picks),
        in_specs=[SMEM] * 6 + [VMEM] * len(arrays) + [ANY] * len(after),
        out_specs=[VMEM] * len(picks),
        scratch_shapes=[
            pltpu.VMEM((own + HALO, chans, total), jnp.bfloat16),
            pltpu.VMEM((2, TAPS * G, len(picks) * width), jnp.bfloat16),
            pltpu.VMEM((2, G, TAPS * G), jnp.bfloat16),
        ],
        compiler_params=params(56 if roomy else 20),
        cost_estimate=takes(1 if len(picks) > 1 else 0.2),
        name="conv_rows",
    )(pair, place, *supports, *arrays, *after)


def mlp_kernel(parts, last, after, place_ref, me_ref, *rest):
    blocks, rest = rest[:parts], rest[parts:]
    up_ref, down_ref, table_ref, *rest = rest
    rest = rest[after:]
    if last:
        earlier_ref, *out_refs, gather_ref, cells_ref = rest
    else:
        out_ref, cells_ref = rest
    width = blocks[0].shape[1]
    place = place_ref[0]
    for block, k in zip(blocks, [0, *issue_order(parts)]):
        origin = pl.multiple_of(source(place, k, parts) * G, G)
        for i in range(2):
            cells_ref[pl.ds(origin, G), i * width : (i + 1) * width] = block[
                i * G : (i + 1) * G, :
            ]
    values = cells_ref[...].astype(jnp.float32)
    center = values - jnp.mean(values, axis=0, keepdims=True)
    spread = jnp.mean(center * center, axis=0, keepdims=True)
    normed = (center * lax.rsqrt(spread + EPS)).astype(jnp.bfloat16)
    lifted = jnp.dot(up_ref[...], normed, preferred_element_type=jnp.float32)
    scale = math.sqrt(2.0 / math.pi)
    inner = lifted * (scale + (scale * 0.044715) * (lifted * lifted))
    half = 0.5 * lifted
    active = (half + half * jnp.tanh(inner)).astype(jnp.bfloat16)
    lowered = jnp.dot(down_ref[...], active, preferred_element_type=jnp.float32)
    result = (values + lowered).astype(jnp.bfloat16)
    found = []
    for i in range(2):
        modes = lax.dot_general(
            table_ref[place],
            result[:, i * width : (i + 1) * width],
            (((1,), (1,)), ((), ())),
            preferred_element_type=jnp.float32,
        )
        found.append(modes.reshape(modes.shape[0] // SLOT, SLOT, modes.shape[1]))
    block = jnp.concatenate(found, axis=1).astype(jnp.bfloat16)
    if not last:
        out_ref[...] = block
        return
    gather_ref[:, 0 : 2 * SLOT, :] = earlier_ref[...]
    gather_ref[:, 2 * SLOT : 4 * SLOT, :] = block
    if len(out_refs) == 1:
        out_refs[0][...] = gather_ref[...]
        return
    for out_ref, k in zip(out_refs, [0, *issue_order(len(out_refs))]):
        out_ref[...] = gather_ref[target(me_ref[0], k, len(out_refs))]


def mlp_rows(place, me, blocks, up, down, tables, earlier, dests, after):
    pair_chans, width = blocks[0].shape
    chan = len(blocks) * pair_chans // 2
    last = earlier is not None
    arrays = [*blocks, up, down, tables, *after] + ([earlier] if last else [])
    shape = (dests, (4 if last else 2) * SLOT, chan)
    outs = jax.ShapeDtypeStruct(shape, jnp.bfloat16)
    out_specs = VMEM
    if last:
        count = dests if dests <= FEW else 1
        split = shape if count == 1 else shape[1:]
        outs = [jax.ShapeDtypeStruct(split, jnp.bfloat16)] * count
        out_specs = [VMEM] * count
    return pl.pallas_call(
        functools.partial(mlp_kernel, len(blocks), last, len(after)),
        out_shape=outs,
        in_specs=[SMEM] * 2
        + [VMEM] * (len(blocks) + 3)
        + [ANY] * len(after)
        + [VMEM] * last,
        out_specs=out_specs,
        scratch_shapes=[pltpu.VMEM(shape, jnp.bfloat16)] * last
        + [pltpu.VMEM((chan, 2 * width), jnp.bfloat16)],
        compiler_params=params(20 if dests <= FEW else 40),
        cost_estimate=takes(1),
        name="mlp_rows",
    )(place, me, *arrays)


def expand_kernel(start_ref, legendre_ref, spread_ref, out_ref):
    _, lats, degrees = legendre_ref.shape
    m = pl.program_id(0)
    degree = lax.broadcasted_iota(jnp.int32, (lats, degrees), 1)
    kept = jnp.where(degree >= start_ref[0] + m, legendre_ref[0].astype(jnp.float32), 0.0)
    wide = lax.dot_general(
        kept.astype(jnp.bfloat16),
        spread_ref[...],
        (((0,), (0,)), ((), ())),
        preferred_element_type=jnp.float32,
    )
    slot = lax.rem(lax.broadcasted_iota(jnp.int32, wide.shape, 1), SLOT)
    for r in range(2):
        out_ref[0, r] = jnp.where(slot == 2 * m + r, wide, 0.0).astype(jnp.bfloat16)


def expand(start, legendre, spread):
    modes, lats, degrees = legendre.shape
    depth = spread.shape[1]
    return pl.pallas_call(
        expand_kernel,
        out_shape=jax.ShapeDtypeStruct((modes, 2, degrees, depth), jnp.bfloat16),
        grid=(modes,),
        in_specs=[
            SMEM,
            pl.BlockSpec((1, lats, degrees), lambda m: (m, 0, 0)),
            pl.BlockSpec((lats, depth), lambda m: (0, 0)),
        ],
        out_specs=pl.BlockSpec((1, 2, degrees, depth), lambda m: (m, 0, 0, 0)),
        compiler_params=params(10 if depth <= 512 else 48),
        cost_estimate=takes(0.2),
        name="expand",
    )(start, legendre, spread)


def final_kernel(me_ref, left_ref, *rest):
    *blocks, out_ref, spectrum_ref, result_ref, sems = rest
    modes = left_ref.shape[0]
    depth, chan = spectrum_ref.shape
    count = len(blocks)
    rows = depth // count
    order = [0, *issue_order(count)] if count > 1 else [0]
    for block, k in zip(blocks, order):
        origin = source(me_ref[0], k, count) * rows if count > 1 else 0
        spectrum_ref[pl.ds(pl.multiple_of(origin, rows), rows), :] = block[...]
    copies = []
    for m in range(modes):
        for r in range(2):
            result_ref[m, :, r * chan : (r + 1) * chan] = jnp.dot(
                left_ref[m, r], spectrum_ref[...], preferred_element_type=jnp.float32
            ).astype(jnp.bfloat16)
        copies.append(pltpu.make_async_copy(result_ref.at[m], out_ref.at[m], sems.at[m]))
        copies[-1].start()
    for copy in copies:
        copy.wait()


def final_sum(me, left, blocks):
    modes, _, degrees, depth = left.shape
    chan = blocks[0].shape[1]
    shape = (modes, degrees, 2 * chan)
    return pl.pallas_call(
        final_kernel,
        out_shape=jax.ShapeDtypeStruct(shape, jnp.bfloat16),
        in_specs=[SMEM] + [VMEM] * (1 + len(blocks)),
        out_specs=HBM,
        scratch_shapes=[
            pltpu.VMEM((depth, chan), jnp.bfloat16),
            pltpu.VMEM(shape, jnp.bfloat16),
            pltpu.SemaphoreType.DMA((modes,)),
        ],
        compiler_params=params(8 if depth <= 512 else 48),
        cost_estimate=takes(1),
        name="final_sum",
    )(me, left, *blocks)


def fourier_blocks(lon, chunks, width, dests, mode_dev):
    chunk = lon // chunks
    index = np.arange(lon, dtype=np.int64)
    mode = np.arange(dests * mode_dev, dtype=np.int64)
    angle = ((mode[:, None] * index[None, :]) % lon) * (2.0 * math.pi / lon)
    paired = np.stack([np.cos(angle), -np.sin(angle)], axis=1) * math.sqrt(2.0 / lon)
    paired = paired.reshape(dests, 2 * mode_dev, chunks, chunk)
    table = np.zeros((chunks, dests, SLOT, width), np.float32)
    table[:, :, : 2 * mode_dev, :chunk] = np.transpose(paired, (2, 0, 1, 3))
    return table.reshape(chunks, dests * SLOT, width).astype(jnp.bfloat16)


def turn(block, axis, count, k):
    return lax.ppermute(block, axis, [(i, target(i, k, count)) for i in range(count)])


def scalar(value):
    return jnp.asarray(value, jnp.int32).reshape(1)


def on_device(
    fields,
    disco_weight,
    support_lat,
    support_lon,
    support_basis,
    support_value,
    w_up,
    w_down,
    legendre,
):
    lat_dev, lon, _ = fields.shape
    num_lat = lax.axis_size("lat")
    num_chan = lax.axis_size("chan")
    mode_dev, _, lats = legendre.shape
    dests = num_lat * num_chan
    width = ceil_to(lon // num_chan, LANES)
    band = lax.axis_index("lat")
    place = scalar(lax.axis_index("chan"))
    index = lax.axis_index(("lat", "chan"))
    me = scalar(index)
    supports = (support_lat, support_lon, support_basis, support_value)

    two_bands = num_lat == 2
    cells = jnp.swapaxes(fields, 1, 2)
    if two_bands:
        edge_out = lax.dynamic_slice_in_dim(cells, HALO * (1 - band), HALO, axis=0)
        edges = [None, lax.ppermute(edge_out, "lat", [(0, 1), (1, 0)])]
        pairs = [band, 1 - band]
    else:
        ends = num_lat - 1
        edges = [
            lax.ppermute(cells[lat_dev - HALO :], "lat", [(i, i + 1) for i in range(ends)]),
            lax.ppermute(cells[:HALO], "lat", [(i + 1, i) for i in range(ends)]),
        ]
        pairs = [0, 1]

    tables = jnp.asarray(fourier_blocks(lon, num_chan, width, dests, mode_dev))
    up = w_up.T
    down = w_down.T

    depth = dests * 4 * SLOT
    row = np.arange(depth)
    source_band = row // (4 * SLOT) // num_chan
    phase = (row // (2 * SLOT)) % 2
    source_pair = (phase ^ source_band) if two_bands else phase
    lat_of = lat_dev * source_band + 2 * source_pair + (row // SLOT) % 2
    spread = (lat_of[None, :] == np.arange(lats)[:, None]).astype(jnp.bfloat16)
    left = expand(scalar(index * mode_dev), jnp.swapaxes(legendre, 1, 2), jnp.asarray(spread))

    order = issue_order(num_chan)
    halves = [
        (scalar(pair), place, supports, cells, edge, disco_weight, num_chan)
        for edge, pair in zip(edges, pairs)
    ]
    received = []
    for half, edge in zip(halves, edges):
        sent = conv_rows(*half, order, [], edge is None)
        received.append([turn(block, "chan", num_chan, k) for k, block in zip(order, sent)])
    after = sent[1:2]
    for half, blocks in zip(halves, received):
        after = conv_rows(*half, (0,), after, False)
        blocks.insert(0, after[0])
    spectrum = None
    after = [*after, left]
    for blocks in received:
        spectrum = mlp_rows(place, me, blocks, up, down, tables, spectrum, dests, after)
        after = []

    both = ("lat", "chan")
    if dests <= FEW:
        blocks = [spectrum[0]] + [
            turn(block, both, dests, k) for k, block in zip(issue_order(dests), spectrum[1:])
        ]
    else:
        whole = lax.all_to_all(spectrum[0], both, split_axis=0, concat_axis=0, tiled=True)
        blocks = [whole.reshape(depth, whole.shape[2])]
    return final_sum(me, left, blocks)


def solution(mesh):
    in_specs = (
        P(("tm", "lat"), None, "chan"),
        P(None, "chan", None),
        P("lat", None),
        P("lat", None),
        P("lat", None),
        P("lat", None),
        P(),
        P(),
        P(("lat", "chan"), None, None),
    )
    out_specs = P(("tm", "lat", "chan"), None, None)
    return jax.shard_map(
        on_device, mesh=mesh, in_specs=in_specs, out_specs=out_specs, check_vma=False
    )
```

```python
import functools
import math

import jax
import jax.numpy as jnp
import numpy as np
from jax import lax
from jax.experimental import pallas as pl
from jax.experimental.pallas import tpu as pltpu
from jax.sharding import PartitionSpec as P

G = 64
S = 9
HALO = 2
DLON = 4
TAPS = S + 1
LANES = 128
SLOT = 8
EPS = 1e-05
FEW = 8
MIB = 1024 * 1024
FLOPS_PER_US = 1_000_000_000

SMEM = pl.BlockSpec(memory_space=pltpu.SMEM)
VMEM = pl.BlockSpec(memory_space=pltpu.VMEM)
ANY = pl.BlockSpec(memory_space=pl.ANY)
HBM = pl.BlockSpec(memory_space=pltpu.HBM)


def ceil_to(value, step):
    return -(-value // step) * step


def params(mib):
    return pltpu.CompilerParams(vmem_limit_bytes=mib * MIB)


def takes(micros):
    return pl.CostEstimate(flops=int(micros * FLOPS_PER_US), bytes_accessed=0, transcendentals=0)


def paired(count):
    return count & (count - 1) == 0


def target(place, k, count):
    return place ^ k if paired(count) else (place + k) % count


def source(place, k, count):
    return place ^ k if paired(count) else (place - k + count) % count


def issue_order(count):
    return [*range(2, count), 1] if paired(count) else list(range(1, count))


def conv_kernel(
    chunks, picks, has_edge, after, flip, lat_ref, lon_ref, basis_ref, value_ref, fields_ref, *rest
):
    if has_edge:
        edge_ref, weight_ref, *rest = rest
    else:
        edge_ref, (weight_ref, *rest) = None, rest
    *out_refs, rows_ref, taps_ref, filt_ref = rest[after:]
    own, _, lon = fields_ref.shape
    chunk = lon // chunks
    width = out_refs[0].shape[1]
    total = rows_ref.shape[2]
    pair = flip if isinstance(flip, int) else flip()
    own_at = HALO * (1 - pair)
    edge_at = own * pair

    def put(slot, cells):
        rows_ref[slot, :, LANES : LANES + lon] = cells
        rows_ref[slot, :, 0:LANES] = cells[:, lon - LANES :]
        full = (lon // LANES) * LANES
        tail = total - LANES - lon
        rows_ref[slot, :, LANES + full :] = jnp.concatenate(
            [cells[:, full:], cells[:, :tail]], axis=1
        )

    for row in range(own):
        put(own_at + row, fields_ref[row])
    for row in range(HALO):
        if has_edge:
            put(edge_at + row, edge_ref[row])
        else:
            rows_ref[edge_at + row] = jnp.zeros(rows_ref.shape[1:], rows_ref.dtype)

    lane = lax.broadcasted_iota(jnp.int32, (G, LANES), 1)
    begins = [LANES + chunk * target(lax.axis_index("chan"), k, chunks) for k in picks]

    def fill(slot, tap, source, offset):
        for k, origin in enumerate(begins):
            begin = origin + offset
            first = lax.div(begin, LANES)
            shift = lax.rem(begin, LANES)
            back = lax.rem(LANES - shift, LANES)
            keep = lane < LANES - shift
            turned = []
            for t in range(width // LANES + 1):
                start = pl.multiple_of((first + t) * LANES, LANES)
                tile = rows_ref[source, :, pl.ds(start, LANES)]
                turned.append(pltpu.roll(tile, back, 1))
            for t in range(width // LANES):
                at = k * width + t * LANES
                taps_ref[slot, tap * G : (tap + 1) * G, at : at + LANES] = jnp.where(
                    keep, turned[t], turned[t + 1]
                )

    eye = jnp.where(
        lax.broadcasted_iota(jnp.int32, (G, G), 0) == lax.broadcasted_iota(jnp.int32, (G, G), 1),
        1.0,
        0.0,
    ).astype(jnp.bfloat16)
    for i in range(2):
        row = 2 * pair + i
        pieces = []
        for tap in range(S):
            picked = weight_ref[basis_ref[row, tap]].astype(jnp.float32) * value_ref[row, tap]
            pieces.append(picked.astype(jnp.bfloat16))
        pieces.append(eye)
        for k in range(TAPS // 2):
            filt_ref[i, :, k * 2 * G : (k + 1) * 2 * G] = jnp.concatenate(
                [pieces[2 * k], pieces[2 * k + 1]], axis=1
            )
        for tap in range(S):
            fill(i, tap, HALO + i + lat_ref[row, tap], lon_ref[row, tap])
        fill(i, S, HALO + i, 0)
        mixed = jnp.dot(filt_ref[i], taps_ref[i], preferred_element_type=jnp.float32).astype(
            jnp.bfloat16
        )
        for k in range(len(picks)):
            out_refs[k][i * G : (i + 1) * G, :] = mixed[:, k * width : (k + 1) * width]


def conv_rows(pair, supports, fields, edge, weight, chunks, picks, after, roomy):
    own, chans, lon = fields.shape
    width = ceil_to(lon // chunks, LANES)
    highest = (LANES + lon - lon // chunks + DLON) // LANES
    total = (highest + 1) * LANES + width
    arrays = [fields] + ([] if edge is None else [edge]) + [weight]
    return pl.pallas_call(
        functools.partial(conv_kernel, chunks, picks, edge is not None, len(after), pair),
        out_shape=[jax.ShapeDtypeStruct((2 * chans, width), jnp.bfloat16)] * len(picks),
        in_specs=[SMEM] * 4 + [VMEM] * len(arrays) + [ANY] * len(after),
        out_specs=[VMEM] * len(picks),
        scratch_shapes=[
            pltpu.VMEM((own + HALO, chans, total), jnp.bfloat16),
            pltpu.VMEM((2, TAPS * G, len(picks) * width), jnp.bfloat16),
            pltpu.VMEM((2, G, TAPS * G), jnp.bfloat16),
        ],
        compiler_params=params(56 if roomy else 20),
        cost_estimate=takes(1 if len(picks) > 1 else 0.2),
        name="conv_rows",
    )(*supports, *arrays, *after)


def mlp_kernel(parts, last, after, *rest):
    blocks, rest = rest[:parts], rest[parts:]
    up_ref, down_ref, table_ref, *rest = rest
    rest = rest[after:]
    if last:
        earlier_ref, out_ref, cells_ref = rest
    else:
        out_ref, cells_ref = rest
    width = blocks[0].shape[1]
    place = lax.axis_index("chan")
    for block, k in zip(blocks, [0, *issue_order(parts)]):
        origin = pl.multiple_of(source(place, k, parts) * G, G)
        for i in range(2):
            cells_ref[pl.ds(origin, G), i * width : (i + 1) * width] = block[
                i * G : (i + 1) * G, :
            ]
    values = cells_ref[...].astype(jnp.float32)
    center = values - jnp.mean(values, axis=0, keepdims=True)
    spread = jnp.mean(center * center, axis=0, keepdims=True)
    normed = (center * lax.rsqrt(spread + EPS)).astype(jnp.bfloat16)
    lifted = jnp.dot(up_ref[...], normed, preferred_element_type=jnp.float32)
    scale = math.sqrt(2.0 / math.pi)
    inner = lifted * (scale + (scale * 0.044715) * (lifted * lifted))
    half = 0.5 * lifted
    active = (half + half * jnp.tanh(inner)).astype(jnp.bfloat16)
    lowered = jnp.dot(down_ref[...], active, preferred_element_type=jnp.float32)
    result = (values + lowered).astype(jnp.bfloat16)
    found = []
    for i in range(2):
        modes = lax.dot_general(
            table_ref[place],
            result[:, i * width : (i + 1) * width],
            (((1,), (1,)), ((), ())),
            preferred_element_type=jnp.float32,
        )
        found.append(modes.reshape(modes.shape[0] // SLOT, SLOT, modes.shape[1]))
    block = jnp.concatenate(found, axis=1).astype(jnp.bfloat16)
    if last:
        out_ref[:, 0 : 2 * SLOT, :] = earlier_ref[...]
        out_ref[:, 2 * SLOT : 4 * SLOT, :] = block
    else:
        out_ref[...] = block


def mlp_rows(blocks, up, down, tables, earlier, dests, after):
    pair_chans, width = blocks[0].shape
    chan = len(blocks) * pair_chans // 2
    last = earlier is not None
    arrays = [*blocks, up, down, tables, *after] + ([earlier] if last else [])
    rows = (4 if last else 2) * SLOT
    return pl.pallas_call(
        functools.partial(mlp_kernel, len(blocks), last, len(after)),
        out_shape=jax.ShapeDtypeStruct((dests, rows, chan), jnp.bfloat16),
        in_specs=[VMEM] * (len(blocks) + 3)
        + [ANY] * len(after)
        + [VMEM] * last,
        out_specs=VMEM,
        scratch_shapes=[pltpu.VMEM((chan, 2 * width), jnp.bfloat16)],
        compiler_params=params(20 if dests <= FEW else 40),
        cost_estimate=takes(1),
        name="mlp_rows",
    )(*arrays)


def expand_kernel(legendre_ref, spread_ref, out_ref):
    _, lats, degrees = legendre_ref.shape
    m = pl.program_id(0)
    first = lax.axis_index(("lat", "chan")) * pl.num_programs(0)
    degree = lax.broadcasted_iota(jnp.int32, (lats, degrees), 1)
    kept = jnp.where(degree >= first + m, legendre_ref[0].astype(jnp.float32), 0.0)
    wide = lax.dot_general(
        kept.astype(jnp.bfloat16),
        spread_ref[...],
        (((0,), (0,)), ((), ())),
        preferred_element_type=jnp.float32,
    )
    slot = lax.rem(lax.broadcasted_iota(jnp.int32, wide.shape, 1), SLOT)
    for r in range(2):
        out_ref[0, r] = jnp.where(slot == 2 * m + r, wide, 0.0).astype(jnp.bfloat16)


def expand(legendre, spread):
    modes, lats, degrees = legendre.shape
    depth = spread.shape[1]
    return pl.pallas_call(
        expand_kernel,
        out_shape=jax.ShapeDtypeStruct((modes, 2, degrees, depth), jnp.bfloat16),
        grid=(modes,),
        in_specs=[
            pl.BlockSpec((1, lats, degrees), lambda m: (m, 0, 0)),
            pl.BlockSpec((lats, depth), lambda m: (0, 0)),
        ],
        out_specs=pl.BlockSpec((1, 2, degrees, depth), lambda m: (m, 0, 0, 0)),
        compiler_params=params(10 if depth <= 512 else 48),
        cost_estimate=takes(0.2),
        name="expand",
    )(legendre, spread)


def final_kernel(left_ref, spectrum_ref, out_ref, result_ref, sems):
    modes = left_ref.shape[0]
    chan = spectrum_ref.shape[1]
    copies = []
    for m in range(modes):
        for r in range(2):
            result_ref[m, :, r * chan : (r + 1) * chan] = jnp.dot(
                left_ref[m, r], spectrum_ref[...], preferred_element_type=jnp.float32
            ).astype(jnp.bfloat16)
        copies.append(pltpu.make_async_copy(result_ref.at[m], out_ref.at[m], sems.at[m]))
        copies[-1].start()
    for copy in copies:
        copy.wait()


def final_sum(left, spectrum):
    modes, _, degrees, depth = left.shape
    shape = (modes, degrees, 2 * spectrum.shape[1])
    return pl.pallas_call(
        final_kernel,
        out_shape=jax.ShapeDtypeStruct(shape, jnp.bfloat16),
        in_specs=[VMEM, VMEM],
        out_specs=HBM,
        scratch_shapes=[pltpu.VMEM(shape, jnp.bfloat16), pltpu.SemaphoreType.DMA((modes,))],
        compiler_params=params(8 if depth <= 512 else 48),
        cost_estimate=takes(1),
        name="final_sum",
    )(left, spectrum)


def fourier_blocks(lon, chunks, width, dests, mode_dev):
    chunk = lon // chunks
    index = np.arange(lon, dtype=np.int64)
    mode = np.arange(dests * mode_dev, dtype=np.int64)
    angle = ((mode[:, None] * index[None, :]) % lon) * (2.0 * math.pi / lon)
    paired = np.stack([np.cos(angle), -np.sin(angle)], axis=1) * math.sqrt(2.0 / lon)
    paired = paired.reshape(dests, 2 * mode_dev, chunks, chunk)
    table = np.zeros((chunks, dests, SLOT, width), np.float32)
    table[:, :, : 2 * mode_dev, :chunk] = np.transpose(paired, (2, 0, 1, 3))
    return table.reshape(chunks, dests * SLOT, width).astype(jnp.bfloat16)


def turn(block, axis, count, k):
    return lax.ppermute(block, axis, [(i, target(i, k, count)) for i in range(count)])


def on_device(
    fields,
    disco_weight,
    support_lat,
    support_lon,
    support_basis,
    support_value,
    w_up,
    w_down,
    legendre,
):
    lat_dev, lon, _ = fields.shape
    num_lat = lax.axis_size("lat")
    num_chan = lax.axis_size("chan")
    mode_dev, _, lats = legendre.shape
    dests = num_lat * num_chan
    width = ceil_to(lon // num_chan, LANES)
    band = lax.axis_index("lat")
    supports = (support_lat, support_lon, support_basis, support_value)

    two_bands = num_lat == 2
    cells = jnp.swapaxes(fields, 1, 2)
    if two_bands:
        edge_out = lax.dynamic_slice_in_dim(cells, HALO * (1 - band), HALO, axis=0)
        edges = [None, lax.ppermute(edge_out, "lat", [(0, 1), (1, 0)])]
        pairs = [lambda: lax.axis_index("lat"), lambda: 1 - lax.axis_index("lat")]
    else:
        ends = num_lat - 1
        edges = [
            lax.ppermute(cells[lat_dev - HALO :], "lat", [(i, i + 1) for i in range(ends)]),
            lax.ppermute(cells[:HALO], "lat", [(i + 1, i) for i in range(ends)]),
        ]
        pairs = [0, 1]

    tables = jnp.asarray(fourier_blocks(lon, num_chan, width, dests, mode_dev))
    up = w_up.T
    down = w_down.T

    depth = dests * 4 * SLOT
    row = np.arange(depth)
    source_band = row // (4 * SLOT) // num_chan
    phase = (row // (2 * SLOT)) % 2
    source_pair = (phase ^ source_band) if two_bands else phase
    lat_of = lat_dev * source_band + 2 * source_pair + (row // SLOT) % 2
    spread = (lat_of[None, :] == np.arange(lats)[:, None]).astype(jnp.bfloat16)
    left = expand(jnp.swapaxes(legendre, 1, 2), jnp.asarray(spread))

    order = issue_order(num_chan)
    halves = [
        (pair, supports, cells, edge, disco_weight, num_chan)
        for edge, pair in zip(edges, pairs)
    ]
    received = []
    for half, edge in zip(halves, edges):
        sent = conv_rows(*half, order, [], edge is None)
        received.append([turn(block, "chan", num_chan, k) for k, block in zip(order, sent)])
    after = sent[1:2]
    for half, blocks in zip(halves, received):
        after = conv_rows(*half, (0,), after, False)
        blocks.insert(0, after[0])
    spectrum = None
    for blocks in received:
        spectrum = mlp_rows(blocks, up, down, tables, spectrum, dests, list(after))
        after = []

    both = ("lat", "chan")
    gathered = lax.all_to_all(spectrum, both, split_axis=0, concat_axis=0, tiled=True)
    return final_sum(left, gathered.reshape(depth, gathered.shape[2]))


def solution(mesh):
    in_specs = (
        P(("tm", "lat"), None, "chan"),
        P(None, "chan", None),
        P("lat", None),
        P("lat", None),
        P("lat", None),
        P("lat", None),
        P(),
        P(),
        P(("lat", "chan"), None, None),
    )
    out_specs = P(("tm", "lat", "chan"), None, None)
    return jax.shard_map(
        on_device, mesh=mesh, in_specs=in_specs, out_specs=out_specs, check_vma=False
    )
```

```python
import functools
import math

import jax
import jax.numpy as jnp
import numpy as np
from jax import lax
from jax.experimental import pallas as pl
from jax.experimental.pallas import tpu as pltpu
from jax.sharding import PartitionSpec as P

G = 64
S = 9
HALO = 2
DLON = 4
TAPS = S + 1
LANES = 128
SLOT = 8
EPS = 1e-05
FEW = 8
MIB = 1024 * 1024
FLOPS_PER_US = 1_000_000_000

SMEM = pl.BlockSpec(memory_space=pltpu.SMEM)
VMEM = pl.BlockSpec(memory_space=pltpu.VMEM)
ANY = pl.BlockSpec(memory_space=pl.ANY)
HBM = pl.BlockSpec(memory_space=pltpu.HBM)


def ceil_to(value, step):
    return -(-value // step) * step


def params(mib):
    return pltpu.CompilerParams(vmem_limit_bytes=mib * MIB)


def takes(micros):
    return pl.CostEstimate(flops=int(micros * FLOPS_PER_US), bytes_accessed=0, transcendentals=0)


def target(place, k, count):
    return lax.rem(place + k, count)


def source(place, k, count):
    return lax.rem(place - k + count, count)


def conv_kernel(
    chunks, picks, has_edge, after, flip, lat_ref, lon_ref, basis_ref, value_ref, fields_ref, *rest
):
    if has_edge:
        edge_ref, weight_ref, *rest = rest
    else:
        edge_ref, (weight_ref, *rest) = None, rest
    *out_refs, rows_ref, taps_ref, filt_ref = rest[after:]
    own, _, lon = fields_ref.shape
    chunk = lon // chunks
    width = out_refs[0].shape[1]
    total = rows_ref.shape[2]
    pair = flip if isinstance(flip, int) else flip()
    own_at = HALO * (1 - pair)
    edge_at = own * pair

    def put(slot, cells):
        rows_ref[slot, :, LANES : LANES + lon] = cells
        rows_ref[slot, :, 0:LANES] = cells[:, lon - LANES :]
        full = (lon // LANES) * LANES
        tail = total - LANES - lon
        rows_ref[slot, :, LANES + full :] = jnp.concatenate(
            [cells[:, full:], cells[:, :tail]], axis=1
        )

    for row in range(own):
        put(own_at + row, fields_ref[row])
    for row in range(HALO):
        if has_edge:
            put(edge_at + row, edge_ref[row])
        else:
            rows_ref[edge_at + row] = jnp.zeros(rows_ref.shape[1:], rows_ref.dtype)

    lane = lax.broadcasted_iota(jnp.int32, (G, LANES), 1)
    begins = [LANES + chunk * target(lax.axis_index("chan"), k, chunks) for k in picks]

    def fill(slot, tap, source, offset):
        for k, origin in enumerate(begins):
            begin = origin + offset
            first = lax.div(begin, LANES)
            shift = lax.rem(begin, LANES)
            back = lax.rem(LANES - shift, LANES)
            keep = lane < LANES - shift
            turned = []
            for t in range(width // LANES + 1):
                start = pl.multiple_of((first + t) * LANES, LANES)
                tile = rows_ref[source, :, pl.ds(start, LANES)]
                turned.append(pltpu.roll(tile, back, 1))
            for t in range(width // LANES):
                at = k * width + t * LANES
                taps_ref[slot, tap * G : (tap + 1) * G, at : at + LANES] = jnp.where(
                    keep, turned[t], turned[t + 1]
                )

    eye = jnp.where(
        lax.broadcasted_iota(jnp.int32, (G, G), 0) == lax.broadcasted_iota(jnp.int32, (G, G), 1),
        1.0,
        0.0,
    ).astype(jnp.bfloat16)
    for i in range(2):
        row = 2 * pair + i
        pieces = []
        for tap in range(S):
            picked = weight_ref[basis_ref[row, tap]].astype(jnp.float32) * value_ref[row, tap]
            pieces.append(picked.astype(jnp.bfloat16))
        pieces.append(eye)
        for k in range(TAPS // 2):
            filt_ref[i, :, k * 2 * G : (k + 1) * 2 * G] = jnp.concatenate(
                [pieces[2 * k], pieces[2 * k + 1]], axis=1
            )
        for tap in range(S):
            fill(i, tap, HALO + i + lat_ref[row, tap], lon_ref[row, tap])
        fill(i, S, HALO + i, 0)
        mixed = jnp.dot(filt_ref[i], taps_ref[i], preferred_element_type=jnp.float32).astype(
            jnp.bfloat16
        )
        for k in range(len(picks)):
            out_refs[k][i * G : (i + 1) * G, :] = mixed[:, k * width : (k + 1) * width]


def conv_rows(pair, supports, fields, edge, weight, chunks, picks, after, roomy):
    own, chans, lon = fields.shape
    width = ceil_to(lon // chunks, LANES)
    highest = (LANES + lon - lon // chunks + DLON) // LANES
    total = (highest + 1) * LANES + width
    arrays = [fields] + ([] if edge is None else [edge]) + [weight]
    return pl.pallas_call(
        functools.partial(conv_kernel, chunks, picks, edge is not None, len(after), pair),
        out_shape=[jax.ShapeDtypeStruct((2 * chans, width), jnp.bfloat16)] * len(picks),
        in_specs=[SMEM] * 4 + [VMEM] * len(arrays) + [ANY] * len(after),
        out_specs=[VMEM] * len(picks),
        scratch_shapes=[
            pltpu.VMEM((own + HALO, chans, total), jnp.bfloat16),
            pltpu.VMEM((2, TAPS * G, len(picks) * width), jnp.bfloat16),
            pltpu.VMEM((2, G, TAPS * G), jnp.bfloat16),
        ],
        compiler_params=params(56 if roomy else 20),
        cost_estimate=takes(1 if len(picks) > 1 else 0.2),
        name="conv_rows",
    )(*supports, *arrays, *after)


def mlp_kernel(parts, last, after, *rest):
    blocks, rest = rest[:parts], rest[parts:]
    up_ref, down_ref, table_ref, *rest = rest
    rest = rest[after:]
    if last:
        earlier_ref, out_ref, cells_ref = rest
    else:
        out_ref, cells_ref = rest
    width = blocks[0].shape[1]
    place = lax.axis_index("chan")
    for block, k in zip(blocks, range(parts)):
        origin = pl.multiple_of(source(place, k, parts) * G, G)
        for i in range(2):
            cells_ref[pl.ds(origin, G), i * width : (i + 1) * width] = block[
                i * G : (i + 1) * G, :
            ]
    values = cells_ref[...].astype(jnp.float32)
    center = values - jnp.mean(values, axis=0, keepdims=True)
    spread = jnp.mean(center * center, axis=0, keepdims=True)
    normed = (center * lax.rsqrt(spread + EPS)).astype(jnp.bfloat16)
    lifted = jnp.dot(up_ref[...], normed, preferred_element_type=jnp.float32)
    scale = math.sqrt(2.0 / math.pi)
    inner = lifted * (scale + (scale * 0.044715) * (lifted * lifted))
    half = 0.5 * lifted
    active = (half + half * jnp.tanh(inner)).astype(jnp.bfloat16)
    lowered = jnp.dot(down_ref[...], active, preferred_element_type=jnp.float32)
    result = (values + lowered).astype(jnp.bfloat16)
    found = []
    for i in range(2):
        modes = lax.dot_general(
            table_ref[place],
            result[:, i * width : (i + 1) * width],
            (((1,), (1,)), ((), ())),
            preferred_element_type=jnp.float32,
        )
        found.append(modes.reshape(modes.shape[0] // SLOT, SLOT, modes.shape[1]))
    block = jnp.concatenate(found, axis=1).astype(jnp.bfloat16)
    if last:
        out_ref[:, 0 : 2 * SLOT, :] = earlier_ref[...]
        out_ref[:, 2 * SLOT : 4 * SLOT, :] = block
    else:
        out_ref[...] = block


def mlp_rows(blocks, up, down, tables, earlier, dests, after):
    pair_chans, width = blocks[0].shape
    chan = len(blocks) * pair_chans // 2
    last = earlier is not None
    arrays = [*blocks, up, down, tables, *after] + ([earlier] if last else [])
    rows = (4 if last else 2) * SLOT
    return pl.pallas_call(
        functools.partial(mlp_kernel, len(blocks), last, len(after)),
        out_shape=jax.ShapeDtypeStruct((dests, rows, chan), jnp.bfloat16),
        in_specs=[VMEM] * (len(blocks) + 3)
        + [ANY] * len(after)
        + [VMEM] * last,
        out_specs=VMEM,
        scratch_shapes=[pltpu.VMEM((chan, 2 * width), jnp.bfloat16)],
        compiler_params=params(20 if dests <= FEW else 40),
        cost_estimate=takes(1),
        name="mlp_rows",
    )(*arrays)


def expand_kernel(legendre_ref, spread_ref, out_ref):
    _, lats, degrees = legendre_ref.shape
    m = pl.program_id(0)
    first = lax.axis_index(("lat", "chan")) * pl.num_programs(0)
    degree = lax.broadcasted_iota(jnp.int32, (lats, degrees), 1)
    kept = jnp.where(degree >= first + m, legendre_ref[0].astype(jnp.float32), 0.0)
    wide = lax.dot_general(
        kept.astype(jnp.bfloat16),
        spread_ref[...],
        (((0,), (0,)), ((), ())),
        preferred_element_type=jnp.float32,
    )
    slot = lax.rem(lax.broadcasted_iota(jnp.int32, wide.shape, 1), SLOT)
    for r in range(2):
        out_ref[0, r] = jnp.where(slot == 2 * m + r, wide, 0.0).astype(jnp.bfloat16)


def expand(legendre, spread):
    modes, lats, degrees = legendre.shape
    depth = spread.shape[1]
    return pl.pallas_call(
        expand_kernel,
        out_shape=jax.ShapeDtypeStruct((modes, 2, degrees, depth), jnp.bfloat16),
        grid=(modes,),
        in_specs=[
            pl.BlockSpec((1, lats, degrees), lambda m: (m, 0, 0)),
            pl.BlockSpec((lats, depth), lambda m: (0, 0)),
        ],
        out_specs=pl.BlockSpec((1, 2, degrees, depth), lambda m: (m, 0, 0, 0)),
        compiler_params=params(10 if depth <= 512 else 48),
        cost_estimate=takes(0.2),
        name="expand",
    )(legendre, spread)


def final_kernel(left_ref, spectrum_ref, out_ref, result_ref, sems):
    modes = left_ref.shape[0]
    chan = spectrum_ref.shape[1]
    copies = []
    for m in range(modes):
        for r in range(2):
            result_ref[m, :, r * chan : (r + 1) * chan] = jnp.dot(
                left_ref[m, r], spectrum_ref[...], preferred_element_type=jnp.float32
            ).astype(jnp.bfloat16)
        copies.append(pltpu.make_async_copy(result_ref.at[m], out_ref.at[m], sems.at[m]))
        copies[-1].start()
    for copy in copies:
        copy.wait()


def final_sum(left, spectrum):
    modes, _, degrees, depth = left.shape
    shape = (modes, degrees, 2 * spectrum.shape[1])
    return pl.pallas_call(
        final_kernel,
        out_shape=jax.ShapeDtypeStruct(shape, jnp.bfloat16),
        in_specs=[VMEM, VMEM],
        out_specs=HBM,
        scratch_shapes=[pltpu.VMEM(shape, jnp.bfloat16), pltpu.SemaphoreType.DMA((modes,))],
        compiler_params=params(8 if depth <= 512 else 48),
        cost_estimate=takes(1),
        name="final_sum",
    )(left, spectrum)


def fourier_blocks(lon, chunks, width, dests, mode_dev):
    chunk = lon // chunks
    index = np.arange(lon, dtype=np.int64)
    mode = np.arange(dests * mode_dev, dtype=np.int64)
    angle = ((mode[:, None] * index[None, :]) % lon) * (2.0 * math.pi / lon)
    paired = np.stack([np.cos(angle), -np.sin(angle)], axis=1) * math.sqrt(2.0 / lon)
    paired = paired.reshape(dests, 2 * mode_dev, chunks, chunk)
    table = np.zeros((chunks, dests, SLOT, width), np.float32)
    table[:, :, : 2 * mode_dev, :chunk] = np.transpose(paired, (2, 0, 1, 3))
    return table.reshape(chunks, dests * SLOT, width).astype(jnp.bfloat16)


def turn(block, axis, count, k):
    return lax.ppermute(block, axis, [(i, (i + k) % count) for i in range(count)])


def on_device(
    fields,
    disco_weight,
    support_lat,
    support_lon,
    support_basis,
    support_value,
    w_up,
    w_down,
    legendre,
):
    lat_dev, lon, _ = fields.shape
    num_lat = lax.axis_size("lat")
    num_chan = lax.axis_size("chan")
    mode_dev, _, lats = legendre.shape
    dests = num_lat * num_chan
    width = ceil_to(lon // num_chan, LANES)
    band = lax.axis_index("lat")
    supports = (support_lat, support_lon, support_basis, support_value)

    two_bands = num_lat == 2
    cells = jnp.swapaxes(fields, 1, 2)
    if two_bands:
        edge_out = lax.dynamic_slice_in_dim(cells, HALO * (1 - band), HALO, axis=0)
        edges = [None, lax.ppermute(edge_out, "lat", [(0, 1), (1, 0)])]
        pairs = [lambda: lax.axis_index("lat"), lambda: 1 - lax.axis_index("lat")]
    else:
        ends = num_lat - 1
        edges = [
            lax.ppermute(cells[lat_dev - HALO :], "lat", [(i, i + 1) for i in range(ends)]),
            lax.ppermute(cells[:HALO], "lat", [(i + 1, i) for i in range(ends)]),
        ]
        pairs = [0, 1]

    tables = jnp.asarray(fourier_blocks(lon, num_chan, width, dests, mode_dev))
    up = w_up.T
    down = w_down.T

    depth = dests * 4 * SLOT
    row = np.arange(depth)
    source_band = row // (4 * SLOT) // num_chan
    phase = (row // (2 * SLOT)) % 2
    source_pair = (phase ^ source_band) if two_bands else phase
    lat_of = lat_dev * source_band + 2 * source_pair + (row // SLOT) % 2
    spread = (lat_of[None, :] == np.arange(lats)[:, None]).astype(jnp.bfloat16)
    left = expand(jnp.swapaxes(legendre, 1, 2), jnp.asarray(spread))

    order = list(range(1, num_chan))
    halves = [
        (pair, supports, cells, edge, disco_weight, num_chan)
        for edge, pair in zip(edges, pairs)
    ]
    received = []
    for half, edge in zip(halves, edges):
        sent = conv_rows(*half, order, [], edge is None)
        received.append([turn(block, "chan", num_chan, k) for k, block in zip(order, sent)])
    after = [sent[1], received[0][0]]
    for half, blocks in zip(halves, received):
        after = conv_rows(*half, (0,), after, False)
        blocks.insert(0, after[0])
    spectrum = None
    for blocks in received:
        spectrum = mlp_rows(blocks, up, down, tables, spectrum, dests, list(after))
        after = []

    both = ("lat", "chan")
    gathered = lax.all_to_all(spectrum, both, split_axis=0, concat_axis=0, tiled=True)
    return final_sum(left, gathered.reshape(depth, gathered.shape[2]))


def solution(mesh):
    in_specs = (
        P(("tm", "lat"), None, "chan"),
        P(None, "chan", None),
        P("lat", None),
        P("lat", None),
        P("lat", None),
        P("lat", None),
        P(),
        P(),
        P(("lat", "chan"), None, None),
    )
    out_specs = P(("tm", "lat", "chan"), None, None)
    return jax.shard_map(
        on_device, mesh=mesh, in_specs=in_specs, out_specs=out_specs, check_vma=False
    )
```

```python
import functools
import math

import jax
import jax.numpy as jnp
import numpy as np
from jax import lax
from jax.experimental import pallas as pl
from jax.experimental.pallas import tpu as pltpu
from jax.sharding import PartitionSpec as P

G = 64
S = 9
HALO = 2
DLON = 4
TAPS = S + 1
LANES = 128
SLOT = 8
EPS = 1e-05
FEW = 8
MIB = 1024 * 1024
FLOPS_PER_US = 1_000_000_000

SMEM = pl.BlockSpec(memory_space=pltpu.SMEM)
VMEM = pl.BlockSpec(memory_space=pltpu.VMEM)
ANY = pl.BlockSpec(memory_space=pl.ANY)
HBM = pl.BlockSpec(memory_space=pltpu.HBM)


def ceil_to(value, step):
    return -(-value // step) * step


def params(mib):
    return pltpu.CompilerParams(vmem_limit_bytes=mib * MIB)


def takes(micros):
    return pl.CostEstimate(flops=int(micros * FLOPS_PER_US), bytes_accessed=0, transcendentals=0)


def paired(count):
    return count & (count - 1) == 0


def target(place, k, count):
    return place ^ k if paired(count) else (place + k) % count


def source(place, k, count):
    return place ^ k if paired(count) else (place - k + count) % count


def issue_order(count):
    return [*range(2, count), 1] if paired(count) else list(range(1, count))


def conv_kernel(chunks, picks, has_edge, after, flip, manual, *refs):
    count = len(picks)
    if manual:
        sources, outs, refs = refs[:6], refs[6 : 6 + count], refs[6 + count :]
        *scratch, held, sems, out_sems, rows_ref, taps_ref, filt_ref = refs
        copies = [
            pltpu.make_async_copy(sources[k], scratch[k], sems.at[k]) for k in range(len(sources))
        ]
        for copy in reversed(copies):
            copy.start()
        for copy in copies[:-1]:
            copy.wait()
        lat_ref, lon_ref, basis_ref, value_ref, weight_ref, fields_ref = scratch
        out_refs = [held.at[k] for k in range(count)]
        edge_ref = None
    else:
        lat_ref, lon_ref, basis_ref, value_ref, weight_ref, fields_ref, *refs = refs
        edge_ref, refs = (refs[0], refs[1:]) if has_edge else (None, refs)
        *out_refs, rows_ref, taps_ref, filt_ref = refs[after:]
    own, _, lon = fields_ref.shape
    chunk = lon // chunks
    width = out_refs[0].shape[1]
    total = rows_ref.shape[2]
    pair = flip if isinstance(flip, int) else flip()
    own_at = HALO * (1 - pair)
    edge_at = own * pair

    eye = jnp.where(
        lax.broadcasted_iota(jnp.int32, (G, G), 0) == lax.broadcasted_iota(jnp.int32, (G, G), 1),
        1.0,
        0.0,
    ).astype(jnp.bfloat16)
    for i in range(2):
        row = 2 * pair + i
        pieces = []
        for tap in range(S):
            picked = weight_ref[basis_ref[row, tap]].astype(jnp.float32) * value_ref[row, tap]
            pieces.append(picked.astype(jnp.bfloat16))
        pieces.append(eye)
        for k in range(TAPS // 2):
            filt_ref[i, :, k * 2 * G : (k + 1) * 2 * G] = jnp.concatenate(
                [pieces[2 * k], pieces[2 * k + 1]], axis=1
            )
    if manual:
        copies[-1].wait()

    def put(slot, cells):
        rows_ref[slot, :, LANES : LANES + lon] = cells
        rows_ref[slot, :, 0:LANES] = cells[:, lon - LANES :]
        full = (lon // LANES) * LANES
        tail = total - LANES - lon
        rows_ref[slot, :, LANES + full :] = jnp.concatenate(
            [cells[:, full:], cells[:, :tail]], axis=1
        )

    for row in range(own):
        put(own_at + row, fields_ref[row])
    for row in range(HALO):
        if has_edge:
            put(edge_at + row, edge_ref[row])
        else:
            rows_ref[edge_at + row] = jnp.zeros(rows_ref.shape[1:], rows_ref.dtype)

    lane = lax.broadcasted_iota(jnp.int32, (G, LANES), 1)
    begins = [LANES + chunk * target(lax.axis_index("chan"), k, chunks) for k in picks]

    def fill(slot, tap, source, offset):
        for k, origin in enumerate(begins):
            begin = origin + offset
            first = lax.div(begin, LANES)
            shift = lax.rem(begin, LANES)
            back = lax.rem(LANES - shift, LANES)
            keep = lane < LANES - shift
            turned = []
            for t in range(width // LANES + 1):
                start = pl.multiple_of((first + t) * LANES, LANES)
                tile = rows_ref[source, :, pl.ds(start, LANES)]
                turned.append(pltpu.roll(tile, back, 1))
            for t in range(width // LANES):
                at = k * width + t * LANES
                taps_ref[slot, tap * G : (tap + 1) * G, at : at + LANES] = jnp.where(
                    keep, turned[t], turned[t + 1]
                )

    for i in range(2):
        row = 2 * pair + i
        for tap in range(S):
            fill(i, tap, HALO + i + lat_ref[row, tap], lon_ref[row, tap])
        fill(i, S, HALO + i, 0)
        mixed = jnp.dot(filt_ref[i], taps_ref[i], preferred_element_type=jnp.float32).astype(
            jnp.bfloat16
        )
        for k in range(len(picks)):
            out_refs[k][i * G : (i + 1) * G, :] = mixed[:, k * width : (k + 1) * width]
    if manual:
        copies = [
            pltpu.make_async_copy(out_refs[k], outs[k], out_sems.at[k]) for k in range(count)
        ]
        for copy in copies:
            copy.start()
        for copy in copies:
            copy.wait()


def conv_rows(pair, supports, fields, edge, weight, chunks, picks, after, manual):
    own, chans, lon = fields.shape
    width = ceil_to(lon // chunks, LANES)
    highest = (LANES + lon - lon // chunks + DLON) // LANES
    total = (highest + 1) * LANES + width
    count = len(picks)
    arrays = [*supports, weight, fields] + ([] if edge is None else [edge])
    outs = [jax.ShapeDtypeStruct((2 * chans, width), jnp.bfloat16)] * count
    scratch = [
        pltpu.VMEM((own + HALO, chans, total), jnp.bfloat16),
        pltpu.VMEM((2, TAPS * G, count * width), jnp.bfloat16),
        pltpu.VMEM((2, G, TAPS * G), jnp.bfloat16),
    ]
    if manual:
        in_specs, out_specs = [ANY] * len(arrays), [ANY] * count
        spaces = [pltpu.SMEM] * len(supports) + [pltpu.VMEM] * 2
        scratch = [
            *(space(array.shape, array.dtype) for space, array in zip(spaces, arrays)),
            pltpu.VMEM((count, 2 * chans, width), jnp.bfloat16),
            pltpu.SemaphoreType.DMA((len(arrays),)),
            pltpu.SemaphoreType.DMA((count,)),
            *scratch,
        ]
    else:
        in_specs = [SMEM] * len(supports) + [VMEM] * (len(arrays) - len(supports))
        in_specs, out_specs = in_specs + [ANY] * len(after), [VMEM] * count
    return pl.pallas_call(
        functools.partial(
            conv_kernel, chunks, picks, edge is not None, len(after), pair, manual
        ),
        out_shape=outs,
        in_specs=in_specs,
        out_specs=out_specs,
        scratch_shapes=scratch,
        compiler_params=params(56 if manual else 20),
        cost_estimate=takes(1 if count > 1 else 0.2),
        name="conv_rows",
    )(*arrays, *after)


def mlp_kernel(parts, last, after, *rest):
    blocks, rest = rest[:parts], rest[parts:]
    up_ref, down_ref, table_ref, *rest = rest
    rest = rest[after:]
    if last:
        earlier_ref, out_ref, cells_ref = rest
    else:
        out_ref, cells_ref = rest
    width = blocks[0].shape[1]
    place = lax.axis_index("chan")
    for block, k in zip(blocks, [0, *issue_order(parts)]):
        origin = pl.multiple_of(source(place, k, parts) * G, G)
        for i in range(2):
            cells_ref[pl.ds(origin, G), i * width : (i + 1) * width] = block[
                i * G : (i + 1) * G, :
            ]
    values = cells_ref[...].astype(jnp.float32)
    center = values - jnp.mean(values, axis=0, keepdims=True)
    spread = jnp.mean(center * center, axis=0, keepdims=True)
    normed = (center * lax.rsqrt(spread + EPS)).astype(jnp.bfloat16)
    lifted = jnp.dot(up_ref[...], normed, preferred_element_type=jnp.float32)
    scale = math.sqrt(2.0 / math.pi)
    inner = lifted * (scale + (scale * 0.044715) * (lifted * lifted))
    half = 0.5 * lifted
    active = (half + half * jnp.tanh(inner)).astype(jnp.bfloat16)
    lowered = jnp.dot(down_ref[...], active, preferred_element_type=jnp.float32)
    result = (values + lowered).astype(jnp.bfloat16)
    found = []
    for i in range(2):
        modes = lax.dot_general(
            table_ref[place],
            result[:, i * width : (i + 1) * width],
            (((1,), (1,)), ((), ())),
            preferred_element_type=jnp.float32,
        )
        found.append(modes.reshape(modes.shape[0] // SLOT, SLOT, modes.shape[1]))
    block = jnp.concatenate(found, axis=1).astype(jnp.bfloat16)
    if last:
        out_ref[:, 0 : 2 * SLOT, :] = earlier_ref[...]
        out_ref[:, 2 * SLOT : 4 * SLOT, :] = block
    else:
        out_ref[...] = block


def mlp_rows(blocks, up, down, tables, earlier, dests, after):
    pair_chans, width = blocks[0].shape
    chan = len(blocks) * pair_chans // 2
    last = earlier is not None
    arrays = [*blocks, up, down, tables, *after] + ([earlier] if last else [])
    rows = (4 if last else 2) * SLOT
    return pl.pallas_call(
        functools.partial(mlp_kernel, len(blocks), last, len(after)),
        out_shape=jax.ShapeDtypeStruct((dests, rows, chan), jnp.bfloat16),
        in_specs=[VMEM] * (len(blocks) + 3)
        + [ANY] * len(after)
        + [VMEM] * last,
        out_specs=VMEM,
        scratch_shapes=[pltpu.VMEM((chan, 2 * width), jnp.bfloat16)],
        compiler_params=params(20 if dests <= FEW else 40),
        cost_estimate=takes(1),
        name="mlp_rows",
    )(*arrays)


def expand_kernel(legendre_ref, spread_ref, out_ref):
    _, lats, degrees = legendre_ref.shape
    m = pl.program_id(0)
    first = lax.axis_index(("lat", "chan")) * pl.num_programs(0)
    degree = lax.broadcasted_iota(jnp.int32, (lats, degrees), 1)
    kept = jnp.where(degree >= first + m, legendre_ref[0].astype(jnp.float32), 0.0)
    wide = lax.dot_general(
        kept.astype(jnp.bfloat16),
        spread_ref[...],
        (((0,), (0,)), ((), ())),
        preferred_element_type=jnp.float32,
    )
    slot = lax.rem(lax.broadcasted_iota(jnp.int32, wide.shape, 1), SLOT)
    for r in range(2):
        out_ref[0, r] = jnp.where(slot == 2 * m + r, wide, 0.0).astype(jnp.bfloat16)


def expand(legendre, spread):
    modes, lats, degrees = legendre.shape
    depth = spread.shape[1]
    return pl.pallas_call(
        expand_kernel,
        out_shape=jax.ShapeDtypeStruct((modes, 2, degrees, depth), jnp.bfloat16),
        grid=(modes,),
        in_specs=[
            pl.BlockSpec((1, lats, degrees), lambda m: (m, 0, 0)),
            pl.BlockSpec((lats, depth), lambda m: (0, 0)),
        ],
        out_specs=pl.BlockSpec((1, 2, degrees, depth), lambda m: (m, 0, 0, 0)),
        compiler_params=params(10 if depth <= 512 else 48),
        cost_estimate=takes(0.2),
        name="expand",
    )(legendre, spread)


def final_kernel(left_ref, spectrum_ref, out_ref, result_ref, sems):
    modes = left_ref.shape[0]
    chan = spectrum_ref.shape[1]
    copies = []
    for m in range(modes):
        for r in range(2):
            result_ref[m, :, r * chan : (r + 1) * chan] = jnp.dot(
                left_ref[m, r], spectrum_ref[...], preferred_element_type=jnp.float32
            ).astype(jnp.bfloat16)
        copies.append(pltpu.make_async_copy(result_ref.at[m], out_ref.at[m], sems.at[m]))
        copies[-1].start()
    for copy in copies:
        copy.wait()


def final_sum(left, spectrum):
    modes, _, degrees, depth = left.shape
    shape = (modes, degrees, 2 * spectrum.shape[1])
    return pl.pallas_call(
        final_kernel,
        out_shape=jax.ShapeDtypeStruct(shape, jnp.bfloat16),
        in_specs=[VMEM, VMEM],
        out_specs=HBM,
        scratch_shapes=[pltpu.VMEM(shape, jnp.bfloat16), pltpu.SemaphoreType.DMA((modes,))],
        compiler_params=params(8 if depth <= 512 else 48),
        cost_estimate=takes(1),
        name="final_sum",
    )(left, spectrum)


def fourier_blocks(lon, chunks, width, dests, mode_dev):
    chunk = lon // chunks
    index = np.arange(lon, dtype=np.int64)
    mode = np.arange(dests * mode_dev, dtype=np.int64)
    angle = ((mode[:, None] * index[None, :]) % lon) * (2.0 * math.pi / lon)
    paired = np.stack([np.cos(angle), -np.sin(angle)], axis=1) * math.sqrt(2.0 / lon)
    paired = paired.reshape(dests, 2 * mode_dev, chunks, chunk)
    table = np.zeros((chunks, dests, SLOT, width), np.float32)
    table[:, :, : 2 * mode_dev, :chunk] = np.transpose(paired, (2, 0, 1, 3))
    return table.reshape(chunks, dests * SLOT, width).astype(jnp.bfloat16)


def turn(block, axis, count, k):
    return lax.ppermute(block, axis, [(i, target(i, k, count)) for i in range(count)])


def on_device(
    fields,
    disco_weight,
    support_lat,
    support_lon,
    support_basis,
    support_value,
    w_up,
    w_down,
    legendre,
):
    lat_dev, lon, _ = fields.shape
    num_lat = lax.axis_size("lat")
    num_chan = lax.axis_size("chan")
    mode_dev, _, lats = legendre.shape
    dests = num_lat * num_chan
    width = ceil_to(lon // num_chan, LANES)
    band = lax.axis_index("lat")
    supports = (support_lat, support_lon, support_basis, support_value)

    two_bands = num_lat == 2
    cells = jnp.swapaxes(fields, 1, 2)
    if two_bands:
        edge_out = lax.dynamic_slice_in_dim(cells, HALO * (1 - band), HALO, axis=0)
        edges = [None, lax.ppermute(edge_out, "lat", [(0, 1), (1, 0)])]
        pairs = [lambda: lax.axis_index("lat"), lambda: 1 - lax.axis_index("lat")]
    else:
        ends = num_lat - 1
        edges = [
            lax.ppermute(cells[lat_dev - HALO :], "lat", [(i, i + 1) for i in range(ends)]),
            lax.ppermute(cells[:HALO], "lat", [(i + 1, i) for i in range(ends)]),
        ]
        pairs = [0, 1]

    tables = jnp.asarray(fourier_blocks(lon, num_chan, width, dests, mode_dev))
    up = w_up.T
    down = w_down.T

    depth = dests * 4 * SLOT
    row = np.arange(depth)
    source_band = row // (4 * SLOT) // num_chan
    phase = (row // (2 * SLOT)) % 2
    source_pair = (phase ^ source_band) if two_bands else phase
    lat_of = lat_dev * source_band + 2 * source_pair + (row // SLOT) % 2
    spread = (lat_of[None, :] == np.arange(lats)[:, None]).astype(jnp.bfloat16)
    left = expand(jnp.swapaxes(legendre, 1, 2), jnp.asarray(spread))

    order = issue_order(num_chan)
    halves = [
        (pair, supports, cells, edge, disco_weight, num_chan)
        for edge, pair in zip(edges, pairs)
    ]
    received = []
    for half, edge in zip(halves, edges):
        sent = conv_rows(*half, order, [], edge is None)
        received.append([turn(block, "chan", num_chan, k) for k, block in zip(order, sent)])
    after = sent[1:2]
    for half, blocks in zip(halves, received):
        after = conv_rows(*half, (0,), after, False)
        blocks.insert(0, after[0])
    spectrum = None
    for blocks in received:
        spectrum = mlp_rows(blocks, up, down, tables, spectrum, dests, list(after))
        after = []

    both = ("lat", "chan")
    gathered = lax.all_to_all(spectrum, both, split_axis=0, concat_axis=0, tiled=True)
    return final_sum(left, gathered.reshape(depth, gathered.shape[2]))


def solution(mesh):
    in_specs = (
        P(("tm", "lat"), None, "chan"),
        P(None, "chan", None),
        P("lat", None),
        P("lat", None),
        P("lat", None),
        P("lat", None),
        P(),
        P(),
        P(("lat", "chan"), None, None),
    )
    out_specs = P(("tm", "lat", "chan"), None, None)
    return jax.shard_map(
        on_device, mesh=mesh, in_specs=in_specs, out_specs=out_specs, check_vma=False
    )
```

```python
import functools
import math

import jax
import jax.numpy as jnp
import numpy as np
from jax import lax
from jax.experimental import pallas as pl
from jax.experimental.pallas import tpu as pltpu
from jax.sharding import PartitionSpec as P

G = 64
S = 9
HALO = 2
DLON = 4
TAPS = S + 1
LANES = 128
SLOT = 8
EPS = 1e-05
FEW = 8
MIB = 1024 * 1024
EDGE_COST = 4
FLOPS_PER_US = 1_000_000_000

SMEM = pl.BlockSpec(memory_space=pltpu.SMEM)
VMEM = pl.BlockSpec(memory_space=pltpu.VMEM)
ANY = pl.BlockSpec(memory_space=pl.ANY)
HBM = pl.BlockSpec(memory_space=pltpu.HBM)


def ceil_to(value, step):
    return -(-value // step) * step


def params(mib):
    return pltpu.CompilerParams(vmem_limit_bytes=mib * MIB)


def takes(micros):
    return pl.CostEstimate(flops=int(micros * FLOPS_PER_US), bytes_accessed=0, transcendentals=0)


def paired(count):
    return count & (count - 1) == 0


def target(place, k, count):
    return place ^ k if paired(count) else (place + k) % count


def source(place, k, count):
    return place ^ k if paired(count) else (place - k + count) % count


def issue_order(count):
    return [*range(2, count), 1] if paired(count) else list(range(1, count))


def edge_kernel(fields_ref, same_ref, out_ref):
    start = HALO * (1 - lax.axis_index("lat"))
    for k in range(HALO):
        out_ref[k] = fields_ref[start + k]
    same_ref[...] = fields_ref[...]


def edge_rows(fields):
    shapes = [fields.shape, (HALO, *fields.shape[1:])]
    return pl.pallas_call(
        edge_kernel,
        out_shape=[jax.ShapeDtypeStruct(shape, fields.dtype) for shape in shapes],
        in_specs=[VMEM],
        out_specs=[VMEM] * 2,
        compiler_params=params(8),
        cost_estimate=takes(EDGE_COST),
        name="edge_rows",
    )(fields)


def conv_kernel(
    chunks, picks, has_edge, after, flip, lat_ref, lon_ref, basis_ref, value_ref, fields_ref, *rest
):
    if has_edge:
        edge_ref, weight_ref, *rest = rest
    else:
        edge_ref, (weight_ref, *rest) = None, rest
    *out_refs, rows_ref, taps_ref, filt_ref = rest[after:]
    own, _, lon = fields_ref.shape
    chunk = lon // chunks
    width = out_refs[0].shape[1]
    total = rows_ref.shape[2]
    pair = flip if isinstance(flip, int) else flip()
    own_at = HALO * (1 - pair)
    edge_at = own * pair

    def put(slot, cells):
        rows_ref[slot, :, LANES : LANES + lon] = cells
        rows_ref[slot, :, 0:LANES] = cells[:, lon - LANES :]
        full = (lon // LANES) * LANES
        tail = total - LANES - lon
        rows_ref[slot, :, LANES + full :] = jnp.concatenate(
            [cells[:, full:], cells[:, :tail]], axis=1
        )

    for row in range(own):
        put(own_at + row, fields_ref[row])
    for row in range(HALO):
        if has_edge:
            put(edge_at + row, edge_ref[row])
        else:
            rows_ref[edge_at + row] = jnp.zeros(rows_ref.shape[1:], rows_ref.dtype)

    lane = lax.broadcasted_iota(jnp.int32, (G, LANES), 1)
    begins = [LANES + chunk * target(lax.axis_index("chan"), k, chunks) for k in picks]

    def fill(slot, tap, source, offset):
        for k, origin in enumerate(begins):
            begin = origin + offset
            first = lax.div(begin, LANES)
            shift = lax.rem(begin, LANES)
            back = lax.rem(LANES - shift, LANES)
            keep = lane < LANES - shift
            turned = []
            for t in range(width // LANES + 1):
                start = pl.multiple_of((first + t) * LANES, LANES)
                tile = rows_ref[source, :, pl.ds(start, LANES)]
                turned.append(pltpu.roll(tile, back, 1))
            for t in range(width // LANES):
                at = k * width + t * LANES
                taps_ref[slot, tap * G : (tap + 1) * G, at : at + LANES] = jnp.where(
                    keep, turned[t], turned[t + 1]
                )

    eye = jnp.where(
        lax.broadcasted_iota(jnp.int32, (G, G), 0) == lax.broadcasted_iota(jnp.int32, (G, G), 1),
        1.0,
        0.0,
    ).astype(jnp.bfloat16)
    for i in range(2):
        row = 2 * pair + i
        pieces = []
        for tap in range(S):
            picked = weight_ref[basis_ref[row, tap]].astype(jnp.float32) * value_ref[row, tap]
            pieces.append(picked.astype(jnp.bfloat16))
        pieces.append(eye)
        for k in range(TAPS // 2):
            filt_ref[i, :, k * 2 * G : (k + 1) * 2 * G] = jnp.concatenate(
                [pieces[2 * k], pieces[2 * k + 1]], axis=1
            )
        for tap in range(S):
            fill(i, tap, HALO + i + lat_ref[row, tap], lon_ref[row, tap])
        fill(i, S, HALO + i, 0)
        mixed = jnp.dot(filt_ref[i], taps_ref[i], preferred_element_type=jnp.float32).astype(
            jnp.bfloat16
        )
        for k in range(len(picks)):
            out_refs[k][i * G : (i + 1) * G, :] = mixed[:, k * width : (k + 1) * width]


def conv_rows(pair, supports, fields, edge, weight, chunks, picks, after, roomy):
    own, chans, lon = fields.shape
    width = ceil_to(lon // chunks, LANES)
    highest = (LANES + lon - lon // chunks + DLON) // LANES
    total = (highest + 1) * LANES + width
    arrays = [fields] + ([] if edge is None else [edge]) + [weight]
    return pl.pallas_call(
        functools.partial(conv_kernel, chunks, picks, edge is not None, len(after), pair),
        out_shape=[jax.ShapeDtypeStruct((2 * chans, width), jnp.bfloat16)] * len(picks),
        in_specs=[SMEM] * 4 + [VMEM] * len(arrays) + [ANY] * len(after),
        out_specs=[VMEM] * len(picks),
        scratch_shapes=[
            pltpu.VMEM((own + HALO, chans, total), jnp.bfloat16),
            pltpu.VMEM((2, TAPS * G, len(picks) * width), jnp.bfloat16),
            pltpu.VMEM((2, G, TAPS * G), jnp.bfloat16),
        ],
        compiler_params=params(20),
        cost_estimate=takes(1 if len(picks) > 1 else 0.2),
        name="conv_rows",
    )(*supports, *arrays, *after)


def mlp_kernel(parts, last, after, *rest):
    blocks, rest = rest[:parts], rest[parts:]
    up_ref, down_ref, table_ref, *rest = rest
    rest = rest[after:]
    if last:
        earlier_ref, out_ref, cells_ref = rest
    else:
        out_ref, cells_ref = rest
    width = blocks[0].shape[1]
    place = lax.axis_index("chan")
    for block, k in zip(blocks, [0, *issue_order(parts)]):
        origin = pl.multiple_of(source(place, k, parts) * G, G)
        for i in range(2):
            cells_ref[pl.ds(origin, G), i * width : (i + 1) * width] = block[
                i * G : (i + 1) * G, :
            ]
    values = cells_ref[...].astype(jnp.float32)
    center = values - jnp.mean(values, axis=0, keepdims=True)
    spread = jnp.mean(center * center, axis=0, keepdims=True)
    normed = (center * lax.rsqrt(spread + EPS)).astype(jnp.bfloat16)
    lifted = jnp.dot(up_ref[...], normed, preferred_element_type=jnp.float32)
    scale = math.sqrt(2.0 / math.pi)
    inner = lifted * (scale + (scale * 0.044715) * (lifted * lifted))
    half = 0.5 * lifted
    active = (half + half * jnp.tanh(inner)).astype(jnp.bfloat16)
    lowered = jnp.dot(down_ref[...], active, preferred_element_type=jnp.float32)
    result = (values + lowered).astype(jnp.bfloat16)
    found = []
    for i in range(2):
        modes = lax.dot_general(
            table_ref[place],
            result[:, i * width : (i + 1) * width],
            (((1,), (1,)), ((), ())),
            preferred_element_type=jnp.float32,
        )
        found.append(modes.reshape(modes.shape[0] // SLOT, SLOT, modes.shape[1]))
    block = jnp.concatenate(found, axis=1).astype(jnp.bfloat16)
    if last:
        out_ref[:, 0 : 2 * SLOT, :] = earlier_ref[...]
        out_ref[:, 2 * SLOT : 4 * SLOT, :] = block
    else:
        out_ref[...] = block


def mlp_rows(blocks, up, down, tables, earlier, dests, after):
    pair_chans, width = blocks[0].shape
    chan = len(blocks) * pair_chans // 2
    last = earlier is not None
    arrays = [*blocks, up, down, tables, *after] + ([earlier] if last else [])
    rows = (4 if last else 2) * SLOT
    return pl.pallas_call(
        functools.partial(mlp_kernel, len(blocks), last, len(after)),
        out_shape=jax.ShapeDtypeStruct((dests, rows, chan), jnp.bfloat16),
        in_specs=[VMEM] * (len(blocks) + 3)
        + [ANY] * len(after)
        + [VMEM] * last,
        out_specs=VMEM,
        scratch_shapes=[pltpu.VMEM((chan, 2 * width), jnp.bfloat16)],
        compiler_params=params(20 if dests <= FEW else 40),
        cost_estimate=takes(1),
        name="mlp_rows",
    )(*arrays)


def expand_kernel(legendre_ref, spread_ref, out_ref):
    _, lats, degrees = legendre_ref.shape
    m = pl.program_id(0)
    first = lax.axis_index(("lat", "chan")) * pl.num_programs(0)
    degree = lax.broadcasted_iota(jnp.int32, (lats, degrees), 1)
    kept = jnp.where(degree >= first + m, legendre_ref[0].astype(jnp.float32), 0.0)
    wide = lax.dot_general(
        kept.astype(jnp.bfloat16),
        spread_ref[...],
        (((0,), (0,)), ((), ())),
        preferred_element_type=jnp.float32,
    )
    slot = lax.rem(lax.broadcasted_iota(jnp.int32, wide.shape, 1), SLOT)
    for r in range(2):
        out_ref[0, r] = jnp.where(slot == 2 * m + r, wide, 0.0).astype(jnp.bfloat16)


def expand(legendre, spread):
    modes, lats, degrees = legendre.shape
    depth = spread.shape[1]
    return pl.pallas_call(
        expand_kernel,
        out_shape=jax.ShapeDtypeStruct((modes, 2, degrees, depth), jnp.bfloat16),
        grid=(modes,),
        in_specs=[
            pl.BlockSpec((1, lats, degrees), lambda m: (m, 0, 0)),
            pl.BlockSpec((lats, depth), lambda m: (0, 0)),
        ],
        out_specs=pl.BlockSpec((1, 2, degrees, depth), lambda m: (m, 0, 0, 0)),
        compiler_params=params(10 if depth <= 512 else 48),
        cost_estimate=takes(0.2),
        name="expand",
    )(legendre, spread)


def final_kernel(left_ref, spectrum_ref, out_ref, result_ref, sems):
    modes = left_ref.shape[0]
    chan = spectrum_ref.shape[1]
    copies = []
    for m in range(modes):
        for r in range(2):
            result_ref[m, :, r * chan : (r + 1) * chan] = jnp.dot(
                left_ref[m, r], spectrum_ref[...], preferred_element_type=jnp.float32
            ).astype(jnp.bfloat16)
        copies.append(pltpu.make_async_copy(result_ref.at[m], out_ref.at[m], sems.at[m]))
        copies[-1].start()
    for copy in copies:
        copy.wait()


def final_sum(left, spectrum):
    modes, _, degrees, depth = left.shape
    shape = (modes, degrees, 2 * spectrum.shape[1])
    return pl.pallas_call(
        final_kernel,
        out_shape=jax.ShapeDtypeStruct(shape, jnp.bfloat16),
        in_specs=[VMEM, VMEM],
        out_specs=HBM,
        scratch_shapes=[pltpu.VMEM(shape, jnp.bfloat16), pltpu.SemaphoreType.DMA((modes,))],
        compiler_params=params(8 if depth <= 512 else 48),
        cost_estimate=takes(1),
        name="final_sum",
    )(left, spectrum)


def fourier_blocks(lon, chunks, width, dests, mode_dev):
    chunk = lon // chunks
    index = np.arange(lon, dtype=np.int64)
    mode = np.arange(dests * mode_dev, dtype=np.int64)
    angle = ((mode[:, None] * index[None, :]) % lon) * (2.0 * math.pi / lon)
    paired = np.stack([np.cos(angle), -np.sin(angle)], axis=1) * math.sqrt(2.0 / lon)
    paired = paired.reshape(dests, 2 * mode_dev, chunks, chunk)
    table = np.zeros((chunks, dests, SLOT, width), np.float32)
    table[:, :, : 2 * mode_dev, :chunk] = np.transpose(paired, (2, 0, 1, 3))
    return table.reshape(chunks, dests * SLOT, width).astype(jnp.bfloat16)


def turn(block, axis, count, k):
    return lax.ppermute(block, axis, [(i, target(i, k, count)) for i in range(count)])


def on_device(
    fields,
    disco_weight,
    support_lat,
    support_lon,
    support_basis,
    support_value,
    w_up,
    w_down,
    legendre,
):
    lat_dev, lon, _ = fields.shape
    num_lat = lax.axis_size("lat")
    num_chan = lax.axis_size("chan")
    mode_dev, _, lats = legendre.shape
    dests = num_lat * num_chan
    width = ceil_to(lon // num_chan, LANES)
    supports = (support_lat, support_lon, support_basis, support_value)

    two_bands = num_lat == 2
    cells = jnp.swapaxes(fields, 1, 2)
    if two_bands:
        cells, edge_out = edge_rows(cells)
        edges = [None, lax.ppermute(edge_out, "lat", [(0, 1), (1, 0)])]
        pairs = [lambda: lax.axis_index("lat"), lambda: 1 - lax.axis_index("lat")]
    else:
        ends = num_lat - 1
        edges = [
            lax.ppermute(cells[lat_dev - HALO :], "lat", [(i, i + 1) for i in range(ends)]),
            lax.ppermute(cells[:HALO], "lat", [(i + 1, i) for i in range(ends)]),
        ]
        pairs = [0, 1]

    tables = jnp.asarray(fourier_blocks(lon, num_chan, width, dests, mode_dev))
    up = w_up.T
    down = w_down.T

    depth = dests * 4 * SLOT
    row = np.arange(depth)
    source_band = row // (4 * SLOT) // num_chan
    phase = (row // (2 * SLOT)) % 2
    source_pair = (phase ^ source_band) if two_bands else phase
    lat_of = lat_dev * source_band + 2 * source_pair + (row // SLOT) % 2
    spread = (lat_of[None, :] == np.arange(lats)[:, None]).astype(jnp.bfloat16)
    left = expand(jnp.swapaxes(legendre, 1, 2), jnp.asarray(spread))

    order = issue_order(num_chan)
    halves = [
        (pair, supports, cells, edge, disco_weight, num_chan)
        for edge, pair in zip(edges, pairs)
    ]
    received = []
    for half, edge in zip(halves, edges):
        sent = conv_rows(*half, order, [], edge is None)
        received.append([turn(block, "chan", num_chan, k) for k, block in zip(order, sent)])
    after = sent[1:2]
    for half, blocks in zip(halves, received):
        after = conv_rows(*half, (0,), after, False)
        blocks.insert(0, after[0])
    spectrum = None
    for blocks in received:
        spectrum = mlp_rows(blocks, up, down, tables, spectrum, dests, list(after))
        after = []

    both = ("lat", "chan")
    gathered = lax.all_to_all(spectrum, both, split_axis=0, concat_axis=0, tiled=True)
    return final_sum(left, gathered.reshape(depth, gathered.shape[2]))


def solution(mesh):
    in_specs = (
        P(("tm", "lat"), None, "chan"),
        P(None, "chan", None),
        P("lat", None),
        P("lat", None),
        P("lat", None),
        P("lat", None),
        P(),
        P(),
        P(("lat", "chan"), None, None),
    )
    out_specs = P(("tm", "lat", "chan"), None, None)
    return jax.shard_map(
        on_device, mesh=mesh, in_specs=in_specs, out_specs=out_specs, check_vma=False
    )
```

```python
import functools
import math

import jax
import jax.numpy as jnp
import numpy as np
from jax import lax
from jax.experimental import pallas as pl
from jax.experimental.pallas import tpu as pltpu
from jax.sharding import PartitionSpec as P

G = 64
S = 9
HALO = 2
DLON = 4
TAPS = S + 1
LANES = 128
SLOT = 8
EPS = 1e-05
FEW = 8
MIB = 1024 * 1024
EDGE_COST = 4
FLOPS_PER_US = 1_000_000_000

SMEM = pl.BlockSpec(memory_space=pltpu.SMEM)
VMEM = pl.BlockSpec(memory_space=pltpu.VMEM)
ANY = pl.BlockSpec(memory_space=pl.ANY)
HBM = pl.BlockSpec(memory_space=pltpu.HBM)


def ceil_to(value, step):
    return -(-value // step) * step


def params(mib):
    return pltpu.CompilerParams(vmem_limit_bytes=mib * MIB)


def takes(micros):
    return pl.CostEstimate(flops=int(micros * FLOPS_PER_US), bytes_accessed=0, transcendentals=0)


def paired(count):
    return count & (count - 1) == 0


def target(place, k, count):
    return place ^ k if paired(count) else (place + k) % count


def source(place, k, count):
    return place ^ k if paired(count) else (place - k + count) % count


def issue_order(count):
    return [*range(2, count), 1] if paired(count) else list(range(1, count))


def edge_kernel(fields_ref, same_ref, out_ref):
    start = HALO * (1 - lax.axis_index("lat"))
    for k in range(HALO):
        out_ref[k] = fields_ref[start + k]
    same_ref[...] = fields_ref[...]


def edge_rows(fields):
    shapes = [fields.shape, (HALO, *fields.shape[1:])]
    return pl.pallas_call(
        edge_kernel,
        out_shape=[jax.ShapeDtypeStruct(shape, fields.dtype) for shape in shapes],
        in_specs=[VMEM],
        out_specs=[VMEM] * 2,
        compiler_params=params(8),
        cost_estimate=takes(EDGE_COST),
        name="edge_rows",
    )(fields)


def conv_kernel(
    chunks, picks, has_edge, after, flip, lat_ref, lon_ref, basis_ref, value_ref, fields_ref, *rest
):
    if has_edge:
        edge_ref, weight_ref, *rest = rest
    else:
        edge_ref, (weight_ref, *rest) = None, rest
    *out_refs, rows_ref, taps_ref, filt_ref = rest[after:]
    own, _, lon = fields_ref.shape
    chunk = lon // chunks
    width = out_refs[0].shape[1]
    total = rows_ref.shape[2]
    pair = flip if isinstance(flip, int) else flip()
    own_at = HALO * (1 - pair)
    edge_at = own * pair

    def put(slot, cells):
        rows_ref[slot, :, LANES : LANES + lon] = cells
        rows_ref[slot, :, 0:LANES] = cells[:, lon - LANES :]
        full = (lon // LANES) * LANES
        tail = total - LANES - lon
        rows_ref[slot, :, LANES + full :] = jnp.concatenate(
            [cells[:, full:], cells[:, :tail]], axis=1
        )

    for row in range(own):
        put(own_at + row, fields_ref[row])
    for row in range(HALO):
        if has_edge:
            put(edge_at + row, edge_ref[row])
        else:
            rows_ref[edge_at + row] = jnp.zeros(rows_ref.shape[1:], rows_ref.dtype)

    lane = lax.broadcasted_iota(jnp.int32, (G, LANES), 1)
    begins = [LANES + chunk * target(lax.axis_index("chan"), k, chunks) for k in picks]

    def fill(slot, tap, source, offset):
        for k, origin in enumerate(begins):
            begin = origin + offset
            first = lax.div(begin, LANES)
            shift = lax.rem(begin, LANES)
            back = lax.rem(LANES - shift, LANES)
            keep = lane < LANES - shift
            turned = []
            for t in range(width // LANES + 1):
                start = pl.multiple_of((first + t) * LANES, LANES)
                tile = rows_ref[source, :, pl.ds(start, LANES)]
                turned.append(pltpu.roll(tile, back, 1))
            for t in range(width // LANES):
                at = k * width + t * LANES
                taps_ref[slot, tap * G : (tap + 1) * G, at : at + LANES] = jnp.where(
                    keep, turned[t], turned[t + 1]
                )

    eye = jnp.where(
        lax.broadcasted_iota(jnp.int32, (G, G), 0) == lax.broadcasted_iota(jnp.int32, (G, G), 1),
        1.0,
        0.0,
    ).astype(jnp.bfloat16)
    for i in range(2):
        row = 2 * pair + i
        pieces = []
        for tap in range(S):
            picked = weight_ref[basis_ref[row, tap]].astype(jnp.float32) * value_ref[row, tap]
            pieces.append(picked.astype(jnp.bfloat16))
        pieces.append(eye)
        for k in range(TAPS // 2):
            filt_ref[i, :, k * 2 * G : (k + 1) * 2 * G] = jnp.concatenate(
                [pieces[2 * k], pieces[2 * k + 1]], axis=1
            )
        for tap in range(S):
            fill(i, tap, HALO + i + lat_ref[row, tap], lon_ref[row, tap])
        fill(i, S, HALO + i, 0)
        mixed = jnp.dot(filt_ref[i], taps_ref[i], preferred_element_type=jnp.float32).astype(
            jnp.bfloat16
        )
        for k in range(len(picks)):
            out_refs[k][i * G : (i + 1) * G, :] = mixed[:, k * width : (k + 1) * width]


def conv_rows(pair, supports, fields, edge, weight, chunks, picks, after, roomy):
    own, chans, lon = fields.shape
    width = ceil_to(lon // chunks, LANES)
    highest = (LANES + lon - lon // chunks + DLON) // LANES
    total = (highest + 1) * LANES + width
    arrays = [fields] + ([] if edge is None else [edge]) + [weight]
    return pl.pallas_call(
        functools.partial(conv_kernel, chunks, picks, edge is not None, len(after), pair),
        out_shape=[jax.ShapeDtypeStruct((2 * chans, width), jnp.bfloat16)] * len(picks),
        in_specs=[SMEM] * 4 + [VMEM] * len(arrays) + [ANY] * len(after),
        out_specs=[VMEM] * len(picks),
        scratch_shapes=[
            pltpu.VMEM((own + HALO, chans, total), jnp.bfloat16),
            pltpu.VMEM((2, TAPS * G, len(picks) * width), jnp.bfloat16),
            pltpu.VMEM((2, G, TAPS * G), jnp.bfloat16),
        ],
        compiler_params=params(20),
        cost_estimate=takes(1 if len(picks) > 1 else 0.2),
        name="conv_rows",
    )(*supports, *arrays, *after)


def mlp_kernel(parts, last, after, *rest):
    blocks, rest = rest[:parts], rest[parts:]
    up_ref, down_ref, table_ref, *rest = rest
    rest = rest[after:]
    if last:
        earlier_ref, out_ref, cells_ref = rest
    else:
        out_ref, cells_ref = rest
    width = blocks[0].shape[1]
    place = lax.axis_index("chan")
    for block, k in zip(blocks, [0, *issue_order(parts)]):
        origin = pl.multiple_of(source(place, k, parts) * G, G)
        for i in range(2):
            cells_ref[pl.ds(origin, G), i * width : (i + 1) * width] = block[
                i * G : (i + 1) * G, :
            ]
    values = cells_ref[...].astype(jnp.float32)
    center = values - jnp.mean(values, axis=0, keepdims=True)
    spread = jnp.mean(center * center, axis=0, keepdims=True)
    normed = (center * lax.rsqrt(spread + EPS)).astype(jnp.bfloat16)
    lifted = jnp.dot(up_ref[...], normed, preferred_element_type=jnp.float32)
    scale = math.sqrt(2.0 / math.pi)
    inner = lifted * (scale + (scale * 0.044715) * (lifted * lifted))
    half = 0.5 * lifted
    active = (half + half * jnp.tanh(inner)).astype(jnp.bfloat16)
    lowered = jnp.dot(down_ref[...], active, preferred_element_type=jnp.float32)
    result = (values + lowered).astype(jnp.bfloat16)
    found = []
    for i in range(2):
        modes = lax.dot_general(
            table_ref[place],
            result[:, i * width : (i + 1) * width],
            (((1,), (1,)), ((), ())),
            preferred_element_type=jnp.float32,
        )
        found.append(modes.reshape(modes.shape[0] // SLOT, SLOT, modes.shape[1]))
    block = jnp.concatenate(found, axis=1).astype(jnp.bfloat16)
    if last:
        out_ref[:, 0 : 2 * SLOT, :] = earlier_ref[...]
        out_ref[:, 2 * SLOT : 4 * SLOT, :] = block
    else:
        out_ref[...] = block


def mlp_rows(blocks, up, down, tables, earlier, dests, after):
    pair_chans, width = blocks[0].shape
    chan = len(blocks) * pair_chans // 2
    last = earlier is not None
    arrays = [*blocks, up, down, tables, *after] + ([earlier] if last else [])
    rows = (4 if last else 2) * SLOT
    return pl.pallas_call(
        functools.partial(mlp_kernel, len(blocks), last, len(after)),
        out_shape=jax.ShapeDtypeStruct((dests, rows, chan), jnp.bfloat16),
        in_specs=[VMEM] * (len(blocks) + 3)
        + [ANY] * len(after)
        + [VMEM] * last,
        out_specs=VMEM,
        scratch_shapes=[pltpu.VMEM((chan, 2 * width), jnp.bfloat16)],
        compiler_params=params(20 if dests <= FEW else 40),
        cost_estimate=takes(1),
        name="mlp_rows",
    )(*arrays)


def expand_kernel(legendre_ref, spread_ref, out_ref):
    _, lats, degrees = legendre_ref.shape
    m = pl.program_id(0)
    first = lax.axis_index(("lat", "chan")) * pl.num_programs(0)
    degree = lax.broadcasted_iota(jnp.int32, (lats, degrees), 1)
    kept = jnp.where(degree >= first + m, legendre_ref[0].astype(jnp.float32), 0.0)
    wide = lax.dot_general(
        kept.astype(jnp.bfloat16),
        spread_ref[...],
        (((0,), (0,)), ((), ())),
        preferred_element_type=jnp.float32,
    )
    slot = lax.rem(lax.broadcasted_iota(jnp.int32, wide.shape, 1), SLOT)
    for r in range(2):
        out_ref[0, r] = jnp.where(slot == 2 * m + r, wide, 0.0).astype(jnp.bfloat16)


def expand(legendre, spread):
    modes, lats, degrees = legendre.shape
    depth = spread.shape[1]
    return pl.pallas_call(
        expand_kernel,
        out_shape=jax.ShapeDtypeStruct((modes, 2, degrees, depth), jnp.bfloat16),
        grid=(modes,),
        in_specs=[
            pl.BlockSpec((1, lats, degrees), lambda m: (m, 0, 0)),
            pl.BlockSpec((lats, depth), lambda m: (0, 0)),
        ],
        out_specs=pl.BlockSpec((1, 2, degrees, depth), lambda m: (m, 0, 0, 0)),
        compiler_params=params(10 if depth <= 512 else 48),
        cost_estimate=takes(0.2),
        name="expand",
    )(legendre, spread)


def final_kernel(left_ref, spectrum_ref, out_ref, result_ref, sems):
    modes = left_ref.shape[0]
    chan = spectrum_ref.shape[1]
    copies = []
    for m in range(modes):
        for r in range(2):
            result_ref[m, :, r * chan : (r + 1) * chan] = jnp.dot(
                left_ref[m, r], spectrum_ref[...], preferred_element_type=jnp.float32
            ).astype(jnp.bfloat16)
        copies.append(pltpu.make_async_copy(result_ref.at[m], out_ref.at[m], sems.at[m]))
        copies[-1].start()
    for copy in copies:
        copy.wait()


def final_sum(left, spectrum):
    modes, _, degrees, depth = left.shape
    shape = (modes, degrees, 2 * spectrum.shape[1])
    return pl.pallas_call(
        final_kernel,
        out_shape=jax.ShapeDtypeStruct(shape, jnp.bfloat16),
        in_specs=[VMEM, VMEM],
        out_specs=HBM,
        scratch_shapes=[pltpu.VMEM(shape, jnp.bfloat16), pltpu.SemaphoreType.DMA((modes,))],
        compiler_params=params(8 if depth <= 512 else 48),
        cost_estimate=takes(1),
        name="final_sum",
    )(left, spectrum)


def fourier_blocks(lon, chunks, width, dests, mode_dev):
    chunk = lon // chunks
    index = np.arange(lon, dtype=np.int64)
    mode = np.arange(dests * mode_dev, dtype=np.int64)
    angle = ((mode[:, None] * index[None, :]) % lon) * (2.0 * math.pi / lon)
    paired = np.stack([np.cos(angle), -np.sin(angle)], axis=1) * math.sqrt(2.0 / lon)
    paired = paired.reshape(dests, 2 * mode_dev, chunks, chunk)
    table = np.zeros((chunks, dests, SLOT, width), np.float32)
    table[:, :, : 2 * mode_dev, :chunk] = np.transpose(paired, (2, 0, 1, 3))
    return table.reshape(chunks, dests * SLOT, width).astype(jnp.bfloat16)


def turn(block, axis, count, k):
    return lax.ppermute(block, axis, [(i, target(i, k, count)) for i in range(count)])


def on_device(
    fields,
    disco_weight,
    support_lat,
    support_lon,
    support_basis,
    support_value,
    w_up,
    w_down,
    legendre,
):
    lat_dev, lon, _ = fields.shape
    num_lat = lax.axis_size("lat")
    num_chan = lax.axis_size("chan")
    mode_dev, _, lats = legendre.shape
    dests = num_lat * num_chan
    width = ceil_to(lon // num_chan, LANES)
    supports = (support_lat, support_lon, support_basis, support_value)

    two_bands = num_lat == 2
    cells = jnp.swapaxes(fields, 1, 2)
    if two_bands:
        cells, edge_out = edge_rows(cells)
        edges = [None, lax.ppermute(edge_out, "lat", [(0, 1), (1, 0)])]
        pairs = [lambda: lax.axis_index("lat"), lambda: 1 - lax.axis_index("lat")]
    else:
        ends = num_lat - 1
        edges = [
            lax.ppermute(cells[lat_dev - HALO :], "lat", [(i, i + 1) for i in range(ends)]),
            lax.ppermute(cells[:HALO], "lat", [(i + 1, i) for i in range(ends)]),
        ]
        pairs = [0, 1]

    tables = jnp.asarray(fourier_blocks(lon, num_chan, width, dests, mode_dev))
    up = w_up.T
    down = w_down.T

    depth = dests * 4 * SLOT
    row = np.arange(depth)
    source_band = row // (4 * SLOT) // num_chan
    phase = (row // (2 * SLOT)) % 2
    source_pair = (phase ^ source_band) if two_bands else phase
    lat_of = lat_dev * source_band + 2 * source_pair + (row // SLOT) % 2
    spread = (lat_of[None, :] == np.arange(lats)[:, None]).astype(jnp.bfloat16)
    left = expand(jnp.swapaxes(legendre, 1, 2), jnp.asarray(spread))

    order = issue_order(num_chan)
    halves = [
        (pair, supports, cells, edge, disco_weight, num_chan)
        for edge, pair in zip(edges, pairs)
    ]
    received = []
    for half in halves:
        first = conv_rows(*half, order[:1], [], False)
        rest = conv_rows(*half, [*order[1:], 0], first, False)
        sent = [*first, *rest[:-1]]
        moved = [turn(block, "chan", num_chan, k) for k, block in zip(order, sent)]
        received.append([rest[-1], *moved])
    after = [rest[-1]]
    spectrum = None
    for blocks in received:
        spectrum = mlp_rows(blocks, up, down, tables, spectrum, dests, after)
        after = []

    both = ("lat", "chan")
    gathered = lax.all_to_all(spectrum, both, split_axis=0, concat_axis=0, tiled=True)
    return final_sum(left, gathered.reshape(depth, gathered.shape[2]))


def solution(mesh):
    in_specs = (
        P(("tm", "lat"), None, "chan"),
        P(None, "chan", None),
        P("lat", None),
        P("lat", None),
        P("lat", None),
        P("lat", None),
        P(),
        P(),
        P(("lat", "chan"), None, None),
    )
    out_specs = P(("tm", "lat", "chan"), None, None)
    return jax.shard_map(
        on_device, mesh=mesh, in_specs=in_specs, out_specs=out_specs, check_vma=False
    )
```

```python
import functools
import math

import jax
import jax.numpy as jnp
import numpy as np
from jax import lax
from jax.experimental import pallas as pl
from jax.experimental.pallas import tpu as pltpu
from jax.sharding import PartitionSpec as P

G = 64
S = 9
HALO = 2
DLON = 4
TAPS = S + 1
LANES = 128
SLOT = 8
EPS = 1e-05
FEW = 8
MIB = 1024 * 1024
EDGE_COST = 4
FLOPS_PER_US = 1_000_000_000

SMEM = pl.BlockSpec(memory_space=pltpu.SMEM)
VMEM = pl.BlockSpec(memory_space=pltpu.VMEM)
ANY = pl.BlockSpec(memory_space=pl.ANY)
HBM = pl.BlockSpec(memory_space=pltpu.HBM)


def ceil_to(value, step):
    return -(-value // step) * step


def params(mib):
    return pltpu.CompilerParams(vmem_limit_bytes=mib * MIB)


def takes(micros):
    return pl.CostEstimate(flops=int(micros * FLOPS_PER_US), bytes_accessed=0, transcendentals=0)


def paired(count):
    return count & (count - 1) == 0


def target(place, k, count):
    return place ^ k if paired(count) else (place + k) % count


def source(place, k, count):
    return place ^ k if paired(count) else (place - k + count) % count


def issue_order(count):
    return [*range(2, count), 1] if paired(count) else list(range(1, count))


def edge_kernel(fields_ref, same_ref, out_ref):
    start = HALO * (1 - lax.axis_index("lat"))
    for k in range(HALO):
        out_ref[k] = fields_ref[start + k]
    same_ref[...] = fields_ref[...]


def edge_rows(fields):
    shapes = [fields.shape, (HALO, *fields.shape[1:])]
    return pl.pallas_call(
        edge_kernel,
        out_shape=[jax.ShapeDtypeStruct(shape, fields.dtype) for shape in shapes],
        in_specs=[VMEM],
        out_specs=[VMEM] * 2,
        compiler_params=params(8),
        cost_estimate=takes(EDGE_COST),
        name="edge_rows",
    )(fields)


def conv_kernel(
    chunks, picks, has_edge, after, flip, lat_ref, lon_ref, basis_ref, value_ref, fields_ref, *rest
):
    if has_edge:
        edge_ref, weight_ref, *rest = rest
    else:
        edge_ref, (weight_ref, *rest) = None, rest
    *out_refs, rows_ref, taps_ref, filt_ref = rest[after:]
    own, _, lon = fields_ref.shape
    chunk = lon // chunks
    width = out_refs[0].shape[1]
    total = rows_ref.shape[2]
    pair = flip if isinstance(flip, int) else flip()
    own_at = HALO * (1 - pair)
    edge_at = own * pair

    def put(slot, cells):
        rows_ref[slot, :, LANES : LANES + lon] = cells
        rows_ref[slot, :, 0:LANES] = cells[:, lon - LANES :]
        full = (lon // LANES) * LANES
        tail = total - LANES - lon
        rows_ref[slot, :, LANES + full :] = jnp.concatenate(
            [cells[:, full:], cells[:, :tail]], axis=1
        )

    for row in range(own):
        put(own_at + row, fields_ref[row])
    for row in range(HALO):
        if has_edge:
            put(edge_at + row, edge_ref[row])
        else:
            rows_ref[edge_at + row] = jnp.zeros(rows_ref.shape[1:], rows_ref.dtype)

    lane = lax.broadcasted_iota(jnp.int32, (G, LANES), 1)
    begins = [LANES + chunk * target(lax.axis_index("chan"), k, chunks) for k in picks]

    def fill(slot, tap, source, offset):
        for k, origin in enumerate(begins):
            begin = origin + offset
            first = lax.div(begin, LANES)
            shift = lax.rem(begin, LANES)
            back = lax.rem(LANES - shift, LANES)
            keep = lane < LANES - shift
            turned = []
            for t in range(width // LANES + 1):
                start = pl.multiple_of((first + t) * LANES, LANES)
                tile = rows_ref[source, :, pl.ds(start, LANES)]
                turned.append(pltpu.roll(tile, back, 1))
            for t in range(width // LANES):
                at = k * width + t * LANES
                taps_ref[slot, tap * G : (tap + 1) * G, at : at + LANES] = jnp.where(
                    keep, turned[t], turned[t + 1]
                )

    eye = jnp.where(
        lax.broadcasted_iota(jnp.int32, (G, G), 0) == lax.broadcasted_iota(jnp.int32, (G, G), 1),
        1.0,
        0.0,
    ).astype(jnp.bfloat16)
    for i in range(2):
        row = 2 * pair + i
        pieces = []
        for tap in range(S):
            picked = weight_ref[basis_ref[row, tap]].astype(jnp.float32) * value_ref[row, tap]
            pieces.append(picked.astype(jnp.bfloat16))
        pieces.append(eye)
        for k in range(TAPS // 2):
            filt_ref[i, :, k * 2 * G : (k + 1) * 2 * G] = jnp.concatenate(
                [pieces[2 * k], pieces[2 * k + 1]], axis=1
            )
        for tap in range(S):
            fill(i, tap, HALO + i + lat_ref[row, tap], lon_ref[row, tap])
        fill(i, S, HALO + i, 0)
        mixed = jnp.dot(filt_ref[i], taps_ref[i], preferred_element_type=jnp.float32).astype(
            jnp.bfloat16
        )
        for k in range(len(picks)):
            out_refs[k][i * G : (i + 1) * G, :] = mixed[:, k * width : (k + 1) * width]


def conv_rows(pair, supports, fields, edge, weight, chunks, picks, after, roomy):
    own, chans, lon = fields.shape
    width = ceil_to(lon // chunks, LANES)
    highest = (LANES + lon - lon // chunks + DLON) // LANES
    total = (highest + 1) * LANES + width
    arrays = [fields] + ([] if edge is None else [edge]) + [weight]
    return pl.pallas_call(
        functools.partial(conv_kernel, chunks, picks, edge is not None, len(after), pair),
        out_shape=[jax.ShapeDtypeStruct((2 * chans, width), jnp.bfloat16)] * len(picks),
        in_specs=[SMEM] * 4 + [VMEM] * len(arrays) + [ANY] * len(after),
        out_specs=[VMEM] * len(picks),
        scratch_shapes=[
            pltpu.VMEM((own + HALO, chans, total), jnp.bfloat16),
            pltpu.VMEM((2, TAPS * G, len(picks) * width), jnp.bfloat16),
            pltpu.VMEM((2, G, TAPS * G), jnp.bfloat16),
        ],
        compiler_params=params(20),
        cost_estimate=takes(1 if len(picks) > 1 else 0.2),
        name="conv_rows",
    )(*supports, *arrays, *after)


def mlp_kernel(parts, last, after, *rest):
    blocks, rest = rest[:parts], rest[parts:]
    up_ref, down_ref, table_ref, *rest = rest
    rest = rest[after:]
    if last:
        earlier_ref, out_ref, cells_ref = rest
    else:
        out_ref, cells_ref = rest
    width = blocks[0].shape[1]
    place = lax.axis_index("chan")
    for block, k in zip(blocks, [0, *issue_order(parts)]):
        origin = pl.multiple_of(source(place, k, parts) * G, G)
        for i in range(2):
            cells_ref[pl.ds(origin, G), i * width : (i + 1) * width] = block[
                i * G : (i + 1) * G, :
            ]
    values = cells_ref[...].astype(jnp.float32)
    center = values - jnp.mean(values, axis=0, keepdims=True)
    spread = jnp.mean(center * center, axis=0, keepdims=True)
    normed = (center * lax.rsqrt(spread + EPS)).astype(jnp.bfloat16)
    lifted = jnp.dot(up_ref[...], normed, preferred_element_type=jnp.float32)
    scale = math.sqrt(2.0 / math.pi)
    inner = lifted * (scale + (scale * 0.044715) * (lifted * lifted))
    half = 0.5 * lifted
    active = (half + half * jnp.tanh(inner)).astype(jnp.bfloat16)
    lowered = jnp.dot(down_ref[...], active, preferred_element_type=jnp.float32)
    result = (values + lowered).astype(jnp.bfloat16)
    found = []
    for i in range(2):
        modes = lax.dot_general(
            table_ref[place],
            result[:, i * width : (i + 1) * width],
            (((1,), (1,)), ((), ())),
            preferred_element_type=jnp.float32,
        )
        found.append(modes.reshape(modes.shape[0] // SLOT, SLOT, modes.shape[1]))
    block = jnp.concatenate(found, axis=1).astype(jnp.bfloat16)
    if last:
        out_ref[:, 0 : 2 * SLOT, :] = earlier_ref[...]
        out_ref[:, 2 * SLOT : 4 * SLOT, :] = block
    else:
        out_ref[...] = block


def mlp_rows(blocks, up, down, tables, earlier, dests, after):
    pair_chans, width = blocks[0].shape
    chan = len(blocks) * pair_chans // 2
    last = earlier is not None
    arrays = [*blocks, up, down, tables, *after] + ([earlier] if last else [])
    rows = (4 if last else 2) * SLOT
    return pl.pallas_call(
        functools.partial(mlp_kernel, len(blocks), last, len(after)),
        out_shape=jax.ShapeDtypeStruct((dests, rows, chan), jnp.bfloat16),
        in_specs=[VMEM] * (len(blocks) + 3)
        + [ANY] * len(after)
        + [VMEM] * last,
        out_specs=VMEM,
        scratch_shapes=[pltpu.VMEM((chan, 2 * width), jnp.bfloat16)],
        compiler_params=params(20 if dests <= FEW else 40),
        cost_estimate=takes(1),
        name="mlp_rows",
    )(*arrays)


def expand_kernel(legendre_ref, spread_ref, out_ref):
    _, lats, degrees = legendre_ref.shape
    m = pl.program_id(0)
    first = lax.axis_index(("lat", "chan")) * pl.num_programs(0)
    degree = lax.broadcasted_iota(jnp.int32, (lats, degrees), 1)
    kept = jnp.where(degree >= first + m, legendre_ref[0].astype(jnp.float32), 0.0)
    wide = lax.dot_general(
        kept.astype(jnp.bfloat16),
        spread_ref[...],
        (((0,), (0,)), ((), ())),
        preferred_element_type=jnp.float32,
    )
    slot = lax.rem(lax.broadcasted_iota(jnp.int32, wide.shape, 1), SLOT)
    for r in range(2):
        out_ref[0, r] = jnp.where(slot == 2 * m + r, wide, 0.0).astype(jnp.bfloat16)


def expand(legendre, spread):
    modes, lats, degrees = legendre.shape
    depth = spread.shape[1]
    return pl.pallas_call(
        expand_kernel,
        out_shape=jax.ShapeDtypeStruct((modes, 2, degrees, depth), jnp.bfloat16),
        grid=(modes,),
        in_specs=[
            pl.BlockSpec((1, lats, degrees), lambda m: (m, 0, 0)),
            pl.BlockSpec((lats, depth), lambda m: (0, 0)),
        ],
        out_specs=pl.BlockSpec((1, 2, degrees, depth), lambda m: (m, 0, 0, 0)),
        compiler_params=params(10 if depth <= 512 else 48),
        cost_estimate=takes(0.2),
        name="expand",
    )(legendre, spread)


def final_kernel(left_ref, spectrum_ref, out_ref, result_ref, sems):
    modes = left_ref.shape[0]
    chan = spectrum_ref.shape[1]
    copies = []
    for m in range(modes):
        for r in range(2):
            result_ref[m, :, r * chan : (r + 1) * chan] = jnp.dot(
                left_ref[m, r], spectrum_ref[...], preferred_element_type=jnp.float32
            ).astype(jnp.bfloat16)
        copies.append(pltpu.make_async_copy(result_ref.at[m], out_ref.at[m], sems.at[m]))
        copies[-1].start()
    for copy in copies:
        copy.wait()


def final_sum(left, spectrum):
    modes, _, degrees, depth = left.shape
    shape = (modes, degrees, 2 * spectrum.shape[1])
    return pl.pallas_call(
        final_kernel,
        out_shape=jax.ShapeDtypeStruct(shape, jnp.bfloat16),
        in_specs=[VMEM, VMEM],
        out_specs=HBM,
        scratch_shapes=[pltpu.VMEM(shape, jnp.bfloat16), pltpu.SemaphoreType.DMA((modes,))],
        compiler_params=params(8 if depth <= 512 else 48),
        cost_estimate=takes(1),
        name="final_sum",
    )(left, spectrum)


def fourier_blocks(lon, chunks, width, dests, mode_dev):
    chunk = lon // chunks
    index = np.arange(lon, dtype=np.int64)
    mode = np.arange(dests * mode_dev, dtype=np.int64)
    angle = ((mode[:, None] * index[None, :]) % lon) * (2.0 * math.pi / lon)
    paired = np.stack([np.cos(angle), -np.sin(angle)], axis=1) * math.sqrt(2.0 / lon)
    paired = paired.reshape(dests, 2 * mode_dev, chunks, chunk)
    table = np.zeros((chunks, dests, SLOT, width), np.float32)
    table[:, :, : 2 * mode_dev, :chunk] = np.transpose(paired, (2, 0, 1, 3))
    return table.reshape(chunks, dests * SLOT, width).astype(jnp.bfloat16)


def turn(block, axis, count, k):
    return lax.ppermute(block, axis, [(i, target(i, k, count)) for i in range(count)])


def on_device(
    fields,
    disco_weight,
    support_lat,
    support_lon,
    support_basis,
    support_value,
    w_up,
    w_down,
    legendre,
):
    lat_dev, lon, _ = fields.shape
    num_lat = lax.axis_size("lat")
    num_chan = lax.axis_size("chan")
    mode_dev, _, lats = legendre.shape
    dests = num_lat * num_chan
    width = ceil_to(lon // num_chan, LANES)
    supports = (support_lat, support_lon, support_basis, support_value)

    two_bands = num_lat == 2
    cells = jnp.swapaxes(fields, 1, 2)
    if two_bands:
        cells, edge_out = edge_rows(cells)
        edges = [None, lax.ppermute(edge_out, "lat", [(0, 1), (1, 0)])]
        pairs = [lambda: lax.axis_index("lat"), lambda: 1 - lax.axis_index("lat")]
    else:
        ends = num_lat - 1
        edges = [
            lax.ppermute(cells[lat_dev - HALO :], "lat", [(i, i + 1) for i in range(ends)]),
            lax.ppermute(cells[:HALO], "lat", [(i + 1, i) for i in range(ends)]),
        ]
        pairs = [0, 1]

    tables = jnp.asarray(fourier_blocks(lon, num_chan, width, dests, mode_dev))
    up = w_up.T
    down = w_down.T

    depth = dests * 4 * SLOT
    row = np.arange(depth)
    source_band = row // (4 * SLOT) // num_chan
    phase = (row // (2 * SLOT)) % 2
    source_pair = (phase ^ source_band) if two_bands else phase
    lat_of = lat_dev * source_band + 2 * source_pair + (row // SLOT) % 2
    spread = (lat_of[None, :] == np.arange(lats)[:, None]).astype(jnp.bfloat16)
    left = expand(jnp.swapaxes(legendre, 1, 2), jnp.asarray(spread))

    order = issue_order(num_chan)
    halves = [
        (pair, supports, cells, edge, disco_weight, num_chan)
        for edge, pair in zip(edges, pairs)
    ]
    received = []
    for half in halves:
        if received:
            sent = conv_rows(*half, order, [], False)
            kept = conv_rows(*half, [0], sent[1:2], False)
        else:
            first = conv_rows(*half, order[:1], [], False)
            *rest, own = conv_rows(*half, [*order[1:], 0], first, False)
            sent, kept = [*first, *rest], [own]
        moved = [turn(block, "chan", num_chan, k) for k, block in zip(order, sent)]
        received.append([*kept, *moved])
    after = [*kept]
    spectrum = None
    for blocks in received:
        spectrum = mlp_rows(blocks, up, down, tables, spectrum, dests, after)
        after = []

    both = ("lat", "chan")
    gathered = lax.all_to_all(spectrum, both, split_axis=0, concat_axis=0, tiled=True)
    return final_sum(left, gathered.reshape(depth, gathered.shape[2]))


def solution(mesh):
    in_specs = (
        P(("tm", "lat"), None, "chan"),
        P(None, "chan", None),
        P("lat", None),
        P("lat", None),
        P("lat", None),
        P("lat", None),
        P(),
        P(),
        P(("lat", "chan"), None, None),
    )
    out_specs = P(("tm", "lat", "chan"), None, None)
    return jax.shard_map(
        on_device, mesh=mesh, in_specs=in_specs, out_specs=out_specs, check_vma=False
    )
```

```python
import functools
import math

import jax
import jax.numpy as jnp
import numpy as np
from jax import lax
from jax.experimental import pallas as pl
from jax.experimental.pallas import tpu as pltpu
from jax.sharding import PartitionSpec as P

G = 64
S = 9
HALO = 2
DLON = 4
TAPS = S + 1
LANES = 128
SLOT = 8
EPS = 1e-05
FEW = 8
MIB = 1024 * 1024
EDGE_COST = 4
FLOPS_PER_US = 1_000_000_000

SMEM = pl.BlockSpec(memory_space=pltpu.SMEM)
VMEM = pl.BlockSpec(memory_space=pltpu.VMEM)
ANY = pl.BlockSpec(memory_space=pl.ANY)
HBM = pl.BlockSpec(memory_space=pltpu.HBM)


def ceil_to(value, step):
    return -(-value // step) * step


def params(mib):
    return pltpu.CompilerParams(vmem_limit_bytes=mib * MIB)


def takes(micros):
    return pl.CostEstimate(flops=int(micros * FLOPS_PER_US), bytes_accessed=0, transcendentals=0)


def paired(count):
    return count & (count - 1) == 0


def target(place, k, count):
    return place ^ k if paired(count) else (place + k) % count


def source(place, k, count):
    return place ^ k if paired(count) else (place - k + count) % count


def issue_order(count):
    return [*range(2, count), 1] if paired(count) else list(range(1, count))


def edge_kernel(fields_ref, same_ref, out_ref):
    start = HALO * (1 - lax.axis_index("lat"))
    for k in range(HALO):
        out_ref[k] = fields_ref[start + k]
    same_ref[...] = fields_ref[...]


def edge_rows(fields):
    shapes = [fields.shape, (HALO, *fields.shape[1:])]
    return pl.pallas_call(
        edge_kernel,
        out_shape=[jax.ShapeDtypeStruct(shape, fields.dtype) for shape in shapes],
        in_specs=[VMEM],
        out_specs=[VMEM] * 2,
        compiler_params=params(8),
        cost_estimate=takes(EDGE_COST),
        name="edge_rows",
    )(fields)


def conv_kernel(
    chunks, picks, has_edge, after, flip, lat_ref, lon_ref, basis_ref, value_ref, fields_ref, *rest
):
    if has_edge:
        edge_ref, weight_ref, *rest = rest
    else:
        edge_ref, (weight_ref, *rest) = None, rest
    *out_refs, rows_ref, taps_ref, filt_ref = rest[after:]
    own, _, lon = fields_ref.shape
    chunk = lon // chunks
    width = out_refs[0].shape[1]
    total = rows_ref.shape[2]
    pair = flip if isinstance(flip, int) else flip()
    own_at = HALO * (1 - pair)
    edge_at = own * pair

    def put(slot, cells):
        rows_ref[slot, :, LANES : LANES + lon] = cells
        rows_ref[slot, :, 0:LANES] = cells[:, lon - LANES :]
        full = (lon // LANES) * LANES
        tail = total - LANES - lon
        rows_ref[slot, :, LANES + full :] = jnp.concatenate(
            [cells[:, full:], cells[:, :tail]], axis=1
        )

    for row in range(own):
        put(own_at + row, fields_ref[row])
    for row in range(HALO):
        if has_edge:
            put(edge_at + row, edge_ref[row])
        else:
            rows_ref[edge_at + row] = jnp.zeros(rows_ref.shape[1:], rows_ref.dtype)

    lane = lax.broadcasted_iota(jnp.int32, (G, LANES), 1)
    begins = [LANES + chunk * target(lax.axis_index("chan"), k, chunks) for k in picks]

    def fill(slot, tap, source, offset):
        for k, origin in enumerate(begins):
            begin = origin + offset
            first = lax.div(begin, LANES)
            shift = lax.rem(begin, LANES)
            back = lax.rem(LANES - shift, LANES)
            keep = lane < LANES - shift
            turned = []
            for t in range(width // LANES + 1):
                start = pl.multiple_of((first + t) * LANES, LANES)
                tile = rows_ref[source, :, pl.ds(start, LANES)]
                turned.append(pltpu.roll(tile, back, 1))
            for t in range(width // LANES):
                at = k * width + t * LANES
                taps_ref[slot, tap * G : (tap + 1) * G, at : at + LANES] = jnp.where(
                    keep, turned[t], turned[t + 1]
                )

    eye = jnp.where(
        lax.broadcasted_iota(jnp.int32, (G, G), 0) == lax.broadcasted_iota(jnp.int32, (G, G), 1),
        1.0,
        0.0,
    ).astype(jnp.bfloat16)
    for i in range(2):
        row = 2 * pair + i
        pieces = []
        for tap in range(S):
            picked = weight_ref[basis_ref[row, tap]].astype(jnp.float32) * value_ref[row, tap]
            pieces.append(picked.astype(jnp.bfloat16))
        pieces.append(eye)
        for k in range(TAPS // 2):
            filt_ref[i, :, k * 2 * G : (k + 1) * 2 * G] = jnp.concatenate(
                [pieces[2 * k], pieces[2 * k + 1]], axis=1
            )
        for tap in range(S):
            fill(i, tap, HALO + i + lat_ref[row, tap], lon_ref[row, tap])
        fill(i, S, HALO + i, 0)
        mixed = jnp.dot(filt_ref[i], taps_ref[i], preferred_element_type=jnp.float32).astype(
            jnp.bfloat16
        )
        for k in range(len(picks)):
            out_refs[k][i * G : (i + 1) * G, :] = mixed[:, k * width : (k + 1) * width]


def conv_rows(pair, supports, fields, edge, weight, chunks, picks, after, roomy):
    own, chans, lon = fields.shape
    width = ceil_to(lon // chunks, LANES)
    highest = (LANES + lon - lon // chunks + DLON) // LANES
    total = (highest + 1) * LANES + width
    arrays = [fields] + ([] if edge is None else [edge]) + [weight]
    return pl.pallas_call(
        functools.partial(conv_kernel, chunks, picks, edge is not None, len(after), pair),
        out_shape=[jax.ShapeDtypeStruct((2 * chans, width), jnp.bfloat16)] * len(picks),
        in_specs=[SMEM] * 4 + [VMEM] * len(arrays) + [ANY] * len(after),
        out_specs=[VMEM] * len(picks),
        scratch_shapes=[
            pltpu.VMEM((own + HALO, chans, total), jnp.bfloat16),
            pltpu.VMEM((2, TAPS * G, len(picks) * width), jnp.bfloat16),
            pltpu.VMEM((2, G, TAPS * G), jnp.bfloat16),
        ],
        compiler_params=params(20),
        cost_estimate=takes(1 if len(picks) > 1 else 0.2),
        name="conv_rows",
    )(*supports, *arrays, *after)


def mlp_kernel(parts, last, after, *rest):
    blocks, rest = rest[:parts], rest[parts:]
    up_ref, down_ref, table_ref, *rest = rest
    rest = rest[after:]
    if last:
        earlier_ref, out_ref, cells_ref = rest
    else:
        out_ref, cells_ref = rest
    width = blocks[0].shape[1]
    place = lax.axis_index("chan")
    for block, k in zip(blocks, [0, *issue_order(parts)]):
        origin = pl.multiple_of(source(place, k, parts) * G, G)
        for i in range(2):
            cells_ref[pl.ds(origin, G), i * width : (i + 1) * width] = block[
                i * G : (i + 1) * G, :
            ]
    values = cells_ref[...].astype(jnp.float32)
    center = values - jnp.mean(values, axis=0, keepdims=True)
    spread = jnp.mean(center * center, axis=0, keepdims=True)
    normed = (center * lax.rsqrt(spread + EPS)).astype(jnp.bfloat16)
    lifted = jnp.dot(up_ref[...], normed, preferred_element_type=jnp.float32)
    scale = math.sqrt(2.0 / math.pi)
    inner = lifted * (scale + (scale * 0.044715) * (lifted * lifted))
    half = 0.5 * lifted
    active = (half + half * jnp.tanh(inner)).astype(jnp.bfloat16)
    lowered = jnp.dot(down_ref[...], active, preferred_element_type=jnp.float32)
    result = (values + lowered).astype(jnp.bfloat16)
    found = []
    for i in range(2):
        modes = lax.dot_general(
            table_ref[place],
            result[:, i * width : (i + 1) * width],
            (((1,), (1,)), ((), ())),
            preferred_element_type=jnp.float32,
        )
        found.append(modes.reshape(modes.shape[0] // SLOT, SLOT, modes.shape[1]))
    block = jnp.concatenate(found, axis=1).astype(jnp.bfloat16)
    if last:
        out_ref[:, 0 : 2 * SLOT, :] = earlier_ref[...]
        out_ref[:, 2 * SLOT : 4 * SLOT, :] = block
    else:
        out_ref[...] = block


def mlp_rows(blocks, up, down, tables, earlier, dests, after):
    pair_chans, width = blocks[0].shape
    chan = len(blocks) * pair_chans // 2
    last = earlier is not None
    arrays = [*blocks, up, down, tables, *after] + ([earlier] if last else [])
    rows = (4 if last else 2) * SLOT
    return pl.pallas_call(
        functools.partial(mlp_kernel, len(blocks), last, len(after)),
        out_shape=jax.ShapeDtypeStruct((dests, rows, chan), jnp.bfloat16),
        in_specs=[VMEM] * (len(blocks) + 3)
        + [ANY] * len(after)
        + [VMEM] * last,
        out_specs=VMEM,
        scratch_shapes=[pltpu.VMEM((chan, 2 * width), jnp.bfloat16)],
        compiler_params=params(20 if dests <= FEW else 40),
        cost_estimate=takes(1),
        name="mlp_rows",
    )(*arrays)


def expand_kernel(legendre_ref, spread_ref, out_ref):
    _, lats, degrees = legendre_ref.shape
    m = pl.program_id(0)
    first = lax.axis_index(("lat", "chan")) * pl.num_programs(0)
    degree = lax.broadcasted_iota(jnp.int32, (lats, degrees), 1)
    kept = jnp.where(degree >= first + m, legendre_ref[0].astype(jnp.float32), 0.0)
    wide = lax.dot_general(
        kept.astype(jnp.bfloat16),
        spread_ref[...],
        (((0,), (0,)), ((), ())),
        preferred_element_type=jnp.float32,
    )
    slot = lax.rem(lax.broadcasted_iota(jnp.int32, wide.shape, 1), SLOT)
    for r in range(2):
        out_ref[0, r] = jnp.where(slot == 2 * m + r, wide, 0.0).astype(jnp.bfloat16)


def expand(legendre, spread):
    modes, lats, degrees = legendre.shape
    depth = spread.shape[1]
    return pl.pallas_call(
        expand_kernel,
        out_shape=jax.ShapeDtypeStruct((modes, 2, degrees, depth), jnp.bfloat16),
        grid=(modes,),
        in_specs=[
            pl.BlockSpec((1, lats, degrees), lambda m: (m, 0, 0)),
            pl.BlockSpec((lats, depth), lambda m: (0, 0)),
        ],
        out_specs=pl.BlockSpec((1, 2, degrees, depth), lambda m: (m, 0, 0, 0)),
        compiler_params=params(10 if depth <= 512 else 48),
        cost_estimate=takes(0.2),
        name="expand",
    )(legendre, spread)


def final_kernel(left_ref, spectrum_ref, out_ref, result_ref, sems):
    modes = left_ref.shape[0]
    chan = spectrum_ref.shape[1]
    copies = []
    for m in range(modes):
        for r in range(2):
            result_ref[m, :, r * chan : (r + 1) * chan] = jnp.dot(
                left_ref[m, r], spectrum_ref[...], preferred_element_type=jnp.float32
            ).astype(jnp.bfloat16)
        copies.append(pltpu.make_async_copy(result_ref.at[m], out_ref.at[m], sems.at[m]))
        copies[-1].start()
    for copy in copies:
        copy.wait()


def final_sum(left, spectrum):
    modes, _, degrees, depth = left.shape
    shape = (modes, degrees, 2 * spectrum.shape[1])
    return pl.pallas_call(
        final_kernel,
        out_shape=jax.ShapeDtypeStruct(shape, jnp.bfloat16),
        in_specs=[VMEM, VMEM],
        out_specs=HBM,
        scratch_shapes=[pltpu.VMEM(shape, jnp.bfloat16), pltpu.SemaphoreType.DMA((modes,))],
        compiler_params=params(8 if depth <= 512 else 48),
        cost_estimate=takes(1),
        name="final_sum",
    )(left, spectrum)


def fourier_blocks(lon, chunks, width, dests, mode_dev):
    chunk = lon // chunks
    index = np.arange(lon, dtype=np.int64)
    mode = np.arange(dests * mode_dev, dtype=np.int64)
    angle = ((mode[:, None] * index[None, :]) % lon) * (2.0 * math.pi / lon)
    paired = np.stack([np.cos(angle), -np.sin(angle)], axis=1) * math.sqrt(2.0 / lon)
    paired = paired.reshape(dests, 2 * mode_dev, chunks, chunk)
    table = np.zeros((chunks, dests, SLOT, width), np.float32)
    table[:, :, : 2 * mode_dev, :chunk] = np.transpose(paired, (2, 0, 1, 3))
    return table.reshape(chunks, dests * SLOT, width).astype(jnp.bfloat16)


def turn(block, axis, count, k):
    return lax.ppermute(block, axis, [(i, target(i, k, count)) for i in range(count)])


def on_device(
    fields,
    disco_weight,
    support_lat,
    support_lon,
    support_basis,
    support_value,
    w_up,
    w_down,
    legendre,
):
    lat_dev, lon, _ = fields.shape
    num_lat = lax.axis_size("lat")
    num_chan = lax.axis_size("chan")
    mode_dev, _, lats = legendre.shape
    dests = num_lat * num_chan
    width = ceil_to(lon // num_chan, LANES)
    supports = (support_lat, support_lon, support_basis, support_value)

    two_bands = num_lat == 2
    cells = jnp.swapaxes(fields, 1, 2)
    if two_bands:
        cells, edge_out = edge_rows(cells)
        edges = [None, lax.ppermute(edge_out, "lat", [(0, 1), (1, 0)])]
        pairs = [lambda: lax.axis_index("lat"), lambda: 1 - lax.axis_index("lat")]
    else:
        ends = num_lat - 1
        edges = [
            lax.ppermute(cells[lat_dev - HALO :], "lat", [(i, i + 1) for i in range(ends)]),
            lax.ppermute(cells[:HALO], "lat", [(i + 1, i) for i in range(ends)]),
        ]
        pairs = [0, 1]

    tables = jnp.asarray(fourier_blocks(lon, num_chan, width, dests, mode_dev))
    up = w_up.T
    down = w_down.T

    depth = dests * 4 * SLOT
    row = np.arange(depth)
    source_band = row // (4 * SLOT) // num_chan
    phase = (row // (2 * SLOT)) % 2
    source_pair = (phase ^ source_band) if two_bands else phase
    lat_of = lat_dev * source_band + 2 * source_pair + (row // SLOT) % 2
    spread = (lat_of[None, :] == np.arange(lats)[:, None]).astype(jnp.bfloat16)
    left = expand(jnp.swapaxes(legendre, 1, 2), jnp.asarray(spread))

    order = issue_order(num_chan)
    halves = [
        (pair, supports, cells, edge, disco_weight, num_chan)
        for edge, pair in zip(edges, pairs)
    ]
    received = []
    after, last = [], []
    for half in halves:
        sent = conv_rows(*half, order, after, False)
        moved = [turn(block, "chan", num_chan, k) for k, block in zip(order, sent)]
        after = conv_rows(*half, [0], [sent[1], *last], False)
        received.append([*after, *moved])
        after, last = list(after), moved[:1]
    spectrum = None
    for blocks in received:
        spectrum = mlp_rows(blocks, up, down, tables, spectrum, dests, list(after))
        after = []

    both = ("lat", "chan")
    gathered = lax.all_to_all(spectrum, both, split_axis=0, concat_axis=0, tiled=True)
    return final_sum(left, gathered.reshape(depth, gathered.shape[2]))


def solution(mesh):
    in_specs = (
        P(("tm", "lat"), None, "chan"),
        P(None, "chan", None),
        P("lat", None),
        P("lat", None),
        P("lat", None),
        P("lat", None),
        P(),
        P(),
        P(("lat", "chan"), None, None),
    )
    out_specs = P(("tm", "lat", "chan"), None, None)
    return jax.shard_map(
        on_device, mesh=mesh, in_specs=in_specs, out_specs=out_specs, check_vma=False
    )
```

```python
import functools
import math

import jax
import jax.numpy as jnp
import numpy as np
from jax import lax
from jax.experimental import pallas as pl
from jax.experimental.pallas import tpu as pltpu
from jax.sharding import PartitionSpec as P

G = 64
S = 9
HALO = 2
DLON = 4
TAPS = S + 1
LANES = 128
SLOT = 8
EPS = 1e-05
FEW = 8
MIB = 1024 * 1024
EDGE_COST = 4
COLUMNS = 256
FLOPS_PER_US = 1_000_000_000

SMEM = pl.BlockSpec(memory_space=pltpu.SMEM)
VMEM = pl.BlockSpec(memory_space=pltpu.VMEM)
ANY = pl.BlockSpec(memory_space=pl.ANY)
HBM = pl.BlockSpec(memory_space=pltpu.HBM)


def ceil_to(value, step):
    return -(-value // step) * step


def params(mib):
    return pltpu.CompilerParams(vmem_limit_bytes=mib * MIB)


def takes(micros):
    return pl.CostEstimate(flops=int(micros * FLOPS_PER_US), bytes_accessed=0, transcendentals=0)


def paired(count):
    return count & (count - 1) == 0


def target(place, k, count):
    return place ^ k if paired(count) else (place + k) % count


def source(place, k, count):
    return place ^ k if paired(count) else (place - k + count) % count


def issue_order(count):
    return [*range(2, count), 1] if paired(count) else list(range(1, count))


def edge_kernel(fields_ref, same_ref, out_ref):
    start = HALO * (1 - lax.axis_index("lat"))
    for k in range(HALO):
        out_ref[k] = fields_ref[start + k]
    same_ref[...] = fields_ref[...]


def edge_rows(fields):
    shapes = [fields.shape, (HALO, *fields.shape[1:])]
    return pl.pallas_call(
        edge_kernel,
        out_shape=[jax.ShapeDtypeStruct(shape, fields.dtype) for shape in shapes],
        in_specs=[VMEM],
        out_specs=[VMEM] * 2,
        compiler_params=params(8),
        cost_estimate=takes(EDGE_COST),
        name="edge_rows",
    )(fields)


def conv_kernel(
    chunks, picks, has_edge, after, flip, lat_ref, lon_ref, basis_ref, value_ref, fields_ref, *rest
):
    if has_edge:
        edge_ref, weight_ref, *rest = rest
    else:
        edge_ref, (weight_ref, *rest) = None, rest
    *out_refs, rows_ref, taps_ref, filt_ref = rest[after:]
    own, _, lon = fields_ref.shape
    chunk = lon // chunks
    width = out_refs[0].shape[1]
    total = rows_ref.shape[2]
    pair = flip if isinstance(flip, int) else flip()
    own_at = HALO * (1 - pair)
    edge_at = own * pair

    def put(slot, cells):
        rows_ref[slot, :, LANES : LANES + lon] = cells
        rows_ref[slot, :, 0:LANES] = cells[:, lon - LANES :]
        full = (lon // LANES) * LANES
        tail = total - LANES - lon
        rows_ref[slot, :, LANES + full :] = jnp.concatenate(
            [cells[:, full:], cells[:, :tail]], axis=1
        )

    for row in range(own):
        put(own_at + row, fields_ref[row])
    for row in range(HALO):
        if has_edge:
            put(edge_at + row, edge_ref[row])
        else:
            rows_ref[edge_at + row] = jnp.zeros(rows_ref.shape[1:], rows_ref.dtype)

    lane = lax.broadcasted_iota(jnp.int32, (G, LANES), 1)
    begins = [LANES + chunk * target(lax.axis_index("chan"), k, chunks) for k in picks]

    def fill(slot, tap, source, offset):
        for k, origin in enumerate(begins):
            begin = origin + offset
            first = lax.div(begin, LANES)
            shift = lax.rem(begin, LANES)
            back = lax.rem(LANES - shift, LANES)
            keep = lane < LANES - shift
            turned = []
            for t in range(width // LANES + 1):
                start = pl.multiple_of((first + t) * LANES, LANES)
                tile = rows_ref[source, :, pl.ds(start, LANES)]
                turned.append(pltpu.roll(tile, back, 1))
            for t in range(width // LANES):
                at = k * width + t * LANES
                taps_ref[slot, tap * G : (tap + 1) * G, at : at + LANES] = jnp.where(
                    keep, turned[t], turned[t + 1]
                )

    eye = jnp.where(
        lax.broadcasted_iota(jnp.int32, (G, G), 0) == lax.broadcasted_iota(jnp.int32, (G, G), 1),
        1.0,
        0.0,
    ).astype(jnp.bfloat16)
    for i in range(2):
        row = 2 * pair + i
        pieces = []
        for tap in range(S):
            picked = weight_ref[basis_ref[row, tap]].astype(jnp.float32) * value_ref[row, tap]
            pieces.append(picked.astype(jnp.bfloat16))
        pieces.append(eye)
        for k in range(TAPS // 2):
            filt_ref[i, :, k * 2 * G : (k + 1) * 2 * G] = jnp.concatenate(
                [pieces[2 * k], pieces[2 * k + 1]], axis=1
            )
        for tap in range(S):
            fill(i, tap, HALO + i + lat_ref[row, tap], lon_ref[row, tap])
        fill(i, S, HALO + i, 0)
        mixed = jnp.dot(filt_ref[i], taps_ref[i], preferred_element_type=jnp.float32).astype(
            jnp.bfloat16
        )
        for k in range(len(picks)):
            out_refs[k][i * G : (i + 1) * G, :] = mixed[:, k * width : (k + 1) * width]


def conv_rows(pair, supports, fields, edge, weight, chunks, picks, after, roomy):
    own, chans, lon = fields.shape
    width = ceil_to(lon // chunks, LANES)
    highest = (LANES + lon - lon // chunks + DLON) // LANES
    total = (highest + 1) * LANES + width
    arrays = [fields] + ([] if edge is None else [edge]) + [weight]
    return pl.pallas_call(
        functools.partial(conv_kernel, chunks, picks, edge is not None, len(after), pair),
        out_shape=[jax.ShapeDtypeStruct((2 * chans, width), jnp.bfloat16)] * len(picks),
        in_specs=[SMEM] * 4 + [VMEM] * len(arrays) + [ANY] * len(after),
        out_specs=[VMEM] * len(picks),
        scratch_shapes=[
            pltpu.VMEM((own + HALO, chans, total), jnp.bfloat16),
            pltpu.VMEM((2, TAPS * G, len(picks) * width), jnp.bfloat16),
            pltpu.VMEM((2, G, TAPS * G), jnp.bfloat16),
        ],
        compiler_params=params(20),
        cost_estimate=takes(1 if len(picks) > 1 else 0.2),
        name="conv_rows",
    )(*supports, *arrays, *after)


def mlp_kernel(parts, last, after, *rest):
    blocks, rest = rest[:parts], rest[parts:]
    up_ref, down_ref, table_ref, *rest = rest
    rest = rest[after:]
    if last:
        earlier_ref, out_ref, cells_ref = rest
    else:
        out_ref, cells_ref = rest
    width = blocks[0].shape[1]
    place = lax.axis_index("chan")
    for block, k in zip(blocks, [0, *issue_order(parts)]):
        origin = pl.multiple_of(source(place, k, parts) * G, G)
        for i in range(2):
            cells_ref[pl.ds(origin, G), i * width : (i + 1) * width] = block[
                i * G : (i + 1) * G, :
            ]
    scale = math.sqrt(2.0 / math.pi)
    for at in range(0, 2 * width, COLUMNS):
        columns = slice(at, min(at + COLUMNS, 2 * width))
        values = cells_ref[:, columns].astype(jnp.float32)
        center = values - jnp.mean(values, axis=0, keepdims=True)
        spread = jnp.mean(center * center, axis=0, keepdims=True)
        normed = (center * lax.rsqrt(spread + EPS)).astype(jnp.bfloat16)
        lifted = jnp.dot(up_ref[...], normed, preferred_element_type=jnp.float32)
        inner = lifted * (scale + (scale * 0.044715) * (lifted * lifted))
        half = 0.5 * lifted
        active = (half + half * jnp.tanh(inner)).astype(jnp.bfloat16)
        lowered = jnp.dot(down_ref[...], active, preferred_element_type=jnp.float32)
        cells_ref[:, columns] = (values + lowered).astype(jnp.bfloat16)
    found = []
    for i in range(2):
        modes = lax.dot_general(
            table_ref[place],
            cells_ref[:, i * width : (i + 1) * width],
            (((1,), (1,)), ((), ())),
            preferred_element_type=jnp.float32,
        )
        found.append(modes.reshape(modes.shape[0] // SLOT, SLOT, modes.shape[1]))
    block = jnp.concatenate(found, axis=1).astype(jnp.bfloat16)
    if last:
        out_ref[:, 0 : 2 * SLOT, :] = earlier_ref[...]
        out_ref[:, 2 * SLOT : 4 * SLOT, :] = block
    else:
        out_ref[...] = block


def mlp_rows(blocks, up, down, tables, earlier, dests, after):
    pair_chans, width = blocks[0].shape
    chan = len(blocks) * pair_chans // 2
    last = earlier is not None
    arrays = [*blocks, up, down, tables, *after] + ([earlier] if last else [])
    rows = (4 if last else 2) * SLOT
    return pl.pallas_call(
        functools.partial(mlp_kernel, len(blocks), last, len(after)),
        out_shape=jax.ShapeDtypeStruct((dests, rows, chan), jnp.bfloat16),
        in_specs=[VMEM] * (len(blocks) + 3)
        + [ANY] * len(after)
        + [VMEM] * last,
        out_specs=VMEM,
        scratch_shapes=[pltpu.VMEM((chan, 2 * width), jnp.bfloat16)],
        compiler_params=params(20 if dests <= FEW else 40),
        cost_estimate=takes(1),
        name="mlp_rows",
    )(*arrays)


def expand_kernel(legendre_ref, spread_ref, out_ref):
    _, lats, degrees = legendre_ref.shape
    m = pl.program_id(0)
    first = lax.axis_index(("lat", "chan")) * pl.num_programs(0)
    degree = lax.broadcasted_iota(jnp.int32, (lats, degrees), 1)
    kept = jnp.where(degree >= first + m, legendre_ref[0].astype(jnp.float32), 0.0)
    wide = lax.dot_general(
        kept.astype(jnp.bfloat16),
        spread_ref[...],
        (((0,), (0,)), ((), ())),
        preferred_element_type=jnp.float32,
    )
    slot = lax.rem(lax.broadcasted_iota(jnp.int32, wide.shape, 1), SLOT)
    for r in range(2):
        out_ref[0, r] = jnp.where(slot == 2 * m + r, wide, 0.0).astype(jnp.bfloat16)


def expand(legendre, spread):
    modes, lats, degrees = legendre.shape
    depth = spread.shape[1]
    return pl.pallas_call(
        expand_kernel,
        out_shape=jax.ShapeDtypeStruct((modes, 2, degrees, depth), jnp.bfloat16),
        grid=(modes,),
        in_specs=[
            pl.BlockSpec((1, lats, degrees), lambda m: (m, 0, 0)),
            pl.BlockSpec((lats, depth), lambda m: (0, 0)),
        ],
        out_specs=pl.BlockSpec((1, 2, degrees, depth), lambda m: (m, 0, 0, 0)),
        compiler_params=params(10 if depth <= 512 else 48),
        cost_estimate=takes(0.2),
        name="expand",
    )(legendre, spread)


def final_kernel(left_ref, spectrum_ref, out_ref, result_ref, sems):
    modes = left_ref.shape[0]
    chan = spectrum_ref.shape[1]
    copies = []
    for m in range(modes):
        for r in range(2):
            result_ref[m, :, r * chan : (r + 1) * chan] = jnp.dot(
                left_ref[m, r], spectrum_ref[...], preferred_element_type=jnp.float32
            ).astype(jnp.bfloat16)
        copies.append(pltpu.make_async_copy(result_ref.at[m], out_ref.at[m], sems.at[m]))
        copies[-1].start()
    for copy in copies:
        copy.wait()


def final_sum(left, spectrum):
    modes, _, degrees, depth = left.shape
    shape = (modes, degrees, 2 * spectrum.shape[1])
    return pl.pallas_call(
        final_kernel,
        out_shape=jax.ShapeDtypeStruct(shape, jnp.bfloat16),
        in_specs=[VMEM, VMEM],
        out_specs=HBM,
        scratch_shapes=[pltpu.VMEM(shape, jnp.bfloat16), pltpu.SemaphoreType.DMA((modes,))],
        compiler_params=params(8 if depth <= 512 else 48),
        cost_estimate=takes(1),
        name="final_sum",
    )(left, spectrum)


def fourier_blocks(lon, chunks, width, dests, mode_dev):
    chunk = lon // chunks
    index = np.arange(lon, dtype=np.int64)
    mode = np.arange(dests * mode_dev, dtype=np.int64)
    angle = ((mode[:, None] * index[None, :]) % lon) * (2.0 * math.pi / lon)
    paired = np.stack([np.cos(angle), -np.sin(angle)], axis=1) * math.sqrt(2.0 / lon)
    paired = paired.reshape(dests, 2 * mode_dev, chunks, chunk)
    table = np.zeros((chunks, dests, SLOT, width), np.float32)
    table[:, :, : 2 * mode_dev, :chunk] = np.transpose(paired, (2, 0, 1, 3))
    return table.reshape(chunks, dests * SLOT, width).astype(jnp.bfloat16)


def turn(block, axis, count, k):
    return lax.ppermute(block, axis, [(i, target(i, k, count)) for i in range(count)])


def on_device(
    fields,
    disco_weight,
    support_lat,
    support_lon,
    support_basis,
    support_value,
    w_up,
    w_down,
    legendre,
):
    lat_dev, lon, _ = fields.shape
    num_lat = lax.axis_size("lat")
    num_chan = lax.axis_size("chan")
    mode_dev, _, lats = legendre.shape
    dests = num_lat * num_chan
    width = ceil_to(lon // num_chan, LANES)
    supports = (support_lat, support_lon, support_basis, support_value)

    two_bands = num_lat == 2
    cells = jnp.swapaxes(fields, 1, 2)
    if two_bands:
        cells, edge_out = edge_rows(cells)
        edges = [None, lax.ppermute(edge_out, "lat", [(0, 1), (1, 0)])]
        pairs = [lambda: lax.axis_index("lat"), lambda: 1 - lax.axis_index("lat")]
    else:
        ends = num_lat - 1
        edges = [
            lax.ppermute(cells[lat_dev - HALO :], "lat", [(i, i + 1) for i in range(ends)]),
            lax.ppermute(cells[:HALO], "lat", [(i + 1, i) for i in range(ends)]),
        ]
        pairs = [0, 1]

    tables = jnp.asarray(fourier_blocks(lon, num_chan, width, dests, mode_dev))
    up = w_up.T
    down = w_down.T

    depth = dests * 4 * SLOT
    row = np.arange(depth)
    source_band = row // (4 * SLOT) // num_chan
    phase = (row // (2 * SLOT)) % 2
    source_pair = (phase ^ source_band) if two_bands else phase
    lat_of = lat_dev * source_band + 2 * source_pair + (row // SLOT) % 2
    spread = (lat_of[None, :] == np.arange(lats)[:, None]).astype(jnp.bfloat16)
    left = expand(jnp.swapaxes(legendre, 1, 2), jnp.asarray(spread))

    order = issue_order(num_chan)
    halves = [
        (pair, supports, cells, edge, disco_weight, num_chan)
        for edge, pair in zip(edges, pairs)
    ]
    received = []
    after, last = [], []
    for half in halves:
        sent = conv_rows(*half, order, after, False)
        moved = [turn(block, "chan", num_chan, k) for k, block in zip(order, sent)]
        after = conv_rows(*half, [0], [sent[1], *last], False)
        received.append([*after, *moved])
        after, last = list(after), moved[:1]
    spectrum = None
    for blocks in received:
        spectrum = mlp_rows(blocks, up, down, tables, spectrum, dests, list(after))
        after = []

    both = ("lat", "chan")
    gathered = lax.all_to_all(spectrum, both, split_axis=0, concat_axis=0, tiled=True)
    return final_sum(left, gathered.reshape(depth, gathered.shape[2]))


def solution(mesh):
    in_specs = (
        P(("tm", "lat"), None, "chan"),
        P(None, "chan", None),
        P("lat", None),
        P("lat", None),
        P("lat", None),
        P("lat", None),
        P(),
        P(),
        P(("lat", "chan"), None, None),
    )
    out_specs = P(("tm", "lat", "chan"), None, None)
    return jax.shard_map(
        on_device, mesh=mesh, in_specs=in_specs, out_specs=out_specs, check_vma=False
    )
```

```python
import functools
import math

import jax
import jax.numpy as jnp
import numpy as np
from jax import lax
from jax.experimental import pallas as pl
from jax.experimental.pallas import tpu as pltpu
from jax.sharding import PartitionSpec as P

G = 64
S = 9
HALO = 2
DLON = 4
TAPS = S + 1
LANES = 128
SLOT = 8
EPS = 1e-05
FEW = 8
MIB = 1024 * 1024
EDGE_COST = 4
FLOPS_PER_US = 1_000_000_000

SMEM = pl.BlockSpec(memory_space=pltpu.SMEM)
VMEM = pl.BlockSpec(memory_space=pltpu.VMEM)
ANY = pl.BlockSpec(memory_space=pl.ANY)
HBM = pl.BlockSpec(memory_space=pltpu.HBM)


def ceil_to(value, step):
    return -(-value // step) * step


def params(mib):
    return pltpu.CompilerParams(vmem_limit_bytes=mib * MIB)


def takes(micros):
    return pl.CostEstimate(flops=int(micros * FLOPS_PER_US), bytes_accessed=0, transcendentals=0)


def paired(count):
    return count & (count - 1) == 0


def target(place, k, count):
    return place ^ k if paired(count) else (place + k) % count


def source(place, k, count):
    return place ^ k if paired(count) else (place - k + count) % count


def issue_order(count):
    return [*range(2, count), 1] if paired(count) else list(range(1, count))


def edge_kernel(fields_ref, same_ref, out_ref):
    start = HALO * (1 - lax.axis_index("lat"))
    for k in range(HALO):
        out_ref[k] = fields_ref[start + k]
    same_ref[...] = fields_ref[...]


def edge_rows(fields):
    shapes = [fields.shape, (HALO, *fields.shape[1:])]
    return pl.pallas_call(
        edge_kernel,
        out_shape=[jax.ShapeDtypeStruct(shape, fields.dtype) for shape in shapes],
        in_specs=[VMEM],
        out_specs=[VMEM] * 2,
        compiler_params=params(8),
        cost_estimate=takes(EDGE_COST),
        name="edge_rows",
    )(fields)


def conv_kernel(
    chunks, picks, has_edge, after, flip, lat_ref, lon_ref, basis_ref, value_ref, fields_ref, *rest
):
    if has_edge:
        edge_ref, weight_ref, *rest = rest
    else:
        edge_ref, (weight_ref, *rest) = None, rest
    *out_refs, rows_ref, taps_ref, filt_ref = rest[after:]
    own, _, lon = fields_ref.shape
    chunk = lon // chunks
    width = out_refs[0].shape[1]
    total = rows_ref.shape[2]
    pair = flip if isinstance(flip, int) else flip()
    own_at = HALO * (1 - pair)
    edge_at = own * pair

    def put(slot, cells):
        rows_ref[slot, :, LANES : LANES + lon] = cells
        rows_ref[slot, :, 0:LANES] = cells[:, lon - LANES :]
        full = (lon // LANES) * LANES
        tail = total - LANES - lon
        rows_ref[slot, :, LANES + full :] = jnp.concatenate(
            [cells[:, full:], cells[:, :tail]], axis=1
        )

    for row in range(own):
        put(own_at + row, fields_ref[row])
    for row in range(HALO):
        if has_edge:
            put(edge_at + row, edge_ref[row])
        else:
            rows_ref[edge_at + row] = jnp.zeros(rows_ref.shape[1:], rows_ref.dtype)

    lane = lax.broadcasted_iota(jnp.int32, (G, LANES), 1)
    begins = [LANES + chunk * target(lax.axis_index("chan"), k, chunks) for k in picks]

    def fill(slot, tap, source, offset):
        for k, origin in enumerate(begins):
            begin = origin + offset
            first = lax.div(begin, LANES)
            shift = lax.rem(begin, LANES)
            back = lax.rem(LANES - shift, LANES)
            keep = lane < LANES - shift
            turned = []
            for t in range(width // LANES + 1):
                start = pl.multiple_of((first + t) * LANES, LANES)
                tile = rows_ref[source, :, pl.ds(start, LANES)]
                turned.append(pltpu.roll(tile, back, 1))
            for t in range(width // LANES):
                at = k * width + t * LANES
                taps_ref[slot, tap * G : (tap + 1) * G, at : at + LANES] = jnp.where(
                    keep, turned[t], turned[t + 1]
                )

    eye = jnp.where(
        lax.broadcasted_iota(jnp.int32, (G, G), 0) == lax.broadcasted_iota(jnp.int32, (G, G), 1),
        1.0,
        0.0,
    ).astype(jnp.bfloat16)
    for i in range(2):
        row = 2 * pair + i
        pieces = []
        for tap in range(S):
            picked = weight_ref[basis_ref[row, tap]].astype(jnp.float32) * value_ref[row, tap]
            pieces.append(picked.astype(jnp.bfloat16))
        pieces.append(eye)
        for k in range(TAPS // 2):
            filt_ref[i, :, k * 2 * G : (k + 1) * 2 * G] = jnp.concatenate(
                [pieces[2 * k], pieces[2 * k + 1]], axis=1
            )
        for tap in range(S):
            fill(i, tap, HALO + i + lat_ref[row, tap], lon_ref[row, tap])
        fill(i, S, HALO + i, 0)
        mixed = jnp.dot(filt_ref[i], taps_ref[i], preferred_element_type=jnp.float32).astype(
            jnp.bfloat16
        )
        for k in range(len(picks)):
            out_refs[k][i * G : (i + 1) * G, :] = mixed[:, k * width : (k + 1) * width]


def conv_rows(pair, supports, fields, edge, weight, chunks, picks, after, roomy):
    own, chans, lon = fields.shape
    width = ceil_to(lon // chunks, LANES)
    highest = (LANES + lon - lon // chunks + DLON) // LANES
    total = (highest + 1) * LANES + width
    arrays = [fields] + ([] if edge is None else [edge]) + [weight]
    return pl.pallas_call(
        functools.partial(conv_kernel, chunks, picks, edge is not None, len(after), pair),
        out_shape=[jax.ShapeDtypeStruct((2 * chans, width), jnp.bfloat16)] * len(picks),
        in_specs=[SMEM] * 4 + [VMEM] * len(arrays) + [ANY] * len(after),
        out_specs=[VMEM] * len(picks),
        scratch_shapes=[
            pltpu.VMEM((own + HALO, chans, total), jnp.bfloat16),
            pltpu.VMEM((2, TAPS * G, len(picks) * width), jnp.bfloat16),
            pltpu.VMEM((2, G, TAPS * G), jnp.bfloat16),
        ],
        compiler_params=params(20),
        cost_estimate=takes(1 if len(picks) > 1 else 0.2),
        name="conv_rows",
    )(*supports, *arrays, *after)


def mlp_kernel(parts, last, after, *rest):
    blocks, rest = rest[:parts], rest[parts:]
    up_ref, down_ref, table_ref, *rest = rest
    rest = rest[after:]
    if last:
        earlier_ref, out_ref, cells_ref = rest
    else:
        out_ref, cells_ref = rest
    width = blocks[0].shape[1]
    place = lax.axis_index("chan")
    for block, k in zip(blocks, [0, *issue_order(parts)]):
        origin = pl.multiple_of(source(place, k, parts) * G, G)
        for i in range(2):
            cells_ref[pl.ds(origin, G), i * width : (i + 1) * width] = block[
                i * G : (i + 1) * G, :
            ]
    values = cells_ref[...].astype(jnp.float32)
    center = values - jnp.mean(values, axis=0, keepdims=True)
    spread = jnp.mean(center * center, axis=0, keepdims=True)
    normed = (center * lax.rsqrt(spread + EPS)).astype(jnp.bfloat16)
    lifted = jnp.dot(up_ref[...], normed, preferred_element_type=jnp.float32)
    scale = math.sqrt(2.0 / math.pi)
    inner = lifted * (scale + (scale * 0.044715) * (lifted * lifted))
    half = 0.5 * lifted
    active = (half + half * jnp.tanh(inner)).astype(jnp.bfloat16)
    lowered = jnp.dot(down_ref[...], active, preferred_element_type=jnp.float32)
    result = (values + lowered).astype(jnp.bfloat16)
    found = []
    for i in range(2):
        modes = lax.dot_general(
            table_ref[place],
            result[:, i * width : (i + 1) * width],
            (((1,), (1,)), ((), ())),
            preferred_element_type=jnp.float32,
        )
        found.append(modes.reshape(modes.shape[0] // SLOT, SLOT, modes.shape[1]))
    block = jnp.concatenate(found, axis=1).astype(jnp.bfloat16)
    if last:
        out_ref[:, 0 : 2 * SLOT, :] = earlier_ref[...]
        out_ref[:, 2 * SLOT : 4 * SLOT, :] = block
    else:
        out_ref[...] = block


def mlp_rows(blocks, up, down, tables, earlier, dests, after):
    pair_chans, width = blocks[0].shape
    chan = len(blocks) * pair_chans // 2
    last = earlier is not None
    arrays = [*blocks, up, down, tables, *after] + ([earlier] if last else [])
    rows = (4 if last else 2) * SLOT
    return pl.pallas_call(
        functools.partial(mlp_kernel, len(blocks), last, len(after)),
        out_shape=jax.ShapeDtypeStruct((dests, rows, chan), jnp.bfloat16),
        in_specs=[VMEM] * (len(blocks) + 3)
        + [ANY] * len(after)
        + [VMEM] * last,
        out_specs=VMEM,
        scratch_shapes=[pltpu.VMEM((chan, 2 * width), jnp.bfloat16)],
        compiler_params=params(20 if dests <= FEW else 40),
        cost_estimate=takes(1),
        name="mlp_rows",
    )(*arrays)


def expand_kernel(legendre_ref, spread_ref, out_ref):
    _, lats, degrees = legendre_ref.shape
    m = pl.program_id(0)
    first = lax.axis_index(("lat", "chan")) * pl.num_programs(0)
    degree = lax.broadcasted_iota(jnp.int32, (lats, degrees), 1)
    kept = jnp.where(degree >= first + m, legendre_ref[0].astype(jnp.float32), 0.0)
    wide = lax.dot_general(
        kept.astype(jnp.bfloat16),
        spread_ref[...],
        (((0,), (0,)), ((), ())),
        preferred_element_type=jnp.float32,
    )
    slot = lax.rem(lax.broadcasted_iota(jnp.int32, wide.shape, 1), SLOT)
    for r in range(2):
        out_ref[0, r] = jnp.where(slot == 2 * m + r, wide, 0.0).astype(jnp.bfloat16)


def expand(legendre, spread):
    modes, lats, degrees = legendre.shape
    depth = spread.shape[1]
    return pl.pallas_call(
        expand_kernel,
        out_shape=jax.ShapeDtypeStruct((modes, 2, degrees, depth), jnp.bfloat16),
        grid=(modes,),
        in_specs=[
            pl.BlockSpec((1, lats, degrees), lambda m: (m, 0, 0)),
            pl.BlockSpec((lats, depth), lambda m: (0, 0)),
        ],
        out_specs=pl.BlockSpec((1, 2, degrees, depth), lambda m: (m, 0, 0, 0)),
        compiler_params=params(10 if depth <= 512 else 48),
        cost_estimate=takes(0.2),
        name="expand",
    )(legendre, spread)


def final_kernel(left_ref, spectrum_ref, out_ref, result_ref, sems):
    modes = left_ref.shape[0]
    chan = spectrum_ref.shape[1]
    copies = []
    for m in range(modes):
        for r in range(2):
            result_ref[m, :, r * chan : (r + 1) * chan] = jnp.dot(
                left_ref[m, r], spectrum_ref[...], preferred_element_type=jnp.float32
            ).astype(jnp.bfloat16)
        copies.append(pltpu.make_async_copy(result_ref.at[m], out_ref.at[m], sems.at[m]))
        copies[-1].start()
    for copy in copies:
        copy.wait()


def final_sum(left, spectrum):
    modes, _, degrees, depth = left.shape
    shape = (modes, degrees, 2 * spectrum.shape[1])
    return pl.pallas_call(
        final_kernel,
        out_shape=jax.ShapeDtypeStruct(shape, jnp.bfloat16),
        in_specs=[VMEM, VMEM],
        out_specs=HBM,
        scratch_shapes=[pltpu.VMEM(shape, jnp.bfloat16), pltpu.SemaphoreType.DMA((modes,))],
        compiler_params=params(8 if depth <= 512 else 48),
        cost_estimate=takes(1),
        name="final_sum",
    )(left, spectrum)


def fourier_blocks(lon, chunks, width, dests, mode_dev):
    chunk = lon // chunks
    index = np.arange(lon, dtype=np.int64)
    mode = np.arange(dests * mode_dev, dtype=np.int64)
    angle = ((mode[:, None] * index[None, :]) % lon) * (2.0 * math.pi / lon)
    paired = np.stack([np.cos(angle), -np.sin(angle)], axis=1) * math.sqrt(2.0 / lon)
    paired = paired.reshape(dests, 2 * mode_dev, chunks, chunk)
    table = np.zeros((chunks, dests, SLOT, width), np.float32)
    table[:, :, : 2 * mode_dev, :chunk] = np.transpose(paired, (2, 0, 1, 3))
    return table.reshape(chunks, dests * SLOT, width).astype(jnp.bfloat16)


def turn(block, axis, count, k):
    return lax.ppermute(block, axis, [(i, target(i, k, count)) for i in range(count)])


def on_device(
    fields,
    disco_weight,
    support_lat,
    support_lon,
    support_basis,
    support_value,
    w_up,
    w_down,
    legendre,
):
    lat_dev, lon, _ = fields.shape
    num_lat = lax.axis_size("lat")
    num_chan = lax.axis_size("chan")
    mode_dev, _, lats = legendre.shape
    dests = num_lat * num_chan
    width = ceil_to(lon // num_chan, LANES)
    supports = (support_lat, support_lon, support_basis, support_value)

    two_bands = num_lat == 2
    cells = jnp.swapaxes(fields, 1, 2)
    if two_bands:
        cells, edge_out = edge_rows(cells)
        edges = [None, lax.ppermute(edge_out, "lat", [(0, 1), (1, 0)])]
        pairs = [lambda: lax.axis_index("lat"), lambda: 1 - lax.axis_index("lat")]
    else:
        ends = num_lat - 1
        edges = [
            lax.ppermute(cells[lat_dev - HALO :], "lat", [(i, i + 1) for i in range(ends)]),
            lax.ppermute(cells[:HALO], "lat", [(i + 1, i) for i in range(ends)]),
        ]
        pairs = [0, 1]

    tables = jnp.asarray(fourier_blocks(lon, num_chan, width, dests, mode_dev))
    up = w_up.T
    down = w_down.T

    depth = dests * 4 * SLOT
    row = np.arange(depth)
    source_band = row // (4 * SLOT) // num_chan
    phase = (row // (2 * SLOT)) % 2
    source_pair = (phase ^ source_band) if two_bands else phase
    lat_of = lat_dev * source_band + 2 * source_pair + (row // SLOT) % 2
    spread = (lat_of[None, :] == np.arange(lats)[:, None]).astype(jnp.bfloat16)
    left = expand(jnp.swapaxes(legendre, 1, 2), jnp.asarray(spread))

    order = issue_order(num_chan)
    halves = [
        (pair, supports, cells, edge, disco_weight, num_chan)
        for edge, pair in zip(edges, pairs)
    ]
    received = []
    after, last = [], []
    for half in halves:
        sent = conv_rows(*half, order, after, False)
        moved = [turn(block, "chan", num_chan, k) for k, block in zip(order, sent)]
        after = conv_rows(*half, [0], [sent[0], *last], False)
        received.append([*after, *moved])
        after, last = list(after), moved[:1]
    spectrum = None
    for blocks in received:
        spectrum = mlp_rows(blocks, up, down, tables, spectrum, dests, list(after))
        after = []

    both = ("lat", "chan")
    gathered = lax.all_to_all(spectrum, both, split_axis=0, concat_axis=0, tiled=True)
    return final_sum(left, gathered.reshape(depth, gathered.shape[2]))


def solution(mesh):
    in_specs = (
        P(("tm", "lat"), None, "chan"),
        P(None, "chan", None),
        P("lat", None),
        P("lat", None),
        P("lat", None),
        P("lat", None),
        P(),
        P(),
        P(("lat", "chan"), None, None),
    )
    out_specs = P(("tm", "lat", "chan"), None, None)
    return jax.shard_map(
        on_device, mesh=mesh, in_specs=in_specs, out_specs=out_specs, check_vma=False
    )
```

```python
import functools
import math

import jax
import jax.numpy as jnp
import numpy as np
from jax import lax
from jax.experimental import pallas as pl
from jax.experimental.pallas import tpu as pltpu
from jax.sharding import PartitionSpec as P

G = 64
S = 9
HALO = 2
DLON = 4
TAPS = S + 1
LANES = 128
SLOT = 8
EPS = 1e-05
FEW = 8
MIB = 1024 * 1024
FLOPS_PER_US = 1_000_000_000

SMEM = pl.BlockSpec(memory_space=pltpu.SMEM)
VMEM = pl.BlockSpec(memory_space=pltpu.VMEM)
ANY = pl.BlockSpec(memory_space=pl.ANY)
HBM = pl.BlockSpec(memory_space=pltpu.HBM)


def ceil_to(value, step):
    return -(-value // step) * step


def params(mib):
    return pltpu.CompilerParams(vmem_limit_bytes=mib * MIB)


def takes(micros):
    return pl.CostEstimate(flops=int(micros * FLOPS_PER_US), bytes_accessed=0, transcendentals=0)


def paired(count):
    return count & (count - 1) == 0


def target(place, k, count):
    return place ^ k if paired(count) else (place + k) % count


def source(place, k, count):
    return place ^ k if paired(count) else (place - k + count) % count


def issue_order(count):
    return [*range(2, count), 1] if paired(count) else list(range(1, count))


def conv_kernel(
    chunks, picks, has_edge, after, pair_ref, place_ref, lat_ref, lon_ref, basis_ref, value_ref, fields_ref, *rest
):
    if has_edge:
        edge_ref, weight_ref, *rest = rest
    else:
        edge_ref, (weight_ref, *rest) = None, rest
    *out_refs, rows_ref, taps_ref, filt_ref = rest[after:]
    own, _, lon = fields_ref.shape
    chunk = lon // chunks
    width = out_refs[0].shape[1]
    total = rows_ref.shape[2]
    pair = pair_ref[0]
    own_at = HALO * (1 - pair)
    edge_at = own * pair

    def put(slot, cells):
        rows_ref[slot, :, LANES : LANES + lon] = cells
        rows_ref[slot, :, 0:LANES] = cells[:, lon - LANES :]
        full = (lon // LANES) * LANES
        tail = total - LANES - lon
        rows_ref[slot, :, LANES + full :] = jnp.concatenate(
            [cells[:, full:], cells[:, :tail]], axis=1
        )

    for row in range(own):
        put(own_at + row, fields_ref[row])
    for row in range(HALO):
        if has_edge:
            put(edge_at + row, edge_ref[row])
        else:
            rows_ref[edge_at + row] = jnp.zeros(rows_ref.shape[1:], rows_ref.dtype)

    lane = lax.broadcasted_iota(jnp.int32, (G, LANES), 1)
    begins = [LANES + chunk * target(place_ref[0], k, chunks) for k in picks]

    def fill(slot, tap, source, offset):
        for k, origin in enumerate(begins):
            begin = origin + offset
            first = lax.div(begin, LANES)
            shift = lax.rem(begin, LANES)
            back = lax.rem(LANES - shift, LANES)
            keep = lane < LANES - shift
            turned = []
            for t in range(width // LANES + 1):
                start = pl.multiple_of((first + t) * LANES, LANES)
                tile = rows_ref[source, :, pl.ds(start, LANES)]
                turned.append(pltpu.roll(tile, back, 1))
            for t in range(width // LANES):
                at = k * width + t * LANES
                taps_ref[slot, tap * G : (tap + 1) * G, at : at + LANES] = jnp.where(
                    keep, turned[t], turned[t + 1]
                )

    eye = jnp.where(
        lax.broadcasted_iota(jnp.int32, (G, G), 0) == lax.broadcasted_iota(jnp.int32, (G, G), 1),
        1.0,
        0.0,
    ).astype(jnp.bfloat16)
    for i in range(2):
        row = 2 * pair + i
        pieces = []
        for tap in range(S):
            picked = weight_ref[basis_ref[row, tap]].astype(jnp.float32) * value_ref[row, tap]
            pieces.append(picked.astype(jnp.bfloat16))
        pieces.append(eye)
        for k in range(TAPS // 2):
            filt_ref[i, :, k * 2 * G : (k + 1) * 2 * G] = jnp.concatenate(
                [pieces[2 * k], pieces[2 * k + 1]], axis=1
            )
        for tap in range(S):
            fill(i, tap, HALO + i + lat_ref[row, tap], lon_ref[row, tap])
        fill(i, S, HALO + i, 0)
        mixed = jnp.dot(filt_ref[i], taps_ref[i], preferred_element_type=jnp.float32).astype(
            jnp.bfloat16
        )
        for k in range(len(picks)):
            out_refs[k][i * G : (i + 1) * G, :] = mixed[:, k * width : (k + 1) * width]


def conv_rows(pair, place, supports, fields, edge, weight, chunks, picks, after, roomy):
    own, chans, lon = fields.shape
    width = ceil_to(lon // chunks, LANES)
    highest = (LANES + lon - lon // chunks + DLON) // LANES
    total = (highest + 1) * LANES + width
    arrays = [fields] + ([] if edge is None else [edge]) + [weight]
    return pl.pallas_call(
        functools.partial(conv_kernel, chunks, picks, edge is not None, len(after)),
        out_shape=[jax.ShapeDtypeStruct((2 * chans, width), jnp.bfloat16)] * len(picks),
        in_specs=[SMEM] * 6 + [VMEM] * len(arrays) + [ANY] * len(after),
        out_specs=[VMEM] * len(picks),
        scratch_shapes=[
            pltpu.VMEM((own + HALO, chans, total), jnp.bfloat16),
            pltpu.VMEM((2, TAPS * G, len(picks) * width), jnp.bfloat16),
            pltpu.VMEM((2, G, TAPS * G), jnp.bfloat16),
        ],
        compiler_params=params(56 if roomy else 20),
        cost_estimate=takes(1 if len(picks) > 1 else 0.2),
        name="conv_rows",
    )(pair, place, *supports, *arrays, *after)


def mlp_kernel(parts, last, after, place_ref, *rest):
    blocks, rest = rest[:parts], rest[parts:]
    up_ref, down_ref, table_ref, *rest = rest
    rest = rest[after:]
    if last:
        earlier_ref, out_ref, cells_ref = rest
    else:
        out_ref, cells_ref = rest
    width = blocks[0].shape[1]
    place = place_ref[0]
    for block, k in zip(blocks, [0, *issue_order(parts)]):
        origin = pl.multiple_of(source(place, k, parts) * G, G)
        for i in range(2):
            cells_ref[pl.ds(origin, G), i * width : (i + 1) * width] = block[
                i * G : (i + 1) * G, :
            ]
    values = cells_ref[...].astype(jnp.float32)
    center = values - jnp.mean(values, axis=0, keepdims=True)
    spread = jnp.mean(center * center, axis=0, keepdims=True)
    normed = (center * lax.rsqrt(spread + EPS)).astype(jnp.bfloat16)
    lifted = jnp.dot(up_ref[...], normed, preferred_element_type=jnp.float32)
    scale = math.sqrt(2.0 / math.pi)
    inner = lifted * (scale + (scale * 0.044715) * (lifted * lifted))
    half = 0.5 * lifted
    active = (half + half * jnp.tanh(inner)).astype(jnp.bfloat16)
    lowered = jnp.dot(down_ref[...], active, preferred_element_type=jnp.float32)
    result = (values + lowered).astype(jnp.bfloat16)
    found = []
    for i in range(2):
        modes = lax.dot_general(
            table_ref[place],
            result[:, i * width : (i + 1) * width],
            (((1,), (1,)), ((), ())),
            preferred_element_type=jnp.float32,
        )
        found.append(modes.reshape(modes.shape[0] // SLOT, SLOT, modes.shape[1]))
    block = jnp.concatenate(found, axis=1).astype(jnp.bfloat16)
    if last:
        out_ref[:, 0 : 2 * SLOT, :] = earlier_ref[...]
        out_ref[:, 2 * SLOT : 4 * SLOT, :] = block
    else:
        out_ref[...] = block


def mlp_rows(place, blocks, up, down, tables, earlier, dests, after):
    pair_chans, width = blocks[0].shape
    chan = len(blocks) * pair_chans // 2
    last = earlier is not None
    arrays = [*blocks, up, down, tables, *after] + ([earlier] if last else [])
    rows = (4 if last else 2) * SLOT
    return pl.pallas_call(
        functools.partial(mlp_kernel, len(blocks), last, len(after)),
        out_shape=jax.ShapeDtypeStruct((dests, rows, chan), jnp.bfloat16),
        in_specs=[SMEM]
        + [VMEM] * (len(blocks) + 3)
        + [ANY] * len(after)
        + [VMEM] * last,
        out_specs=VMEM,
        scratch_shapes=[pltpu.VMEM((chan, 2 * width), jnp.bfloat16)],
        compiler_params=params(20 if dests <= FEW else 40),
        cost_estimate=takes(1),
        name="mlp_rows",
    )(place, *arrays)


def expand_kernel(start_ref, legendre_ref, spread_ref, out_ref):
    _, lats, degrees = legendre_ref.shape
    m = pl.program_id(0)
    degree = lax.broadcasted_iota(jnp.int32, (lats, degrees), 1)
    kept = jnp.where(degree >= start_ref[0] + m, legendre_ref[0].astype(jnp.float32), 0.0)
    wide = lax.dot_general(
        kept.astype(jnp.bfloat16),
        spread_ref[...],
        (((0,), (0,)), ((), ())),
        preferred_element_type=jnp.float32,
    )
    slot = lax.rem(lax.broadcasted_iota(jnp.int32, wide.shape, 1), SLOT)
    for r in range(2):
        out_ref[0, r] = jnp.where(slot == 2 * m + r, wide, 0.0).astype(jnp.bfloat16)


def expand(start, legendre, spread):
    modes, lats, degrees = legendre.shape
    depth = spread.shape[1]
    return pl.pallas_call(
        expand_kernel,
        out_shape=jax.ShapeDtypeStruct((modes, 2, degrees, depth), jnp.bfloat16),
        grid=(modes,),
        in_specs=[
            SMEM,
            pl.BlockSpec((1, lats, degrees), lambda m: (m, 0, 0)),
            pl.BlockSpec((lats, depth), lambda m: (0, 0)),
        ],
        out_specs=pl.BlockSpec((1, 2, degrees, depth), lambda m: (m, 0, 0, 0)),
        compiler_params=params(10 if depth <= 512 else 48),
        cost_estimate=takes(0.2),
        name="expand",
    )(start, legendre, spread)


def final_kernel(left_ref, spectrum_ref, out_ref, result_ref, sems):
    modes = left_ref.shape[0]
    chan = spectrum_ref.shape[1]
    copies = []
    for m in range(modes):
        for r in range(2):
            result_ref[m, :, r * chan : (r + 1) * chan] = jnp.dot(
                left_ref[m, r], spectrum_ref[...], preferred_element_type=jnp.float32
            ).astype(jnp.bfloat16)
        copies.append(pltpu.make_async_copy(result_ref.at[m], out_ref.at[m], sems.at[m]))
        copies[-1].start()
    for copy in copies:
        copy.wait()


def final_sum(left, spectrum):
    modes, _, degrees, depth = left.shape
    shape = (modes, degrees, 2 * spectrum.shape[1])
    return pl.pallas_call(
        final_kernel,
        out_shape=jax.ShapeDtypeStruct(shape, jnp.bfloat16),
        in_specs=[VMEM, VMEM],
        out_specs=HBM,
        scratch_shapes=[pltpu.VMEM(shape, jnp.bfloat16), pltpu.SemaphoreType.DMA((modes,))],
        compiler_params=params(8 if depth <= 512 else 48),
        cost_estimate=takes(1),
        name="final_sum",
    )(left, spectrum)


def fourier_blocks(lon, chunks, width, dests, mode_dev):
    chunk = lon // chunks
    index = np.arange(lon, dtype=np.int64)
    mode = np.arange(dests * mode_dev, dtype=np.int64)
    angle = ((mode[:, None] * index[None, :]) % lon) * (2.0 * math.pi / lon)
    paired = np.stack([np.cos(angle), -np.sin(angle)], axis=1) * math.sqrt(2.0 / lon)
    paired = paired.reshape(dests, 2 * mode_dev, chunks, chunk)
    table = np.zeros((chunks, dests, SLOT, width), np.float32)
    table[:, :, : 2 * mode_dev, :chunk] = np.transpose(paired, (2, 0, 1, 3))
    return table.reshape(chunks, dests * SLOT, width).astype(jnp.bfloat16)


def turn(block, axis, count, k):
    return lax.ppermute(block, axis, [(i, target(i, k, count)) for i in range(count)])


def scalar(value):
    return jnp.asarray(value, jnp.int32).reshape(1)


def on_device(
    fields,
    disco_weight,
    support_lat,
    support_lon,
    support_basis,
    support_value,
    w_up,
    w_down,
    legendre,
):
    lat_dev, lon, _ = fields.shape
    num_lat = lax.axis_size("lat")
    num_chan = lax.axis_size("chan")
    mode_dev, _, lats = legendre.shape
    dests = num_lat * num_chan
    width = ceil_to(lon // num_chan, LANES)
    band = lax.axis_index("lat")
    place = scalar(lax.axis_index("chan"))
    index = lax.axis_index(("lat", "chan"))
    supports = (support_lat, support_lon, support_basis, support_value)

    two_bands = num_lat == 2
    cells = jnp.swapaxes(fields, 1, 2)
    if two_bands:
        edge_out = lax.dynamic_slice_in_dim(cells, HALO * (1 - band), HALO, axis=0)
        edges = [None, lax.ppermute(edge_out, "lat", [(0, 1), (1, 0)])]
        pairs = [band, 1 - band]
    else:
        ends = num_lat - 1
        edges = [
            lax.ppermute(cells[lat_dev - HALO :], "lat", [(i, i + 1) for i in range(ends)]),
            lax.ppermute(cells[:HALO], "lat", [(i + 1, i) for i in range(ends)]),
        ]
        pairs = [0, 1]

    tables = jnp.asarray(fourier_blocks(lon, num_chan, width, dests, mode_dev))
    up = w_up.T
    down = w_down.T

    depth = dests * 4 * SLOT
    row = np.arange(depth)
    source_band = row // (4 * SLOT) // num_chan
    phase = (row // (2 * SLOT)) % 2
    source_pair = (phase ^ source_band) if two_bands else phase
    lat_of = lat_dev * source_band + 2 * source_pair + (row // SLOT) % 2
    spread = (lat_of[None, :] == np.arange(lats)[:, None]).astype(jnp.bfloat16)
    left = expand(scalar(index * mode_dev), jnp.swapaxes(legendre, 1, 2), jnp.asarray(spread))

    received = []
    order = issue_order(num_chan)
    for edge, pair in zip(edges, pairs):
        shared = (scalar(pair), place, supports, cells, edge, disco_weight, num_chan)
        if received:
            sent = conv_rows(*shared, order, [], False)
            kept = conv_rows(*shared, (0,), sent[-1:], False)
        else:
            *sent, own = conv_rows(*shared, [*order, 0], [], edge is None)
            kept = [own]
        moved = [turn(block, "chan", num_chan, k) for k, block in zip(order, sent)]
        received.append([*kept, *moved])
    after = kept
    spectrum = None
    after = list(after)
    for blocks in received:
        spectrum = mlp_rows(place, blocks, up, down, tables, spectrum, dests, after)
        after = []

    both = ("lat", "chan")
    gathered = lax.all_to_all(spectrum, both, split_axis=0, concat_axis=0, tiled=True)
    return final_sum(left, gathered.reshape(depth, gathered.shape[2]))


def solution(mesh):
    in_specs = (
        P(("tm", "lat"), None, "chan"),
        P(None, "chan", None),
        P("lat", None),
        P("lat", None),
        P("lat", None),
        P("lat", None),
        P(),
        P(),
        P(("lat", "chan"), None, None),
    )
    out_specs = P(("tm", "lat", "chan"), None, None)
    return jax.shard_map(
        on_device, mesh=mesh, in_specs=in_specs, out_specs=out_specs, check_vma=False
    )
```

```python
import functools
import math

import jax
import jax.numpy as jnp
import numpy as np
from jax import lax
from jax.experimental import pallas as pl
from jax.experimental.pallas import tpu as pltpu
from jax.sharding import PartitionSpec as P

G = 64
S = 9
HALO = 2
DLON = 4
TAPS = S + 1
LANES = 128
SLOT = 8
EPS = 1e-05
FEW = 8
MIB = 1024 * 1024
FLOPS_PER_US = 1_000_000_000

SMEM = pl.BlockSpec(memory_space=pltpu.SMEM)
VMEM = pl.BlockSpec(memory_space=pltpu.VMEM)
ANY = pl.BlockSpec(memory_space=pl.ANY)
HBM = pl.BlockSpec(memory_space=pltpu.HBM)


def ceil_to(value, step):
    return -(-value // step) * step


def params(mib):
    return pltpu.CompilerParams(vmem_limit_bytes=mib * MIB)


def takes(micros):
    return pl.CostEstimate(flops=int(micros * FLOPS_PER_US), bytes_accessed=0, transcendentals=0)


def paired(count):
    return count & (count - 1) == 0


def target(place, k, count):
    return place ^ k if paired(count) else (place + k) % count


def source(place, k, count):
    return place ^ k if paired(count) else (place - k + count) % count


def issue_order(count):
    return list(range(count - 1, 0, -1)) if paired(count) else list(range(1, count))


def conv_kernel(
    chunks, picks, has_edge, after, pair_ref, place_ref, lat_ref, lon_ref, basis_ref, value_ref, fields_ref, *rest
):
    if has_edge:
        edge_ref, weight_ref, *rest = rest
    else:
        edge_ref, (weight_ref, *rest) = None, rest
    *out_refs, rows_ref, taps_ref, filt_ref = rest[after:]
    own, _, lon = fields_ref.shape
    chunk = lon // chunks
    width = out_refs[0].shape[1]
    total = rows_ref.shape[2]
    pair = pair_ref[0]
    own_at = HALO * (1 - pair)
    edge_at = own * pair

    def put(slot, cells):
        rows_ref[slot, :, LANES : LANES + lon] = cells
        rows_ref[slot, :, 0:LANES] = cells[:, lon - LANES :]
        full = (lon // LANES) * LANES
        tail = total - LANES - lon
        rows_ref[slot, :, LANES + full :] = jnp.concatenate(
            [cells[:, full:], cells[:, :tail]], axis=1
        )

    for row in range(own):
        put(own_at + row, fields_ref[row])
    for row in range(HALO):
        if has_edge:
            put(edge_at + row, edge_ref[row])
        else:
            rows_ref[edge_at + row] = jnp.zeros(rows_ref.shape[1:], rows_ref.dtype)

    lane = lax.broadcasted_iota(jnp.int32, (G, LANES), 1)
    begins = [LANES + chunk * target(place_ref[0], k, chunks) for k in picks]

    def fill(slot, tap, source, offset):
        for k, origin in enumerate(begins):
            begin = origin + offset
            first = lax.div(begin, LANES)
            shift = lax.rem(begin, LANES)
            back = lax.rem(LANES - shift, LANES)
            keep = lane < LANES - shift
            turned = []
            for t in range(width // LANES + 1):
                start = pl.multiple_of((first + t) * LANES, LANES)
                tile = rows_ref[source, :, pl.ds(start, LANES)]
                turned.append(pltpu.roll(tile, back, 1))
            for t in range(width // LANES):
                at = k * width + t * LANES
                taps_ref[slot, tap * G : (tap + 1) * G, at : at + LANES] = jnp.where(
                    keep, turned[t], turned[t + 1]
                )

    eye = jnp.where(
        lax.broadcasted_iota(jnp.int32, (G, G), 0) == lax.broadcasted_iota(jnp.int32, (G, G), 1),
        1.0,
        0.0,
    ).astype(jnp.bfloat16)
    for i in range(2):
        row = 2 * pair + i
        pieces = []
        for tap in range(S):
            picked = weight_ref[basis_ref[row, tap]].astype(jnp.float32) * value_ref[row, tap]
            pieces.append(picked.astype(jnp.bfloat16))
        pieces.append(eye)
        for k in range(TAPS // 2):
            filt_ref[i, :, k * 2 * G : (k + 1) * 2 * G] = jnp.concatenate(
                [pieces[2 * k], pieces[2 * k + 1]], axis=1
            )
        for tap in range(S):
            fill(i, tap, HALO + i + lat_ref[row, tap], lon_ref[row, tap])
        fill(i, S, HALO + i, 0)
        mixed = jnp.dot(filt_ref[i], taps_ref[i], preferred_element_type=jnp.float32).astype(
            jnp.bfloat16
        )
        for k in range(len(picks)):
            out_refs[k][i * G : (i + 1) * G, :] = mixed[:, k * width : (k + 1) * width]


def conv_rows(pair, place, supports, fields, edge, weight, chunks, picks, after, roomy):
    own, chans, lon = fields.shape
    width = ceil_to(lon // chunks, LANES)
    highest = (LANES + lon - lon // chunks + DLON) // LANES
    total = (highest + 1) * LANES + width
    arrays = [fields] + ([] if edge is None else [edge]) + [weight]
    return pl.pallas_call(
        functools.partial(conv_kernel, chunks, picks, edge is not None, len(after)),
        out_shape=[jax.ShapeDtypeStruct((2 * chans, width), jnp.bfloat16)] * len(picks),
        in_specs=[SMEM] * 6 + [VMEM] * len(arrays) + [ANY] * len(after),
        out_specs=[VMEM] * len(picks),
        scratch_shapes=[
            pltpu.VMEM((own + HALO, chans, total), jnp.bfloat16),
            pltpu.VMEM((2, TAPS * G, len(picks) * width), jnp.bfloat16),
            pltpu.VMEM((2, G, TAPS * G), jnp.bfloat16),
        ],
        compiler_params=params(56 if roomy else 20),
        cost_estimate=takes(1 if len(picks) > 1 else 0.2),
        name="conv_rows",
    )(pair, place, *supports, *arrays, *after)


def mlp_kernel(parts, last, after, place_ref, *rest):
    blocks, rest = rest[:parts], rest[parts:]
    up_ref, down_ref, table_ref, *rest = rest
    rest = rest[after:]
    if last:
        earlier_ref, out_ref, cells_ref = rest
    else:
        out_ref, cells_ref = rest
    width = blocks[0].shape[1]
    place = place_ref[0]
    for block, k in zip(blocks, [0, *issue_order(parts)]):
        origin = pl.multiple_of(source(place, k, parts) * G, G)
        for i in range(2):
            cells_ref[pl.ds(origin, G), i * width : (i + 1) * width] = block[
                i * G : (i + 1) * G, :
            ]
    values = cells_ref[...].astype(jnp.float32)
    center = values - jnp.mean(values, axis=0, keepdims=True)
    spread = jnp.mean(center * center, axis=0, keepdims=True)
    normed = (center * lax.rsqrt(spread + EPS)).astype(jnp.bfloat16)
    lifted = jnp.dot(up_ref[...], normed, preferred_element_type=jnp.float32)
    scale = math.sqrt(2.0 / math.pi)
    inner = lifted * (scale + (scale * 0.044715) * (lifted * lifted))
    half = 0.5 * lifted
    active = (half + half * jnp.tanh(inner)).astype(jnp.bfloat16)
    lowered = jnp.dot(down_ref[...], active, preferred_element_type=jnp.float32)
    result = (values + lowered).astype(jnp.bfloat16)
    found = []
    for i in range(2):
        modes = lax.dot_general(
            table_ref[place],
            result[:, i * width : (i + 1) * width],
            (((1,), (1,)), ((), ())),
            preferred_element_type=jnp.float32,
        )
        found.append(modes.reshape(modes.shape[0] // SLOT, SLOT, modes.shape[1]))
    block = jnp.concatenate(found, axis=1).astype(jnp.bfloat16)
    if last:
        out_ref[:, 0 : 2 * SLOT, :] = earlier_ref[...]
        out_ref[:, 2 * SLOT : 4 * SLOT, :] = block
    else:
        out_ref[...] = block


def mlp_rows(place, blocks, up, down, tables, earlier, dests, after):
    pair_chans, width = blocks[0].shape
    chan = len(blocks) * pair_chans // 2
    last = earlier is not None
    arrays = [*blocks, up, down, tables, *after] + ([earlier] if last else [])
    rows = (4 if last else 2) * SLOT
    return pl.pallas_call(
        functools.partial(mlp_kernel, len(blocks), last, len(after)),
        out_shape=jax.ShapeDtypeStruct((dests, rows, chan), jnp.bfloat16),
        in_specs=[SMEM]
        + [VMEM] * (len(blocks) + 3)
        + [ANY] * len(after)
        + [VMEM] * last,
        out_specs=VMEM,
        scratch_shapes=[pltpu.VMEM((chan, 2 * width), jnp.bfloat16)],
        compiler_params=params(20 if dests <= FEW else 40),
        cost_estimate=takes(1),
        name="mlp_rows",
    )(place, *arrays)


def expand_kernel(start_ref, legendre_ref, spread_ref, out_ref):
    _, lats, degrees = legendre_ref.shape
    m = pl.program_id(0)
    degree = lax.broadcasted_iota(jnp.int32, (lats, degrees), 1)
    kept = jnp.where(degree >= start_ref[0] + m, legendre_ref[0].astype(jnp.float32), 0.0)
    wide = lax.dot_general(
        kept.astype(jnp.bfloat16),
        spread_ref[...],
        (((0,), (0,)), ((), ())),
        preferred_element_type=jnp.float32,
    )
    slot = lax.rem(lax.broadcasted_iota(jnp.int32, wide.shape, 1), SLOT)
    for r in range(2):
        out_ref[0, r] = jnp.where(slot == 2 * m + r, wide, 0.0).astype(jnp.bfloat16)


def expand(start, legendre, spread):
    modes, lats, degrees = legendre.shape
    depth = spread.shape[1]
    return pl.pallas_call(
        expand_kernel,
        out_shape=jax.ShapeDtypeStruct((modes, 2, degrees, depth), jnp.bfloat16),
        grid=(modes,),
        in_specs=[
            SMEM,
            pl.BlockSpec((1, lats, degrees), lambda m: (m, 0, 0)),
            pl.BlockSpec((lats, depth), lambda m: (0, 0)),
        ],
        out_specs=pl.BlockSpec((1, 2, degrees, depth), lambda m: (m, 0, 0, 0)),
        compiler_params=params(10 if depth <= 512 else 48),
        cost_estimate=takes(0.2),
        name="expand",
    )(start, legendre, spread)


def final_kernel(left_ref, spectrum_ref, out_ref, result_ref, sems):
    modes = left_ref.shape[0]
    chan = spectrum_ref.shape[1]
    copies = []
    for m in range(modes):
        for r in range(2):
            result_ref[m, :, r * chan : (r + 1) * chan] = jnp.dot(
                left_ref[m, r], spectrum_ref[...], preferred_element_type=jnp.float32
            ).astype(jnp.bfloat16)
        copies.append(pltpu.make_async_copy(result_ref.at[m], out_ref.at[m], sems.at[m]))
        copies[-1].start()
    for copy in copies:
        copy.wait()


def final_sum(left, spectrum):
    modes, _, degrees, depth = left.shape
    shape = (modes, degrees, 2 * spectrum.shape[1])
    return pl.pallas_call(
        final_kernel,
        out_shape=jax.ShapeDtypeStruct(shape, jnp.bfloat16),
        in_specs=[VMEM, VMEM],
        out_specs=HBM,
        scratch_shapes=[pltpu.VMEM(shape, jnp.bfloat16), pltpu.SemaphoreType.DMA((modes,))],
        compiler_params=params(8 if depth <= 512 else 48),
        cost_estimate=takes(1),
        name="final_sum",
    )(left, spectrum)


def fourier_blocks(lon, chunks, width, dests, mode_dev):
    chunk = lon // chunks
    index = np.arange(lon, dtype=np.int64)
    mode = np.arange(dests * mode_dev, dtype=np.int64)
    angle = ((mode[:, None] * index[None, :]) % lon) * (2.0 * math.pi / lon)
    paired = np.stack([np.cos(angle), -np.sin(angle)], axis=1) * math.sqrt(2.0 / lon)
    paired = paired.reshape(dests, 2 * mode_dev, chunks, chunk)
    table = np.zeros((chunks, dests, SLOT, width), np.float32)
    table[:, :, : 2 * mode_dev, :chunk] = np.transpose(paired, (2, 0, 1, 3))
    return table.reshape(chunks, dests * SLOT, width).astype(jnp.bfloat16)


def turn(block, axis, count, k):
    return lax.ppermute(block, axis, [(i, target(i, k, count)) for i in range(count)])


def scalar(value):
    return jnp.asarray(value, jnp.int32).reshape(1)


def on_device(
    fields,
    disco_weight,
    support_lat,
    support_lon,
    support_basis,
    support_value,
    w_up,
    w_down,
    legendre,
):
    lat_dev, lon, _ = fields.shape
    num_lat = lax.axis_size("lat")
    num_chan = lax.axis_size("chan")
    mode_dev, _, lats = legendre.shape
    dests = num_lat * num_chan
    width = ceil_to(lon // num_chan, LANES)
    band = lax.axis_index("lat")
    place = scalar(lax.axis_index("chan"))
    index = lax.axis_index(("lat", "chan"))
    supports = (support_lat, support_lon, support_basis, support_value)

    two_bands = num_lat == 2
    cells = jnp.swapaxes(fields, 1, 2)
    if two_bands:
        edge_out = lax.dynamic_slice_in_dim(cells, HALO * (1 - band), HALO, axis=0)
        edges = [None, lax.ppermute(edge_out, "lat", [(0, 1), (1, 0)])]
        pairs = [band, 1 - band]
    else:
        ends = num_lat - 1
        edges = [
            lax.ppermute(cells[lat_dev - HALO :], "lat", [(i, i + 1) for i in range(ends)]),
            lax.ppermute(cells[:HALO], "lat", [(i + 1, i) for i in range(ends)]),
        ]
        pairs = [0, 1]

    tables = jnp.asarray(fourier_blocks(lon, num_chan, width, dests, mode_dev))
    up = w_up.T
    down = w_down.T

    depth = dests * 4 * SLOT
    row = np.arange(depth)
    source_band = row // (4 * SLOT) // num_chan
    phase = (row // (2 * SLOT)) % 2
    source_pair = (phase ^ source_band) if two_bands else phase
    lat_of = lat_dev * source_band + 2 * source_pair + (row // SLOT) % 2
    spread = (lat_of[None, :] == np.arange(lats)[:, None]).astype(jnp.bfloat16)
    left = expand(scalar(index * mode_dev), jnp.swapaxes(legendre, 1, 2), jnp.asarray(spread))

    received = []
    after = []
    order = issue_order(num_chan)
    for edge, pair in zip(edges, pairs):
        shared = (scalar(pair), place, supports, cells, edge, disco_weight, num_chan)
        sent = conv_rows(*shared, order, after, edge is None)
        moved = [turn(block, "chan", num_chan, k) for k, block in zip(order, sent)]
        kept = conv_rows(*shared, (0,), sent[-1:], False)
        received.append([*kept, *moved])
        after = kept
    spectrum = None
    after = list(after)
    for blocks in received:
        spectrum = mlp_rows(place, blocks, up, down, tables, spectrum, dests, after)
        after = []

    both = ("lat", "chan")
    gathered = lax.all_to_all(spectrum, both, split_axis=0, concat_axis=0, tiled=True)
    return final_sum(left, gathered.reshape(depth, gathered.shape[2]))


def solution(mesh):
    in_specs = (
        P(("tm", "lat"), None, "chan"),
        P(None, "chan", None),
        P("lat", None),
        P("lat", None),
        P("lat", None),
        P("lat", None),
        P(),
        P(),
        P(("lat", "chan"), None, None),
    )
    out_specs = P(("tm", "lat", "chan"), None, None)
    return jax.shard_map(
        on_device, mesh=mesh, in_specs=in_specs, out_specs=out_specs, check_vma=False
    )
```
